256 devices in a mesh: dp: 64 (over z_hi, y, x), shard: 4 (over z_lo, core).
Axes of the slice: x: 4, y: 4, z: 8 (z_hi: 4, z_lo: 2; z = z_hi * 2 + z_lo), core: 2. Of those that a mesh axis runs over, the one named last changes fastest.
Arguments:
- context: bfloat16 [65536, 2048], P(('dp', 'shard')), may hold values from -6 to 6
- out_grad: bfloat16 [65536, 2048], P(('dp', 'shard')), may hold values from -6 to 6
- weight: bfloat16 [2048, 2048], P('shard'), may hold values from -0.125 to 0.125
- error: float32 [64, 2048, 2048], P('dp', 'shard'), may hold values from -6 to 6
- warm: bfloat16 [2048, 256], P('shard'), may hold values from -1 to 1
Outputs:
- in_grad: bfloat16 [65536, 2048], P(('dp', 'shard'))
- new_error: float32 [64, 2048, 2048], P('dp', 'shard')
- factor_q: float32 [2048, 256], P('shard')
The draws below stay inside these ranges and needn't reach their ends.
All inputs are finite; a program needn't handle non-finite values.
Results may differ from the reference program's by a relative error of at most 0.0085.
Values may be sent and summed in bfloat16 or wider, within the bound.
No kernel may reach another device: no remote copies, remote signals or barrier semaphores. Data moves between devices by JAX's collectives and lax.ppermute only.
A program may use at most 128 MiB of HBM per device.

```python
import math
import jax
import jax.numpy as jnp
from jax import lax

FEAT = 2048
RANK = 256
TOK_DEV = 256
CTX = 2048
TOKENS = 65536
N_DP = 64
N_SHARD = 4


def draw_context(key, part):
    key = jax.random.fold_in(key, 11)
    values = jnp.clip(jax.random.normal(key, (TOKENS, CTX), jnp.float32), -6.0, 6.0)
    return values.astype(jnp.bfloat16)


def draw_out_grad(key, part):
    key = jax.random.fold_in(key, 23)
    values = jnp.clip(jax.random.normal(key, (TOKENS, FEAT), jnp.float32), -6.0, 6.0)
    return values.astype(jnp.bfloat16)


def draw_error(key, part):
    key = jax.random.fold_in(key, 37)
    values = jnp.clip(jax.random.normal(key, (N_DP, CTX, FEAT), jnp.float32), -6.0, 6.0)
    return values.astype(jnp.float32)


def draw_warm(key, part):
    key = jax.random.fold_in(key, 41)
    values = jnp.clip(jax.random.normal(key, (FEAT, RANK), jnp.float32), -6.0, 6.0)
    values = values * (1.0 / FEAT ** 0.5)
    return values.astype(jnp.bfloat16)


def shard_levels(stream_key, shape, cuts, smallest, top_value):
    def one(axis_at, shards_of):
        heights = jax.random.uniform(jax.random.fold_in(jax.random.fold_in(stream_key, 6), axis_at), (shards_of,), jnp.float32, smallest / len(cuts), top_value / len(cuts))
        return jnp.repeat(jnp.exp(heights), shape[axis_at] // shards_of).reshape((-1,) + (1,) * (len(shape) - axis_at - 1))

    loudness = one(*cuts[0])
    for cut in cuts[1:]:
        loudness = loudness * one(*cut)
    return loudness


def noise(rng, shape, width, most, shards=(), dtype=jnp.bfloat16):
    values = jax.random.normal(rng, shape, jnp.float32) * width
    if len(shards) > 0:
        values = shard_levels(rng, shape, shards, -0.22, 0.18) * values
    return jnp.clip(values, min=-most, max=most).astype(dtype)


def setup_inputs(seed: int = 0) -> dict:
    key_of = jax.random.split(jax.random.key(seed), 6)
    return {
        "context": draw_context(jax.random.fold_in(key_of[5], 71), 0),
        "out_grad": draw_out_grad(jax.random.fold_in(key_of[5], 71), 0),
        "weight": noise(key_of[2], (CTX, FEAT), FEAT ** -0.5, 0.125, ((0, 4),)),
        "error": draw_error(jax.random.fold_in(key_of[5], 71), 0),
        "warm": draw_warm(jax.random.fold_in(key_of[5], 71), 0),
    }


def reference(context, out_grad, weight, error, warm):
    hi = lax.Precision.HIGHEST
    in_grad = lax.dot_general(out_grad.astype(jnp.float32), weight.astype(jnp.float32), (((1,), (1,)), ((), ())), preferred_element_type=jnp.float32).astype(jnp.bfloat16)
    scale = 1.0 / math.sqrt(TOK_DEV * N_SHARD)
    ctx_blocks = context.reshape(N_DP, N_SHARD, TOK_DEV, CTX)
    grad_blocks = out_grad.reshape(N_DP, N_SHARD, TOK_DEV, FEAT)

    def one_term(pair):
        part = lax.dot_general(pair[0].astype(jnp.float32), pair[1].astype(jnp.float32), (((0,), (0,)), ((), ())), preferred_element_type=jnp.float32) * scale
        part = lax.optimization_barrier(part.astype(jnp.bfloat16))
        return part.astype(jnp.float32)

    def replica(pair):
        return lax.optimization_barrier(jnp.sum(lax.map(one_term, pair), axis=0))
    grads = lax.map(replica, (ctx_blocks, grad_blocks))
    merged = grads + error
    warm_full = warm.astype(jnp.float32)
    factor_p = jnp.einsum('dkn,nr->kr', merged, warm_full, precision=hi)
    gram = jnp.dot(factor_p.T, factor_p, precision=hi)
    lower = jnp.linalg.cholesky(gram)
    basis = lax.linalg.triangular_solve(lower, factor_p, left_side=False, lower=True, transpose_a=True)
    factor_q = jnp.einsum('dkn,kr->nr', merged, basis, precision=hi) / N_DP
    approx = jnp.dot(basis, factor_q.T, precision=hi)
    new_error = merged - approx[None]
    return (in_grad, new_error, factor_q)
```

```python
import math

import jax
import jax.numpy as jnp
import numpy as np
from jax import lax
from jax.sharding import Mesh, PartitionSpec as P

BF16 = jnp.bfloat16
F32 = jnp.float32
HI = lax.Precision.HIGHEST
AXES = ("zh", "y", "x", "zl", "core")
SIZES = (4, 4, 4, 2, 2)


def swap(x, axis):
    return lax.ppermute(x, axis, [(0, 1), (1, 0)])


def dot(a, b, ca, cb):
    return lax.dot_general(
        a.astype(BF16), b.astype(BF16), (((ca,), (cb,)), ((), ())), preferred_element_type=F32
    )


def dot_hi(a, b, ca, cb):
    return lax.dot_general(
        a, b, (((ca,), (cb,)), ((), ())), precision=HI, preferred_element_type=F32
    )


def pick(pair, which):
    return lax.dynamic_index_in_dim(pair, which, 0, keepdims=False)


def in_order(mine, other, at):
    first = at == 0
    return jnp.stack([jnp.where(first, mine, other), jnp.where(first, other, mine)])


def reduce_half(half):
    rows, cols = half.shape
    parts = half.astype(BF16).reshape(16, rows // 16, cols)
    parts = lax.all_to_all(parts, ("y", "x"), 0, 0)
    part = parts.astype(F32).sum(0)
    part = part + swap(part.astype(BF16), "zl").astype(F32)
    sent = part.astype(BF16)
    for step in (1, 2, 3):
        part = part + lax.ppermute(
            sent, "zh", [(i, (i + step) % 4) for i in range(4)]
        ).astype(F32)
    whole = jnp.broadcast_to(part.astype(BF16)[None], (16, rows // 16, cols))
    return lax.all_to_all(whole, ("y", "x"), 0, 0).reshape(rows, cols)


def on_device(context, out_grad, weight, error, warm):
    tokens, feat = out_grad.shape
    rows, rank = warm.shape
    replicas = SIZES[0] * SIZES[1] * SIZES[2]
    scale = 1.0 / math.sqrt(tokens * 4)
    core = lax.axis_index("core")
    zl = lax.axis_index("zl")
    error = error[0]
    error_low = error.astype(BF16)

    warm_far = swap(warm, "zl")
    warm_near = swap(warm, "core")
    warm_diag = swap(warm_far, "core")
    warm_full = in_order(
        in_order(warm, warm_near, core), in_order(warm_far, warm_diag, core), zl
    ).reshape(feat, rank)

    grad_far = swap(out_grad, "zl")
    grad_near = swap(out_grad, "core")
    grad_diag = swap(grad_far, "core")

    def columns(to_zl, to_core):
        return lax.dynamic_slice_in_dim(context, (to_zl * 2 + to_core) * rows, rows, 1)

    ctx_own = columns(zl, core)
    ctx_far = swap(
        jnp.stack([columns(1 - zl, core), columns(1 - zl, 1 - core)]), "zl"
    )
    ctx_near = swap(jnp.stack([columns(zl, 1 - core), ctx_far[1]]), "core")
    ctx_all = jnp.concatenate([ctx_own, ctx_far[0], ctx_near[0], ctx_near[1]], 0)
    grad_all = jnp.concatenate([out_grad, grad_far, grad_near, grad_diag], 0)

    cols_all = dot(grad_all, weight, 1, 1).astype(BF16).reshape(4, tokens, rows)
    back_far = swap(jnp.stack([cols_all[1], cols_all[3]]), "zl")
    back_near = swap(jnp.stack([cols_all[2], back_far[1]]), "core")
    in_grad = in_order(
        in_order(cols_all[0], back_near[0], core), in_order(back_far[0], back_near[1], core), zl
    ).reshape(4, tokens, rows)
    in_grad = jnp.concatenate([in_grad[i] for i in range(4)], 1)

    proj = (dot(out_grad, warm_full, 1, 0) * scale).astype(BF16)
    left = dot(context, proj, 0, 0).reshape(2, 2, rows, rank)
    left = jnp.moveaxis(left, 1, 0)
    got = swap(pick(left, 1 - core).astype(BF16), "core").astype(F32)
    half = pick(left, core) + got
    left_error = dot(error_low, warm_full, 1, 0)
    half = half + jnp.stack([jnp.where(zl == i, left_error, 0.0) for i in range(2)])
    half = reduce_half(half.reshape(2 * rows, rank))
    other = swap(half, "core")
    left_own = pick(half.reshape(2, rows, rank), zl)
    left_full = jnp.moveaxis(
        in_order(half.reshape(2, rows, rank), other.reshape(2, rows, rank), core), 0, 1
    ).reshape(4 * rows, rank)

    wide = left_full.astype(F32)
    gram = dot_hi(wide, wide, 0, 0)
    lower = jnp.linalg.cholesky(gram)
    inverse = lax.linalg.triangular_solve(
        lower, jnp.eye(rank, dtype=F32), left_side=True, lower=True
    )

    proj = (dot(context, left_full, 1, 0) * scale).astype(BF16)
    right = dot(out_grad, proj, 0, 0) + dot(error_low, left_own, 0, 0)
    right = right.reshape(2, feat // 2, rank)
    got = swap(pick(right, 1 - core).astype(BF16), "core").astype(F32)
    half = reduce_half(pick(right, core) + got)
    other = swap(half, "core")
    right_full = in_order(half, other, core).reshape(feat, rank).astype(F32)

    q_full = dot_hi(right_full, inverse, 1, 1) * (1.0 / replicas)
    factor_q = lax.dynamic_slice_in_dim(q_full, (zl * 2 + core) * rows, rows, 0)
    basis = dot_hi(left_own.astype(F32), inverse, 1, 1)
    new_error = error + dot(ctx_all, grad_all, 0, 0) * scale - dot(basis, q_full, 1, 1)
    return in_grad, new_error[None], factor_q


def solution(mesh):
    split = Mesh(np.asarray(mesh.devices).reshape(SIZES), AXES)
    every = ("zh", "y", "x", "zl", "core")
    shard = ("zl", "core")
    return jax.shard_map(
        on_device,
        mesh=split,
        in_specs=(
            P(every, None),
            P(every, None),
            P(shard, None),
            P(("zh", "y", "x"), shard, None),
            P(shard, None),
        ),
        out_specs=(P(every, None), P(("zh", "y", "x"), shard, None), P(shard, None)),
        check_vma=False,
    )
```

```python
import functools
import math

import jax
import jax.numpy as jnp
import numpy as np
from jax import lax
from jax.experimental import pallas as pl
from jax.experimental.pallas import tpu as pltpu
from jax.sharding import Mesh, PartitionSpec as P

BF16 = jnp.bfloat16
F32 = jnp.float32
HI = lax.Precision.HIGHEST
AXES = ("zh", "y", "x", "zl", "core")
SIZES = (4, 4, 4, 2, 2)
ROWS = 512
RANK = 256
FEAT = 2048
TOK = 256
HALF = RANK // 2
CHUNKS, CHUNK_ROWS, CHUNK_COLS = 16, 16, 1024
VMEM = pl.BlockSpec(memory_space=pltpu.VMEM)
SMEM = pl.BlockSpec(memory_space=pltpu.SMEM)


def swap(x, axis):
    return lax.ppermute(x, axis, [(0, 1), (1, 0)])


def mm(a, b, ca, cb):
    return lax.dot_general(a, b, (((ca,), (cb,)), ((), ())), preferred_element_type=F32)


def two(x):
    high = x.astype(BF16)
    return high, (x - high.astype(F32)).astype(BF16)


def chunk_at(n):
    return n // 2 * CHUNK_ROWS, n % 2 * CHUNK_COLS


def split_halves(core, total, keep, send):
    for n in range(CHUNKS):
        row, col = chunk_at(n)
        cols = pl.ds(col, CHUNK_COLS)
        keep[n] = total[pl.ds(pl.multiple_of(core * HALF + row, CHUNK_ROWS), CHUNK_ROWS), cols]
        send[n] = total[
            pl.ds(pl.multiple_of((1 - core) * HALF + row, CHUNK_ROWS), CHUNK_ROWS), cols
        ].astype(send.dtype)


def join_halves(core, mine, other, whole):
    for n in range(CHUNKS):
        row, col = chunk_at(n)
        cols = pl.ds(col, CHUNK_COLS)
        whole[pl.ds(pl.multiple_of(core * HALF + row, CHUNK_ROWS), CHUNK_ROWS), cols] = mine[n]
        whole[pl.ds(pl.multiple_of((1 - core) * HALF + row, CHUNK_ROWS), CHUNK_ROWS), cols] = other[n]


def block(zl, core):
    return pl.ds(pl.multiple_of((zl * 2 + core) * ROWS, ROWS), ROWS)


def left_kernel(scale, at, og, ctx, err, w0, w1, w2, w3, keep, send, total):
    zl, core = at[0], at[1]
    where = ((zl, core), (zl, 1 - core), (1 - zl, core), (1 - zl, 1 - core))
    proj = jnp.zeros((TOK, RANK), F32)
    own = jnp.zeros((ROWS, RANK), F32)
    for (a, b), w in zip(where, (w0, w1, w2, w3)):
        cols = block(a, b)
        proj += mm(og[:, cols], w[...], 1, 0)
        high, low = two(err[:, cols])
        own += mm(high, w[...], 1, 0) + mm(low, w[...], 1, 0)
    high, low = two(proj * scale)
    total[...] = mm(high, ctx[...], 0, 0) + mm(low, ctx[...], 0, 0)
    total[:, block(zl, core)] += own.T
    split_halves(core, total, keep, send)


def right_kernel(scale, at, ctx, og, err, mine, other, keep, send, left, total):
    zl, core = at[0], at[1]
    join_halves(core, mine, other, left)
    proj = mm(ctx[...], left[...], 1, 1) * scale
    high, low = two(proj)
    total[...] = mm(high, og[...], 0, 0) + mm(low, og[...], 0, 0)
    own = left[:, block(zl, core)]
    high, low = two(err[...])
    total[...] += mm(own, high, 1, 0) + mm(own, low, 1, 0)
    split_halves(core, total, keep, send)


def last_kernel(share, at, mine, other, inverse, basis, merged, new_error, factor_q, right, q):
    zl, core = at[0], at[1]
    join_halves(core, mine, other, right)
    high, low = two(inverse[...])
    q[...] = (mm(high, right[...], 1, 0) + mm(low, right[...], 1, 0)) * share
    factor_q[...] = q[:, block(zl, core)].T
    low = q[...].astype(BF16)
    new_error[...] = merged[...] - mm(basis[...], low, 0, 0)


def call(kernel, outs, scratch, args, flops, name, limit=40):
    moved = sum(math.prod(a.shape) * a.dtype.itemsize for a in args[1:])
    moved += sum(math.prod(s) * jnp.dtype(d).itemsize for s, d in outs)
    return pl.pallas_call(
        kernel,
        out_shape=[jax.ShapeDtypeStruct(s, d) for s, d in outs],
        in_specs=[SMEM] + [VMEM] * (len(args) - 1),
        out_specs=[VMEM] * len(outs),
        scratch_shapes=[pltpu.VMEM(s, d) for s, d in scratch],
        compiler_params=pltpu.CompilerParams(vmem_limit_bytes=limit * 2**20),
        cost_estimate=pl.CostEstimate(flops=flops, bytes_accessed=moved, transcendentals=0),
        name=name,
    )(*args)


CHUNKED = (CHUNKS, CHUNK_ROWS, CHUNK_COLS)


def reduce_half(half):
    parts = lax.all_to_all(half.astype(BF16), ("y", "x"), 0, 0)
    part = parts.astype(F32).sum(0)
    part = part + swap(part, "zl")
    one, opposite, three = (
        lax.ppermute(part, "zh", [(i, (i + step) % 4) for i in range(4)]) for step in (1, 2, 3)
    )
    part = (part + opposite) + (one + three)
    whole = jnp.broadcast_to(part.astype(BF16)[None], CHUNKED)
    return lax.all_to_all(whole, ("y", "x"), 0, 0)


def all_reduce(keep, send):
    half = reduce_half(keep + swap(send, "core").astype(F32))
    return half, swap(half, "core")


def in_order(mine, other, at):
    first = at == 0
    return jnp.stack([jnp.where(first, mine, other), jnp.where(first, other, mine)])


def on_device(context, out_grad, weight, error, warm):
    scale = 1.0 / math.sqrt(TOK * 4)
    core = lax.axis_index("core")
    zl = lax.axis_index("zl")
    at = jnp.stack([zl, core]).astype(jnp.int32)
    error = error[0]

    warm_far = swap(warm, "zl")
    warm_near = swap(warm, "core")
    warm_diag = swap(warm_far, "core")

    keep, send = call(
        functools.partial(left_kernel, scale),
        [(CHUNKED, F32), (CHUNKED, BF16)],
        [((RANK, FEAT), F32)],
        (at, out_grad, context, error, warm, warm_near, warm_far, warm_diag),
        2_000_000_000,
        "left",
    )
    mine, other = all_reduce(keep, send)

    keep, send, left = call(
        functools.partial(right_kernel, scale),
        [(CHUNKED, F32), (CHUNKED, BF16), ((RANK, FEAT), BF16)],
        [((RANK, FEAT), F32)],
        (at, context, out_grad, error, mine, other),
        2_000_000_000,
        "right",
    )

    gram = mm(left, left, 1, 1)
    lower = jnp.linalg.cholesky(gram)
    inverse = lax.linalg.triangular_solve(
        lower, jnp.eye(RANK, dtype=F32), left_side=True, lower=True
    )
    left_own = lax.dynamic_slice_in_dim(left, (zl * 2 + core) * ROWS, ROWS, 1)
    basis = lax.dot_general(
        inverse, left_own.astype(F32), (((1,), (0,)), ((), ())), precision=HI
    ).astype(BF16)

    mine, other = all_reduce(keep, send)

    out_grad, context, _ = lax.optimization_barrier((out_grad, context, warm_far))
    grad_far = swap(out_grad, "zl")
    grad_near = swap(out_grad, "core")
    grad_diag = swap(grad_far, "core")
    grads = (out_grad, grad_near, grad_far, grad_diag)

    def columns(to_zl, to_core):
        return lax.dynamic_slice_in_dim(context, (to_zl * 2 + to_core) * ROWS, ROWS, 1)

    ctx_far = swap(jnp.stack([columns(1 - zl, core), columns(1 - zl, 1 - core)]), "zl")
    ctx_near = swap(jnp.stack([columns(zl, 1 - core), ctx_far[1]]), "core")
    ctxs = (columns(zl, core), ctx_near[0], ctx_far[0], ctx_near[1])
    merged = error
    for c, g in zip(ctxs, grads):
        merged = merged + mm(c, g, 0, 0) * scale

    own, near, far, diag = (mm(g, weight, 1, 1).astype(BF16) for g in grads)
    back_far = swap(jnp.stack([far, diag]), "zl")
    back_near = swap(jnp.stack([near, back_far[1]]), "core")
    in_grad = in_order(
        in_order(own, back_near[0], core), in_order(back_far[0], back_near[1], core), zl
    ).reshape(4, TOK, ROWS)
    in_grad = jnp.concatenate([in_grad[i] for i in range(4)], 1)

    new_error, factor_q = call(
        functools.partial(last_kernel, 1.0 / (SIZES[0] * SIZES[1] * SIZES[2])),
        [((ROWS, FEAT), F32), ((ROWS, RANK), F32)],
        [((RANK, FEAT), BF16), ((RANK, FEAT), F32)],
        (at, mine, other, inverse, basis, merged),
        1_200_000_000,
        "last",
    )
    return in_grad, new_error[None], factor_q


def solution(mesh):
    split = Mesh(np.asarray(mesh.devices).reshape(SIZES), AXES)
    every = ("zh", "y", "x", "zl", "core")
    shard = ("zl", "core")
    return jax.shard_map(
        on_device,
        mesh=split,
        in_specs=(
            P(every, None),
            P(every, None),
            P(shard, None),
            P(("zh", "y", "x"), shard, None),
            P(shard, None),
        ),
        out_specs=(P(every, None), P(("zh", "y", "x"), shard, None), P(shard, None)),
        check_vma=False,
    )
```

```python
import functools
import math

import jax
import jax.numpy as jnp
import numpy as np
from jax import lax
from jax.experimental import pallas as pl
from jax.experimental.pallas import tpu as pltpu
from jax.sharding import Mesh, PartitionSpec as P

BF16 = jnp.bfloat16
F32 = jnp.float32
HI = lax.Precision.HIGHEST
PART = 64
SUB = 8
AXES = ("zh", "y", "x", "zl", "core")
SIZES = (4, 4, 4, 2, 2)
ROWS = 512
RANK = 256
FEAT = 2048
TOK = 256
HALF = RANK // 2
CHUNKS, CHUNK_ROWS, CHUNK_COLS = 16, 16, 1024
VMEM = pl.BlockSpec(memory_space=pltpu.VMEM)
SMEM = pl.BlockSpec(memory_space=pltpu.SMEM)


def swap(x, axis):
    return lax.ppermute(x, axis, [(0, 1), (1, 0)])


def mm(a, b, ca, cb):
    return lax.dot_general(a, b, (((ca,), (cb,)), ((), ())), preferred_element_type=F32)


def two(x):
    high = x.astype(BF16)
    return high, (x - high.astype(F32)).astype(BF16)


def chunk_at(n):
    return n // 2 * CHUNK_ROWS, n % 2 * CHUNK_COLS


def split_halves(core, total, keep, send):
    for n in range(CHUNKS):
        row, col = chunk_at(n)
        cols = pl.ds(col, CHUNK_COLS)
        keep[n] = total[pl.ds(pl.multiple_of(core * HALF + row, CHUNK_ROWS), CHUNK_ROWS), cols]
        send[n] = total[
            pl.ds(pl.multiple_of((1 - core) * HALF + row, CHUNK_ROWS), CHUNK_ROWS), cols
        ].astype(send.dtype)


def join_halves(core, mine, other, whole):
    for n in range(CHUNKS):
        row, col = chunk_at(n)
        cols = pl.ds(col, CHUNK_COLS)
        whole[pl.ds(pl.multiple_of(core * HALF + row, CHUNK_ROWS), CHUNK_ROWS), cols] = mine[n]
        whole[pl.ds(pl.multiple_of((1 - core) * HALF + row, CHUNK_ROWS), CHUNK_ROWS), cols] = other[n]


def block(zl, core):
    return pl.ds(pl.multiple_of((zl * 2 + core) * ROWS, ROWS), ROWS)


def prepare_kernel(at, ctx, err, own, near, far, diag, high, low):
    zl, core = at[0], at[1]
    own[...] = ctx[:, block(zl, core)]
    near[...] = ctx[:, block(zl, 1 - core)]
    far[...] = ctx[:, block(1 - zl, core)]
    diag[...] = ctx[:, block(1 - zl, 1 - core)]
    high[...], low[...] = two(err[...])


def left_kernel(scale, at, og, ctx, high, low, w0, w1, w2, w3, keep, send, total):
    zl, core = at[0], at[1]
    where = ((zl, core), (zl, 1 - core), (1 - zl, core), (1 - zl, 1 - core))
    proj = jnp.zeros((TOK, RANK), F32)
    own = jnp.zeros((ROWS, RANK), F32)
    for (a, b), w in zip(where, (w0, w1, w2, w3)):
        cols = block(a, b)
        proj += mm(og[:, cols], w[...], 1, 0)
        own += mm(high[:, cols], w[...], 1, 0) + mm(low[:, cols], w[...], 1, 0)
    first, second = two(proj * scale)
    total[...] = mm(first, ctx[...], 0, 0) + mm(second, ctx[...], 0, 0)
    total[:, block(zl, core)] += own.T
    split_halves(core, total, keep, send)


def right_kernel(scale, at, ctx, og, high, low, mine, other, keep, send, left, total):
    zl, core = at[0], at[1]
    join_halves(core, mine, other, left)
    first, second = two(mm(ctx[...], left[...], 1, 1) * scale)
    total[...] = mm(first, og[...], 0, 0) + mm(second, og[...], 0, 0)
    own = left[:, block(zl, core)]
    total[...] += mm(own, high[...], 1, 0) + mm(own, low[...], 1, 0)
    split_halves(core, total, keep, send)


def add_kernel(keep, got, out):
    out[...] = (keep[...] + got[...].astype(F32)).astype(BF16)


def sum_kernel(parts, out):
    out[...] = parts[...].astype(F32).sum(0)


def spread_kernel(part, one, opposite, three, out):
    whole = ((part[...] + opposite[...]) + (one[...] + three[...])).astype(BF16)
    for n in range(CHUNKS):
        out[n] = whole


def row_of(x, k):
    return jnp.broadcast_to(x[k : k + 1, :], x.shape)


def factor_block(rows):
    shape = rows[0].shape
    sub = lax.broadcasted_iota(jnp.int32, shape, 0)
    for p in range(len(rows)):
        cols = [
            [jnp.broadcast_to(r[:, SUB * p + k : SUB * p + k + 1], shape) for k in range(SUB)]
            for r in rows[p:]
        ]
        for k in range(SUB):
            diagonal = row_of(cols[0][k], k)
            inv = lax.rsqrt(diagonal)
            inv = inv * (1.5 - 0.5 * diagonal * inv * inv)
            pivot = row_of(rows[p], k) * inv
            later = [row_of(cols[0][j], k) * inv for j in range(k + 1, SUB)]
            for g, col in enumerate(cols, p):
                times = col[k] * inv
                if g == p:
                    times = jnp.where(sub > k, times, 0.0)
                rows[g] = rows[g] - times * pivot
                if g == p:
                    rows[g] = jnp.where(sub == k, pivot, rows[g])
                for j, entry in zip(range(k + 1, SUB), later):
                    col[j] = col[j] - times * entry
    return rows


def dot_hi(a, b, ca, cb):
    return lax.dot_general(
        a, b, (((ca,), (cb,)), ((), ())), precision=HI, preferred_element_type=F32
    )


def eye(n):
    shape = (n, n)
    same = lax.broadcasted_iota(jnp.int32, shape, 0) == lax.broadcasted_iota(jnp.int32, shape, 1)
    return same.astype(F32)


def eliminate(start, a):
    stop = start + PART
    rows = jnp.concatenate([a[start:stop, start:stop], eye(PART)], 1)
    rows = factor_block([rows[n : n + SUB] for n in range(0, PART, SUB)])
    inverse = jnp.concatenate(rows, 0)[:, PART:]
    panel = dot_hi(inverse, a[start:stop, :], 1, 0)
    a[start:stop, :] = panel
    if stop < RANK:
        a[stop:, :] = a[stop:, :] - dot_hi(panel[:, stop:RANK], panel, 0, 0)


def gram_kernel(left, a):
    a[:, :RANK] = mm(left[...], left[...], 1, 1)
    a[:, RANK:] = eye(RANK)
    eliminate(0, a)


def step_kernel(start, a_in, a):
    eliminate(start, a)


def basis_kernel(at, a_in, left, inverse, basis, a):
    a[...] = a_in[...]
    eliminate(RANK - PART, a)
    inverse[...] = a[:, RANK:]
    first, second = two(a[:, RANK:])
    own = left[:, block(at[0], at[1])]
    basis[...] = (mm(first, own, 1, 0) + mm(second, own, 1, 0)).astype(BF16)


def grad_kernel(g0, g1, g2, g3, weight, o0, o1, o2, o3):
    for g, o in ((g0, o0), (g1, o1), (g2, o2), (g3, o3)):
        o[...] = mm(g[...], weight[...], 1, 1).astype(BF16)


def merge_kernel(scale, err, c0, c1, g0, g1, out):
    total = mm(c0[...], g0[...], 0, 0) + mm(c1[...], g1[...], 0, 0)
    out[...] = err[...] + total * scale


def last_kernel(
    share, at, mine, other, inverse, basis, merged, i0, i1, i2, i3, new_error, factor_q, in_grad, right
):
    step = pl.program_id(0)
    zl, core = at[0], at[1]

    @pl.when(step == 0)
    def _():
        join_halves(core, mine, other, right)

    cols = pl.ds(pl.multiple_of(step * ROWS, ROWS), ROWS)
    first, second = two(inverse[...])
    q = (mm(first, right[:, cols], 1, 0) + mm(second, right[:, cols], 1, 0)) * share
    new_error[...] = merged[...] - mm(basis[...], q.astype(BF16), 0, 0)
    at_zl, at_core = step // 2, step % 2

    @pl.when((at_zl == zl) & (at_core == core))
    def _():
        factor_q[...] = q.T
        in_grad[...] = i0[...]

    @pl.when((at_zl == zl) & (at_core != core))
    def _():
        in_grad[...] = i1[...]

    @pl.when((at_zl != zl) & (at_core == core))
    def _():
        in_grad[...] = i2[...]

    @pl.when((at_zl != zl) & (at_core != core))
    def _():
        in_grad[...] = i3[...]


def size(shape, dtype):
    return math.prod(shape) * jnp.dtype(dtype).itemsize


def call(kernel, outs, args, flops, name, scratch=(), alias=None, limit=16):
    moved = sum(size(a.shape, a.dtype) for a in args) + sum(size(s, d) for s, d in outs)
    return pl.pallas_call(
        kernel,
        out_shape=[jax.ShapeDtypeStruct(s, d) for s, d in outs],
        in_specs=[SMEM if a.dtype == jnp.int32 else VMEM for a in args],
        out_specs=[VMEM] * len(outs),
        scratch_shapes=[pltpu.VMEM(s, d) for s, d in scratch],
        input_output_aliases=alias or {},
        compiler_params=pltpu.CompilerParams(vmem_limit_bytes=limit * 2**20),
        cost_estimate=pl.CostEstimate(flops=flops, bytes_accessed=moved, transcendentals=0),
        name=name,
    )(*args)


CHUNKED = (CHUNKS, CHUNK_ROWS, CHUNK_COLS)
CHUNK = (CHUNK_ROWS, CHUNK_COLS)


def tied(x, *others):
    return lax.optimization_barrier((x,) + others)[0]


def across_plane(keep, send):
    got = swap(send, "core")
    (half,) = call(add_kernel, [(CHUNKED, BF16)], (keep, got), 1_000_000, "add")
    parts = lax.all_to_all(half, ("y", "x"), 0, 0)
    (part,) = call(sum_kernel, [(CHUNK, F32)], (parts,), 1_000_000, "sum")
    return part


def across_z(part, beside=()):
    far = tied(swap(part, "zl"), *beside)
    part = part + far
    return (part,) + tuple(
        lax.ppermute(part, "zh", [(i, (i + step) % 4) for i in range(4)]) for step in (1, 2, 3)
    )


def back_over_plane(part, one, opposite, three, beside=()):
    (whole,) = call(
        spread_kernel,
        [(CHUNKED, BF16)],
        (tied(part, *beside), one, opposite, three),
        1_000_000,
        "spread",
    )
    return lax.all_to_all(whole, ("y", "x"), 0, 0)


def on_device(context, out_grad, weight, error, warm):
    scale = 1.0 / math.sqrt(TOK * 4)
    core = lax.axis_index("core")
    zl = lax.axis_index("zl")
    at = jnp.stack([zl, core]).astype(jnp.int32)
    error = error[0]
    tokens = ((TOK, ROWS), BF16)

    warm_far = swap(warm, "zl")
    warm_near = swap(warm, "core")
    c_own, c_near, c_far, c_diag, high, low = call(
        prepare_kernel,
        [tokens] * 4 + [((ROWS, FEAT), BF16)] * 2,
        (at, context, error),
        4_000_000,
        "prepare",
    )
    warm_diag = swap(tied(warm_far, low), "core")

    keep, send = call(
        functools.partial(left_kernel, scale),
        [(CHUNKED, F32), (CHUNKED, BF16)],
        (at, out_grad, context, high, low, warm, warm_near, warm_far, warm_diag),
        2_000_000_000,
        "left",
        [((RANK, FEAT), F32)],
    )
    g_far = swap(tied(out_grad, warm_far), "zl")
    g_near = swap(tied(out_grad, warm_far), "core")
    part = across_plane(keep, send)
    g_diag = swap(g_far, "core")
    c_near = swap(c_near, "core")
    zs = across_z(tied(part, g_far, g_near))
    (merged,) = call(
        functools.partial(merge_kernel, scale),
        [((ROWS, FEAT), F32)],
        (error, c_own, c_near, out_grad, g_near),
        1_100_000_000,
        "merge",
    )
    c_far, c_diag = (tied(c, zs[1]) for c in (c_far, c_diag))
    c_far, c_diag = swap(c_far, "zl"), swap(c_diag, "zl")
    mine = back_over_plane(*zs, beside=(g_diag, merged))

    i_own, i_near, i_far, i_diag = call(
        grad_kernel, [tokens] * 4, (out_grad, g_near, g_far, g_diag, weight), 2_200_000_000, "grad"
    )
    mine = tied(mine, i_own)
    other = swap(mine, "core")
    i_diag = swap(i_diag, "zl")
    i_far = swap(i_far, "zl")
    i_near = swap(i_near, "core")

    keep, send, left = call(
        functools.partial(right_kernel, scale),
        [(CHUNKED, F32), (CHUNKED, BF16), ((RANK, FEAT), BF16)],
        (at, context, out_grad, high, low, mine, other),
        2_000_000_000,
        "right",
        [((RANK, FEAT), F32)],
    )
    part = across_plane(keep, send)

    table = ((RANK, 2 * RANK), F32)
    (a,) = call(gram_kernel, [table], (left,), 300_000_000, "gram")
    part = tied(part, a, c_far, c_diag, i_far, i_diag, i_near)
    i_diag = swap(i_diag, "core")
    c_diag = swap(c_diag, "core")
    (a,) = call(
        functools.partial(step_kernel, PART), [table], (a,), 300_000_000, "step", alias={0: 0}
    )
    zs = across_z(part, (a,))
    (a,) = call(
        functools.partial(step_kernel, 2 * PART), [table], (a,), 300_000_000, "step", alias={0: 0}
    )
    mine = back_over_plane(*zs, beside=(a, c_diag))
    inverse, basis = call(
        basis_kernel,
        [((RANK, RANK), F32), ((RANK, ROWS), BF16)],
        (at, a, left),
        300_000_000,
        "basis",
        [table],
    )
    (merged,) = call(
        functools.partial(merge_kernel, scale),
        [((ROWS, FEAT), F32)],
        (merged, c_far, c_diag, g_far, g_diag),
        1_100_000_000,
        "merge",
        alias={0: 0},
    )
    mine = tied(mine, merged, basis)
    other = swap(mine, "core")

    whole = lambda *shape: pl.BlockSpec(shape, lambda j: (0,) * len(shape))
    column = lambda rows: pl.BlockSpec((rows, ROWS), lambda j: (0, j))
    new_error, factor_q, in_grad = pl.pallas_call(
        functools.partial(last_kernel, 1.0 / (SIZES[0] * SIZES[1] * SIZES[2])),
        grid=(4,),
        out_shape=[
            jax.ShapeDtypeStruct((ROWS, FEAT), F32),
            jax.ShapeDtypeStruct((ROWS, RANK), F32),
            jax.ShapeDtypeStruct((TOK, FEAT), BF16),
        ],
        in_specs=[SMEM, VMEM, VMEM, VMEM, VMEM, column(ROWS)] + [VMEM] * 4,
        out_specs=[column(ROWS), whole(ROWS, RANK), column(TOK)],
        scratch_shapes=[pltpu.VMEM((RANK, FEAT), BF16)],
        compiler_params=pltpu.CompilerParams(vmem_limit_bytes=20 * 2**20),
        cost_estimate=pl.CostEstimate(
            flops=1_200_000_000, bytes_accessed=12_000_000, transcendentals=0
        ),
        name="last",
    )(at, mine, other, inverse, basis, merged, i_own, i_near, i_far, i_diag)
    return in_grad, new_error[None], factor_q


def solution(mesh):
    split = Mesh(np.asarray(mesh.devices).reshape(SIZES), AXES)
    every = ("zh", "y", "x", "zl", "core")
    shard = ("zl", "core")
    return jax.shard_map(
        on_device,
        mesh=split,
        in_specs=(
            P(every, None),
            P(every, None),
            P(shard, None),
            P(("zh", "y", "x"), shard, None),
            P(shard, None),
        ),
        out_specs=(P(every, None), P(("zh", "y", "x"), shard, None), P(shard, None)),
        check_vma=False,
    )
```

```python
import functools
import math

import jax
import jax.numpy as jnp
import numpy as np
from jax import lax
from jax.experimental import pallas as pl
from jax.experimental.pallas import tpu as pltpu
from jax.sharding import Mesh, PartitionSpec as P

BF16 = jnp.bfloat16
F32 = jnp.float32
HI = lax.Precision.HIGHEST
PART = 64
SUB = 8
AXES = ("zh", "y", "x", "zl", "core")
SIZES = (4, 4, 4, 2, 2)
ROWS = 512
RANK = 256
FEAT = 2048
TOK = 256
HALF = RANK // 2
CHUNKS, CHUNK_ROWS, CHUNK_COLS = 16, 16, 1024
VMEM = pl.BlockSpec(memory_space=pltpu.VMEM)
SMEM = pl.BlockSpec(memory_space=pltpu.SMEM)
ANY = pl.BlockSpec(memory_space=pl.ANY)


def swap(x, axis):
    return lax.ppermute(x, axis, [(0, 1), (1, 0)])


def mm(a, b, ca, cb):
    return lax.dot_general(a, b, (((ca,), (cb,)), ((), ())), preferred_element_type=F32)


def two(x):
    high = x.astype(BF16)
    return high, (x - high.astype(F32)).astype(BF16)


def chunk_at(n):
    return n // 2 * CHUNK_ROWS, n % 2 * CHUNK_COLS


def fetch(sources, targets, sems):
    copies = [
        pltpu.make_async_copy(src, dst, sems.at[n]) for n, (src, dst) in enumerate(zip(sources, targets))
    ]
    for copy in copies:
        copy.start()
    return copies


def split_halves(core, total, keep, send):
    for n in range(CHUNKS):
        row, col = chunk_at(n)
        cols = pl.ds(col, CHUNK_COLS)
        keep[n] = total[pl.ds(pl.multiple_of(core * HALF + row, CHUNK_ROWS), CHUNK_ROWS), cols]
        send[n] = total[
            pl.ds(pl.multiple_of((1 - core) * HALF + row, CHUNK_ROWS), CHUNK_ROWS), cols
        ].astype(send.dtype)


def join_halves(core, mine, other, whole):
    for n in range(CHUNKS):
        row, col = chunk_at(n)
        cols = pl.ds(col, CHUNK_COLS)
        whole[pl.ds(pl.multiple_of(core * HALF + row, CHUNK_ROWS), CHUNK_ROWS), cols] = mine[n]
        whole[pl.ds(pl.multiple_of((1 - core) * HALF + row, CHUNK_ROWS), CHUNK_ROWS), cols] = other[n]


def block(zl, core):
    return pl.ds(pl.multiple_of((zl * 2 + core) * ROWS, ROWS), ROWS)


def prepare_kernel(at, ctx, err, own, near, far, high, low):
    zl, core = at[0], at[1]
    own[...] = ctx[:, block(zl, core)]
    near[...] = ctx[:, block(zl, 1 - core)]
    far[0] = ctx[:, block(1 - zl, core)]
    far[1] = ctx[:, block(1 - zl, 1 - core)]
    high[...], low[...] = two(err[...])


def left_kernel(
    scale, at, og, ctx, high_hbm, low_hbm, w0, w1, w2, w3, keep, send, total, high, low, sems
):
    zl, core = at[0], at[1]
    copies = fetch((high_hbm, low_hbm), (high, low), sems)
    where = ((zl, core), (zl, 1 - core), (1 - zl, core), (1 - zl, 1 - core))
    proj = jnp.zeros((TOK, RANK), F32)
    for (a, b), w in zip(where, (w0, w1, w2, w3)):
        proj += mm(og[:, block(a, b)], w[...], 1, 0)
    first, second = two(proj * scale)
    total[...] = mm(first, ctx[...], 0, 0) + mm(second, ctx[...], 0, 0)
    for copy in copies:
        copy.wait()
    own = jnp.zeros((ROWS, RANK), F32)
    for (a, b), w in zip(where, (w0, w1, w2, w3)):
        cols = block(a, b)
        own += mm(high[:, cols], w[...], 1, 0) + mm(low[:, cols], w[...], 1, 0)
    total[:, block(zl, core)] += own.T
    split_halves(core, total, keep, send)


def right_kernel(
    scale, at, ctx, og, high_hbm, low_hbm, mine_hbm, other_hbm,
    keep, send, left, total, high, low, mine, other, sems,
):
    zl, core = at[0], at[1]
    copies = fetch((mine_hbm, other_hbm, high_hbm, low_hbm), (mine, other, high, low), sems)
    copies[0].wait()
    copies[1].wait()
    join_halves(core, mine, other, left)
    first, second = two(mm(ctx[...], left[...], 1, 1) * scale)
    total[...] = mm(first, og[...], 0, 0) + mm(second, og[...], 0, 0)
    own = left[:, block(zl, core)]
    copies[2].wait()
    copies[3].wait()
    total[...] += mm(own, high[...], 1, 0) + mm(own, low[...], 1, 0)
    split_halves(core, total, keep, send)


def add_kernel(keep, got, out):
    out[...] = (keep[...] + got[...].astype(F32)).astype(BF16)


def sum_kernel(parts, out):
    out[...] = parts[...].astype(F32).sum(0)


def spread_kernel(part, one, opposite, three, out):
    whole = ((part[...] + opposite[...]) + (one[...] + three[...])).astype(BF16)
    for n in range(CHUNKS):
        out[n] = whole


def row_of(x, k):
    return jnp.broadcast_to(x[k : k + 1, :], x.shape)


def factor_block(rows):
    shape = rows[0].shape
    sub = lax.broadcasted_iota(jnp.int32, shape, 0)
    for p in range(len(rows)):
        cols = [
            [jnp.broadcast_to(r[:, SUB * p + k : SUB * p + k + 1], shape) for k in range(SUB)]
            for r in rows[p:]
        ]
        for k in range(SUB):
            diagonal = row_of(cols[0][k], k)
            inv = lax.rsqrt(diagonal)
            inv = inv * (1.5 - 0.5 * diagonal * inv * inv)
            pivot = row_of(rows[p], k) * inv
            later = [row_of(cols[0][j], k) * inv for j in range(k + 1, SUB)]
            for g, col in enumerate(cols, p):
                times = col[k] * inv
                if g == p:
                    times = jnp.where(sub > k, times, 0.0)
                rows[g] = rows[g] - times * pivot
                if g == p:
                    rows[g] = jnp.where(sub == k, pivot, rows[g])
                for j, entry in zip(range(k + 1, SUB), later):
                    col[j] = col[j] - times * entry
    return rows


def dot_hi(a, b, ca, cb):
    return lax.dot_general(
        a, b, (((ca,), (cb,)), ((), ())), precision=HI, preferred_element_type=F32
    )


def eye(n):
    shape = (n, n)
    same = lax.broadcasted_iota(jnp.int32, shape, 0) == lax.broadcasted_iota(jnp.int32, shape, 1)
    return same.astype(F32)


def eliminate(start, a):
    stop = start + PART
    rows = jnp.concatenate([a[start:stop, start:stop], eye(PART)], 1)
    rows = factor_block([rows[n : n + SUB] for n in range(0, PART, SUB)])
    inverse = jnp.concatenate(rows, 0)[:, PART:]
    panel = dot_hi(inverse, a[start:stop, :], 1, 0)
    a[start:stop, :] = panel
    if stop < RANK:
        a[stop:, :] = a[stop:, :] - dot_hi(panel[:, stop:RANK], panel, 0, 0)


def gram_kernel(left, a):
    a[:, :RANK] = mm(left[...], left[...], 1, 1)
    a[:, RANK:] = eye(RANK)
    eliminate(0, a)


def step_kernel(start, a_in, a):
    eliminate(start, a)


def basis_kernel(at, a_in, left, inverse, basis, a):
    a[...] = a_in[...]
    eliminate(RANK - PART, a)
    inverse[...] = a[:, RANK:]
    first, second = two(a[:, RANK:])
    own = left[:, block(at[0], at[1])]
    basis[...] = (mm(first, own, 1, 0) + mm(second, own, 1, 0)).astype(BF16)


def grad_kernel(h0, h1, h2, h3, weight_hbm, o0, o1, far, weight, g0, g1, g2, g3, sems):
    copies = fetch((weight_hbm, h0, h1, h2, h3), (weight, g0, g1, g2, g3), sems)
    copies[0].wait()
    for g, o, copy in zip((g0, g1, g2, g3), (o0, o1, far.at[0], far.at[1]), copies[1:]):
        copy.wait()
        o[...] = mm(g[...], weight[...], 1, 1).astype(BF16)


def merge_kernel(scale, err, c0, c1, g0, g1, out):
    total = mm(c0[...], g0[...], 0, 0) + mm(c1[...], g1[...], 0, 0)
    out[...] = err[...] + total * scale


def last_kernel(
    share, scale, at, mine_hbm, other_hbm, inverse, basis, merged, c2, c3, g2, g3, i0, i1, i2, i3,
    new_error, factor_q, in_grad, right, mine, other, sems,
):
    step = pl.program_id(0)
    zl, core = at[0], at[1]

    @pl.when(step == 0)
    def _():
        copies = fetch((mine_hbm, other_hbm), (mine, other), sems)
        copies[0].wait()
        copies[1].wait()
        join_halves(core, mine, other, right)

    cols = pl.ds(pl.multiple_of(step * ROWS, ROWS), ROWS)
    first, second = two(inverse[...])
    q = (mm(first, right[:, cols], 1, 0) + mm(second, right[:, cols], 1, 0)) * share
    total = mm(c2[...], g2[...], 0, 0) + mm(c3[...], g3[...], 0, 0)
    new_error[...] = merged[...] + total * scale - mm(basis[...], q.astype(BF16), 0, 0)
    at_zl, at_core = step // 2, step % 2

    @pl.when((at_zl == zl) & (at_core == core))
    def _():
        factor_q[...] = q.T
        in_grad[...] = i0[...]

    @pl.when((at_zl == zl) & (at_core != core))
    def _():
        in_grad[...] = i1[...]

    @pl.when((at_zl != zl) & (at_core == core))
    def _():
        in_grad[...] = i2[...]

    @pl.when((at_zl != zl) & (at_core != core))
    def _():
        in_grad[...] = i3[...]


def size(shape, dtype):
    return math.prod(shape) * jnp.dtype(dtype).itemsize


def in_hbm(x):
    return pltpu.with_memory_space_constraint(x, pltpu.HBM)


def call(
    kernel, outs, args, flops, name, scratch=(), alias=None, limit=20, loose=(), held=(), free=False, sems=0
):
    args = [in_hbm(a) if n in held else a for n, a in enumerate(args)]
    moved = sum(size(a.shape, a.dtype) for a in args) + sum(size(s, d) for s, d in outs)
    scratch = [pltpu.VMEM(s, d) for s, d in scratch]
    if sems:
        scratch.append(pltpu.SemaphoreType.DMA((sems,)))
    return pl.pallas_call(
        kernel,
        out_shape=[(pltpu.HBM if free else jax.ShapeDtypeStruct)(s, d) for s, d in outs],
        in_specs=[
            SMEM if a.dtype == jnp.int32 else ANY if n in loose or n in held else VMEM
            for n, a in enumerate(args)
        ],
        out_specs=[pl.BlockSpec(s, lambda s=s: (0,) * len(s)) if free else VMEM for s, _ in outs],
        scratch_shapes=scratch,
        input_output_aliases=alias or {},
        compiler_params=pltpu.CompilerParams(vmem_limit_bytes=limit * 2**20),
        cost_estimate=pl.CostEstimate(flops=flops, bytes_accessed=moved, transcendentals=0),
        name=name,
    )(*args)


def call_grid(kernel, steps, outs, ins, args, flops, name, scratch=(), sems=0, limit=24):
    args = [a if spec in (SMEM, ANY, VMEM) else in_hbm(a) for a, spec in zip(args, ins)]
    moved = sum(size(a.shape, a.dtype) for a in args) + sum(size(s, d) for s, d, _ in outs)
    scratch = [pltpu.VMEM(s, d) for s, d in scratch]
    if sems:
        scratch.append(pltpu.SemaphoreType.DMA((sems,)))
    return pl.pallas_call(
        kernel,
        grid=(steps,),
        out_shape=[pltpu.HBM(s, d) for s, d, _ in outs],
        in_specs=ins,
        out_specs=[spec for _, _, spec in outs],
        scratch_shapes=scratch,
        compiler_params=pltpu.CompilerParams(vmem_limit_bytes=limit * 2**20),
        cost_estimate=pl.CostEstimate(flops=flops, bytes_accessed=moved, transcendentals=0),
        name=name,
    )(*args)


def whole(*shape):
    return pl.BlockSpec(shape, lambda j: (0,) * len(shape))


def column(rows):
    return pl.BlockSpec((rows, ROWS), lambda j: (0, j))


def rows_of(rows, cols):
    return pl.BlockSpec((rows, cols), lambda j: (j, 0))


CHUNKED = (CHUNKS, CHUNK_ROWS, CHUNK_COLS)
CHUNK = (CHUNK_ROWS, CHUNK_COLS)


def tied(x, *others):
    return lax.optimization_barrier((x,) + others)[0]


def across_plane(keep, send, beside=()):
    got = swap(send, "core")
    (half,) = call(add_kernel, [(CHUNKED, BF16)], (keep, tied(got, *beside)), 1_000_000, "add")
    parts = lax.all_to_all(half, ("y", "x"), 0, 0)
    (part,) = call(sum_kernel, [(CHUNK, F32)], (parts,), 1_000_000, "sum")
    return part


def across_z(part, beside=()):
    far = tied(swap(part, "zl"), *beside)
    part = part + far
    return (part,) + tuple(
        lax.ppermute(part, "zh", [(i, (i + step) % 4) for i in range(4)]) for step in (1, 2, 3)
    )


def back_over_plane(part, one, opposite, three, beside=()):
    (whole,) = call(
        spread_kernel,
        [(CHUNKED, BF16)],
        (tied(part, *beside), one, opposite, three),
        1_000_000,
        "spread",
    )
    return lax.all_to_all(whole, ("y", "x"), 0, 0)


def on_device(context, out_grad, weight, error, warm):
    scale = 1.0 / math.sqrt(TOK * 4)
    core = lax.axis_index("core")
    zl = lax.axis_index("zl")
    at = jnp.stack([zl, core]).astype(jnp.int32)
    error = error[0]
    tokens = ((TOK, ROWS), BF16)
    pair = ((2, TOK, ROWS), BF16)

    warm_far = swap(warm, "zl")
    warm_near = swap(warm, "core")
    quarter = rows_of(TOK // 4, ROWS)
    strip = rows_of(ROWS // 4, FEAT)
    c_own, c_near, c_far, high, low = call_grid(
        prepare_kernel,
        4,
        [tokens + (quarter,)] * 2
        + [pair + (pl.BlockSpec((2, TOK // 4, ROWS), lambda j: (0, j, 0)),)]
        + [((ROWS, FEAT), BF16, strip)] * 2,
        [SMEM, rows_of(TOK // 4, FEAT), strip],
        (at, context, error),
        4_000_000,
        "prepare",
    )
    warm_diag = swap(tied(warm_far, low), "core")

    big = ((ROWS, FEAT), BF16)
    keep, send = call(
        functools.partial(left_kernel, scale),
        [(CHUNKED, F32), (CHUNKED, BF16)],
        (at, out_grad, context, high, low, warm, warm_near, warm_far, warm_diag),
        2_000_000_000,
        "left",
        [((RANK, FEAT), F32), big, big],
        held=(3, 4),
        sems=2,
    )
    g_far = swap(tied(out_grad, warm_far, low), "zl")
    g_near = swap(tied(out_grad, warm_far, low), "core")
    part = across_plane(keep, send)
    g_diag = swap(tied(g_far, part), "core")
    c_near = swap(c_near, "core")
    zs = across_z(tied(part, g_far, g_near))
    (merged,) = call_grid(
        functools.partial(merge_kernel, scale),
        4,
        [((ROWS, FEAT), F32, column(ROWS))],
        [column(ROWS), whole(TOK, ROWS), whole(TOK, ROWS), column(TOK), column(TOK)],
        (error, c_own, c_near, out_grad, g_near),
        1_100_000_000,
        "merge",
    )
    c_far = swap(tied(c_far, zs[1]), "zl")
    mine = back_over_plane(*zs, beside=(g_diag, merged))

    i_own, i_near, i_far = call(
        grad_kernel,
        [tokens] * 2 + [pair],
        (out_grad, g_near, g_far, g_diag, weight),
        2_200_000_000,
        "grad",
        [big] + [((TOK, FEAT), BF16)] * 4,
        held=range(5),
        free=True,
        sems=5,
    )
    other = swap(tied(mine, i_own, c_far), "core")
    i_far = swap(i_far, "zl")
    i_near = swap(i_near, "core")

    keep, send, left = call(
        functools.partial(right_kernel, scale),
        [(CHUNKED, F32), (CHUNKED, BF16), ((RANK, FEAT), BF16)],
        (at, context, out_grad, high, low, mine, other),
        2_000_000_000,
        "right",
        [((RANK, FEAT), F32), big, big, (CHUNKED, BF16), (CHUNKED, BF16)],
        loose=(6,),
        held=(3, 4, 5),
        sems=4,
    )
    part = across_plane(keep, send)

    table = ((RANK, 2 * RANK), F32)
    (a,) = call(gram_kernel, [table], (left,), 300_000_000, "gram")
    part = tied(part, a, i_far, i_near)
    i_diag = swap(tied(i_far, part)[1], "core")
    c_diag = swap(c_far[1], "core")
    (a,) = call(
        functools.partial(step_kernel, PART), [table], (a,), 300_000_000, "step", alias={0: 0}
    )
    zs = across_z(part, (a,))
    (a,) = call(
        functools.partial(step_kernel, 2 * PART), [table], (a,), 300_000_000, "step", alias={0: 0}
    )
    mine = back_over_plane(*zs, beside=(a, c_diag, i_diag))
    inverse, basis = call(
        basis_kernel,
        [((RANK, RANK), F32), ((RANK, ROWS), BF16)],
        (at, a, left),
        300_000_000,
        "basis",
        [table],
    )
    other = swap(tied(mine, basis), "core")

    block_in = whole(TOK, ROWS)
    first = pl.BlockSpec((None, TOK, ROWS), lambda j: (0, 0, 0))
    new_error, factor_q, in_grad = call_grid(
        functools.partial(last_kernel, 1.0 / (SIZES[0] * SIZES[1] * SIZES[2]), scale),
        4,
        [
            ((ROWS, FEAT), F32, column(ROWS)),
            ((ROWS, RANK), F32, whole(ROWS, RANK)),
            ((TOK, FEAT), BF16, column(TOK)),
        ],
        [SMEM, ANY, ANY, VMEM, VMEM, column(ROWS), first, block_in, column(TOK), column(TOK)]
        + [block_in, block_in, first, block_in],
        (
            at, mine, other, inverse, basis, merged, c_far, c_diag, g_far, g_diag,
            i_own, i_near, i_far, i_diag,
        ),
        2_300_000_000,
        "last",
        [((RANK, FEAT), BF16), (CHUNKED, BF16), (CHUNKED, BF16)],
        sems=2,
    )
    return in_grad, new_error[None], factor_q


def solution(mesh):
    split = Mesh(np.asarray(mesh.devices).reshape(SIZES), AXES)
    every = ("zh", "y", "x", "zl", "core")
    shard = ("zl", "core")
    return jax.shard_map(
        on_device,
        mesh=split,
        in_specs=(
            P(every, None),
            P(every, None),
            P(shard, None),
            P(("zh", "y", "x"), shard, None),
            P(shard, None),
        ),
        out_specs=(P(every, None), P(("zh", "y", "x"), shard, None), P(shard, None)),
        check_vma=False,
    )
```

```python
import functools
import math

import jax
import jax.numpy as jnp
import numpy as np
from jax import lax
from jax.experimental import pallas as pl
from jax.experimental.pallas import tpu as pltpu
from jax.sharding import Mesh, PartitionSpec as P

BF16 = jnp.bfloat16
F32 = jnp.float32
HI = lax.Precision.HIGHEST
PART = 64
SUB = 8
AXES = ("zh", "y", "x", "zl", "core")
SIZES = (4, 4, 4, 2, 2)
ROWS = 512
RANK = 256
FEAT = 2048
TOK = 256
HALF = RANK // 2
CHUNKS, CHUNK_ROWS, CHUNK_COLS = 16, 16, 1024
VMEM = pl.BlockSpec(memory_space=pltpu.VMEM)
SMEM = pl.BlockSpec(memory_space=pltpu.SMEM)
ANY = pl.BlockSpec(memory_space=pl.ANY)


def swap(x, axis):
    return lax.ppermute(x, axis, [(0, 1), (1, 0)])


def mm(a, b, ca, cb):
    return lax.dot_general(a, b, (((ca,), (cb,)), ((), ())), preferred_element_type=F32)


def two(x):
    high = x.astype(BF16)
    return high, (x - high.astype(F32)).astype(BF16)


def chunk_at(n):
    return n // 2 * CHUNK_ROWS, n % 2 * CHUNK_COLS


def fetch(sources, targets, sems):
    copies = [
        pltpu.make_async_copy(src, dst, sems.at[n]) for n, (src, dst) in enumerate(zip(sources, targets))
    ]
    for copy in copies:
        copy.start()
    return copies


def split_halves(core, total, keep, send):
    for n in range(CHUNKS):
        row, col = chunk_at(n)
        cols = pl.ds(col, CHUNK_COLS)
        keep[n] = total[pl.ds(pl.multiple_of(core * HALF + row, CHUNK_ROWS), CHUNK_ROWS), cols]
        send[n] = total[
            pl.ds(pl.multiple_of((1 - core) * HALF + row, CHUNK_ROWS), CHUNK_ROWS), cols
        ].astype(send.dtype)


def join_halves(core, mine, other, whole):
    for n in range(CHUNKS):
        row, col = chunk_at(n)
        cols = pl.ds(col, CHUNK_COLS)
        whole[pl.ds(pl.multiple_of(core * HALF + row, CHUNK_ROWS), CHUNK_ROWS), cols] = mine[n]
        whole[pl.ds(pl.multiple_of((1 - core) * HALF + row, CHUNK_ROWS), CHUNK_ROWS), cols] = other[n]


def block(zl, core):
    return pl.ds(pl.multiple_of((zl * 2 + core) * ROWS, ROWS), ROWS)


def prepare_kernel(at, ctx, err, own, near, far, low):
    zl, core = at[0], at[1]
    own[...] = ctx[:, block(zl, core)]
    near[...] = ctx[:, block(zl, 1 - core)]
    far[0] = ctx[:, block(1 - zl, core)]
    far[1] = ctx[:, block(1 - zl, 1 - core)]
    rows = err.shape[0]
    low[pl.ds(pl.multiple_of(pl.program_id(0) * rows, rows), rows), :] = err[...].astype(BF16)


def left_kernel(scale, at, og, ctx, low, w0, w1, w2, w3, keep, send, total):
    zl, core = at[0], at[1]
    where = ((zl, core), (zl, 1 - core), (1 - zl, core), (1 - zl, 1 - core))
    proj = jnp.zeros((TOK, RANK), F32)
    own = jnp.zeros((ROWS, RANK), F32)
    for (a, b), w in zip(where, (w0, w1, w2, w3)):
        cols = block(a, b)
        proj += mm(og[:, cols], w[...], 1, 0)
        own += mm(low[:, cols], w[...], 1, 0)
    first, second = two(proj * scale)
    total[...] = mm(first, ctx[...], 0, 0) + mm(second, ctx[...], 0, 0)
    total[:, block(zl, core)] += own.T
    split_halves(core, total, keep, send)


def right_kernel(
    scale, at, ctx, og, low_hbm, mine_hbm, other_hbm,
    keep, send, left, total, low, mine, other, sems,
):
    zl, core = at[0], at[1]
    copies = fetch((mine_hbm, other_hbm, low_hbm), (mine, other, low), sems)
    copies[0].wait()
    copies[1].wait()
    join_halves(core, mine, other, left)
    first, second = two(mm(ctx[...], left[...], 1, 1) * scale)
    total[...] = mm(first, og[...], 0, 0) + mm(second, og[...], 0, 0)
    own = left[:, block(zl, core)]
    copies[2].wait()
    total[...] += mm(own, low[...], 1, 0)
    split_halves(core, total, keep, send)


def add_kernel(keep, got, out):
    out[...] = (keep[...] + got[...].astype(F32)).astype(BF16)


def sum_kernel(parts, out):
    out[...] = parts[...].astype(F32).sum(0)


def spread_kernel(part, one, opposite, three, out):
    whole = ((part[...] + opposite[...]) + (one[...] + three[...])).astype(BF16)
    for n in range(CHUNKS):
        out[n] = whole


def row_of(x, k):
    return jnp.broadcast_to(x[k : k + 1, :], x.shape)


def factor_block(rows):
    shape = rows[0].shape
    sub = lax.broadcasted_iota(jnp.int32, shape, 0)
    for p in range(len(rows)):
        cols = [
            [jnp.broadcast_to(r[:, SUB * p + k : SUB * p + k + 1], shape) for k in range(SUB)]
            for r in rows[p:]
        ]
        for k in range(SUB):
            diagonal = row_of(cols[0][k], k)
            inv = lax.rsqrt(diagonal)
            inv = inv * (1.5 - 0.5 * diagonal * inv * inv)
            pivot = row_of(rows[p], k) * inv
            later = [row_of(cols[0][j], k) * inv for j in range(k + 1, SUB)]
            for g, col in enumerate(cols, p):
                times = col[k] * inv
                if g == p:
                    times = jnp.where(sub > k, times, 0.0)
                rows[g] = rows[g] - times * pivot
                if g == p:
                    rows[g] = jnp.where(sub == k, pivot, rows[g])
                for j, entry in zip(range(k + 1, SUB), later):
                    col[j] = col[j] - times * entry
    return rows


def dot_hi(a, b, ca, cb):
    return lax.dot_general(
        a, b, (((ca,), (cb,)), ((), ())), precision=HI, preferred_element_type=F32
    )


def eye(n):
    shape = (n, n)
    same = lax.broadcasted_iota(jnp.int32, shape, 0) == lax.broadcasted_iota(jnp.int32, shape, 1)
    return same.astype(F32)


def eliminate(start, a):
    stop = start + PART
    rows = jnp.concatenate([a[start:stop, start:stop], eye(PART)], 1)
    rows = factor_block([rows[n : n + SUB] for n in range(0, PART, SUB)])
    inverse = jnp.concatenate(rows, 0)[:, PART:]
    panel = dot_hi(inverse, a[start:stop, :], 1, 0)
    a[start:stop, :] = panel
    if stop < RANK:
        a[stop:, :] = a[stop:, :] - dot_hi(panel[:, stop:RANK], panel, 0, 0)


def gram_kernel(left, a):
    a[:, :RANK] = mm(left[...], left[...], 1, 1)
    a[:, RANK:] = eye(RANK)
    eliminate(0, a)


def step_kernel(start, a_in, a):
    eliminate(start, a)


def basis_kernel(at, a_in, left, inverse, basis, a):
    a[...] = a_in[...]
    eliminate(RANK - PART, a)
    inverse[...] = a[:, RANK:]
    first, second = two(a[:, RANK:])
    own = left[:, block(at[0], at[1])]
    basis[...] = (mm(first, own, 1, 0) + mm(second, own, 1, 0)).astype(BF16)


def grad_kernel(h0, h1, h2, h3, weight_hbm, o0, o1, far, weight, g0, g1, g2, g3, sems):
    copies = fetch((weight_hbm, h0, h1, h2, h3), (weight, g0, g1, g2, g3), sems)
    copies[0].wait()
    for g, o, copy in zip((g0, g1, g2, g3), (o0, o1, far.at[0], far.at[1]), copies[1:]):
        copy.wait()
        o[...] = mm(g[...], weight[...], 1, 1).astype(BF16)


def merge_kernel(scale, err, c0, c1, g0, g1, out, t0, t1):
    @pl.when(pl.program_id(0) == 0)
    def _():
        t0[...] = c0[...].T
        t1[...] = c1[...].T

    total = mm(t0[...], g0[...], 1, 0) + mm(t1[...], g1[...], 1, 0)
    out[...] = err[...] + total * scale


def last_kernel(
    share, at, mine_hbm, other_hbm, inverse, basis, merged, i0, i1, i2, i3,
    new_error, factor_q, in_grad, right, mine, other, sems,
):
    step = pl.program_id(0)
    zl, core = at[0], at[1]

    @pl.when(step == 0)
    def _():
        copies = fetch((mine_hbm, other_hbm), (mine, other), sems)
        copies[0].wait()
        copies[1].wait()
        join_halves(core, mine, other, right)

    cols = pl.ds(pl.multiple_of(step * ROWS, ROWS), ROWS)
    first, second = two(inverse[...])
    q = (mm(first, right[:, cols], 1, 0) + mm(second, right[:, cols], 1, 0)) * share
    new_error[...] = merged[...] - mm(basis[...], q.astype(BF16), 0, 0)
    at_zl, at_core = step // 2, step % 2

    @pl.when((at_zl == zl) & (at_core == core))
    def _():
        factor_q[...] = q.T
        in_grad[...] = i0[...]

    @pl.when((at_zl == zl) & (at_core != core))
    def _():
        in_grad[...] = i1[...]

    @pl.when((at_zl != zl) & (at_core == core))
    def _():
        in_grad[...] = i2[...]

    @pl.when((at_zl != zl) & (at_core != core))
    def _():
        in_grad[...] = i3[...]


def size(shape, dtype):
    return math.prod(shape) * jnp.dtype(dtype).itemsize


def in_hbm(x):
    return pltpu.with_memory_space_constraint(x, pltpu.HBM)


def call(
    kernel, outs, args, flops, name, scratch=(), alias=None, limit=20, loose=(), held=(), free=False, sems=0
):
    args = [in_hbm(a) if n in held else a for n, a in enumerate(args)]
    moved = sum(size(a.shape, a.dtype) for a in args) + sum(size(s, d) for s, d in outs)
    scratch = [pltpu.VMEM(s, d) for s, d in scratch]
    if sems:
        scratch.append(pltpu.SemaphoreType.DMA((sems,)))
    return pl.pallas_call(
        kernel,
        out_shape=[(pltpu.HBM if free else jax.ShapeDtypeStruct)(s, d) for s, d in outs],
        in_specs=[
            SMEM if a.dtype == jnp.int32 else ANY if n in loose or n in held else VMEM
            for n, a in enumerate(args)
        ],
        out_specs=[pl.BlockSpec(s, lambda s=s: (0,) * len(s)) if free else VMEM for s, _ in outs],
        scratch_shapes=scratch,
        input_output_aliases=alias or {},
        compiler_params=pltpu.CompilerParams(vmem_limit_bytes=limit * 2**20),
        cost_estimate=pl.CostEstimate(flops=flops, bytes_accessed=moved, transcendentals=0),
        name=name,
    )(*args)


def call_grid(kernel, steps, outs, ins, args, flops, name, scratch=(), sems=0, limit=24, loose=()):
    args = [
        a if spec in (SMEM, ANY, VMEM) or n in loose else in_hbm(a)
        for n, (a, spec) in enumerate(zip(args, ins))
    ]
    moved = sum(size(a.shape, a.dtype) for a in args) + sum(size(s, d) for s, d, _ in outs)
    scratch = [pltpu.VMEM(s, d) for s, d in scratch]
    if sems:
        scratch.append(pltpu.SemaphoreType.DMA((sems,)))
    return pl.pallas_call(
        kernel,
        grid=(steps,),
        out_shape=[
            (jax.ShapeDtypeStruct if spec is VMEM else pltpu.HBM)(s, d) for s, d, spec in outs
        ],
        in_specs=ins,
        out_specs=[spec for _, _, spec in outs],
        scratch_shapes=scratch,
        compiler_params=pltpu.CompilerParams(vmem_limit_bytes=limit * 2**20),
        cost_estimate=pl.CostEstimate(flops=flops, bytes_accessed=moved, transcendentals=0),
        name=name,
    )(*args)


def whole(*shape):
    return pl.BlockSpec(shape, lambda j: (0,) * len(shape))


def column(rows):
    return pl.BlockSpec((rows, ROWS), lambda j: (0, j))


def rows_of(rows, cols):
    return pl.BlockSpec((rows, cols), lambda j: (j, 0))


CHUNKED = (CHUNKS, CHUNK_ROWS, CHUNK_COLS)
CHUNK = (CHUNK_ROWS, CHUNK_COLS)


def tied(x, *others):
    return lax.optimization_barrier((x,) + others)[0]


def across_plane(keep, send, beside=()):
    got = swap(send, "core")
    (half,) = call(add_kernel, [(CHUNKED, BF16)], (keep, got), 1_000_000, "add")
    parts = tied(lax.all_to_all(half, ("y", "x"), 0, 0), *beside)
    (part,) = call(sum_kernel, [(CHUNK, F32)], (parts,), 1_000_000, "sum")
    return part


def across_z(part, beside=()):
    far = tied(swap(part, "zl"), *beside)
    part = part + far
    return (part,) + tuple(
        lax.ppermute(part, "zh", [(i, (i + step) % 4) for i in range(4)]) for step in (1, 2, 3)
    )


def back_over_plane(part, one, opposite, three, beside=()):
    (whole,) = call(
        spread_kernel,
        [(CHUNKED, BF16)],
        (tied(part, *beside), one, opposite, three),
        1_000_000,
        "spread",
    )
    return lax.all_to_all(whole, ("y", "x"), 0, 0)


def on_device(context, out_grad, weight, error, warm):
    scale = 1.0 / math.sqrt(TOK * 4)
    core = lax.axis_index("core")
    zl = lax.axis_index("zl")
    at = jnp.stack([zl, core]).astype(jnp.int32)
    error = error[0]
    tokens = ((TOK, ROWS), BF16)
    pair = ((2, TOK, ROWS), BF16)

    warm_far = swap(warm, "zl")
    warm_near = swap(warm, "core")
    quarter = rows_of(TOK // 4, ROWS)
    strip = rows_of(ROWS // 4, FEAT)
    c_own, c_near, c_far, low = call_grid(
        prepare_kernel,
        4,
        [tokens + (quarter,)] * 2
        + [pair + (pl.BlockSpec((2, TOK // 4, ROWS), lambda j: (0, j, 0)),)]
        + [((ROWS, FEAT), BF16, VMEM)],
        [SMEM, rows_of(TOK // 4, FEAT), strip],
        (at, context, error),
        4_000_000,
        "prepare",
    )
    warm_diag = swap(tied(warm_far, low), "core")

    big = ((ROWS, FEAT), BF16)
    keep, send = call(
        functools.partial(left_kernel, scale),
        [(CHUNKED, F32), (CHUNKED, BF16)],
        (at, out_grad, context, low, warm, warm_near, warm_far, warm_diag),
        2_000_000_000,
        "left",
        [((RANK, FEAT), F32)],
    )
    g_far = swap(tied(out_grad, warm_far, low), "zl")
    g_near = swap(tied(out_grad, warm_far, low), "core")
    c_near = swap(c_near, "core")
    turned = [((ROWS, TOK), BF16)] * 2
    (merged,) = call_grid(
        functools.partial(merge_kernel, scale),
        4,
        [((ROWS, FEAT), F32, column(ROWS))],
        [column(ROWS), VMEM, VMEM, column(TOK), column(TOK)],
        (error, c_own, c_near, out_grad, g_near),
        1_100_000_000,
        "merge",
        turned,
        loose=(3, 4),
    )
    part = across_plane(keep, send, (merged,))
    g_diag = swap(tied(g_far, part), "core")
    zs = across_z(tied(part, g_far))
    c_far = swap(tied(c_far, zs[1]), "zl")
    mine = back_over_plane(*zs)

    i_own, i_near, i_far = call(
        grad_kernel,
        [tokens] * 2 + [pair],
        (out_grad, g_near, g_far, g_diag, weight),
        2_200_000_000,
        "grad",
        [big] + [((TOK, FEAT), BF16)] * 4,
        held=range(5),
        free=True,
        sems=5,
    )
    other = swap(tied(mine, i_own, c_far), "core")
    i_far = swap(i_far, "zl")
    i_near = swap(i_near, "core")

    keep, send, left = call(
        functools.partial(right_kernel, scale),
        [(CHUNKED, F32), (CHUNKED, BF16), ((RANK, FEAT), BF16)],
        (at, context, out_grad, low, mine, other),
        2_000_000_000,
        "right",
        [((RANK, FEAT), F32), big, (CHUNKED, BF16), (CHUNKED, BF16)],
        loose=(5,),
        held=(3, 4),
        sems=3,
    )

    table = ((RANK, 2 * RANK), F32)
    (a,) = call(gram_kernel, [table], (left,), 300_000_000, "gram")
    c_diag = swap(c_far, "core")
    (a,) = call(
        functools.partial(step_kernel, PART), [table], (a,), 300_000_000, "step", alias={0: 0}
    )
    part = across_plane(keep, send, (a,))
    part = tied(part, i_far, i_near)
    zs = across_z(part)
    i_diag = swap(tied(i_far, zs[0]), "core")
    (a,) = call(
        functools.partial(step_kernel, 2 * PART), [table], (a,), 300_000_000, "step", alias={0: 0}
    )
    mine = back_over_plane(*zs, beside=(a, c_diag, i_diag))
    inverse, basis = call(
        basis_kernel,
        [((RANK, RANK), F32), ((RANK, ROWS), BF16)],
        (at, a, left),
        300_000_000,
        "basis",
        [table],
    )
    block_in = whole(TOK, ROWS)
    first = pl.BlockSpec((None, TOK, ROWS), lambda j: (0, 0, 0))
    second = pl.BlockSpec((None, TOK, ROWS), lambda j: (1, 0, 0))
    (merged,) = call_grid(
        functools.partial(merge_kernel, scale),
        4,
        [((ROWS, FEAT), F32, column(ROWS))],
        [column(ROWS), first, second, column(TOK), column(TOK)],
        (merged, c_far, c_diag, g_far, g_diag),
        1_100_000_000,
        "merge",
        turned,
    )
    other = swap(tied(mine, basis, merged), "core")

    new_error, factor_q, in_grad = call_grid(
        functools.partial(last_kernel, 1.0 / (SIZES[0] * SIZES[1] * SIZES[2])),
        4,
        [
            ((ROWS, FEAT), F32, column(ROWS)),
            ((ROWS, RANK), F32, whole(ROWS, RANK)),
            ((TOK, FEAT), BF16, column(TOK)),
        ],
        [SMEM, ANY, ANY, VMEM, VMEM, column(ROWS)]
        + [block_in, block_in, first, second],
        (at, mine, other, inverse, basis, merged, i_own, i_near, i_far, i_diag),
        1_200_000_000,
        "last",
        [((RANK, FEAT), BF16), (CHUNKED, BF16), (CHUNKED, BF16)],
        sems=2,
    )
    return in_grad, new_error[None], factor_q


def solution(mesh):
    split = Mesh(np.asarray(mesh.devices).reshape(SIZES), AXES)
    every = ("zh", "y", "x", "zl", "core")
    shard = ("zl", "core")
    return jax.shard_map(
        on_device,
        mesh=split,
        in_specs=(
            P(every, None),
            P(every, None),
            P(shard, None),
            P(("zh", "y", "x"), shard, None),
            P(shard, None),
        ),
        out_specs=(P(every, None), P(("zh", "y", "x"), shard, None), P(shard, None)),
        check_vma=False,
    )
```

```python
import functools
import math

import jax
import jax.numpy as jnp
import numpy as np
from jax import lax
from jax.experimental import pallas as pl
from jax.experimental.pallas import tpu as pltpu
from jax.sharding import Mesh, PartitionSpec as P

BF16 = jnp.bfloat16
F32 = jnp.float32
HI = lax.Precision.HIGHEST
PART = 64
SUB = 8
AXES = ("zh", "y", "x", "zl", "core")
SIZES = (4, 4, 4, 2, 2)
ROWS = 512
RANK = 256
FEAT = 2048
TOK = 256
HALF = RANK // 2
CHUNKS, CHUNK_ROWS, CHUNK_COLS = 16, 16, 1024
VMEM = pl.BlockSpec(memory_space=pltpu.VMEM)
SMEM = pl.BlockSpec(memory_space=pltpu.SMEM)
ANY = pl.BlockSpec(memory_space=pl.ANY)


def swap(x, axis):
    return lax.ppermute(x, axis, [(0, 1), (1, 0)])


def mm(a, b, ca, cb):
    return lax.dot_general(a, b, (((ca,), (cb,)), ((), ())), preferred_element_type=F32)


def two(x):
    high = x.astype(BF16)
    return high, (x - high.astype(F32)).astype(BF16)


def chunk_at(n):
    return n // 2 * CHUNK_ROWS, n % 2 * CHUNK_COLS


def fetch(sources, targets, sems):
    copies = [
        pltpu.make_async_copy(src, dst, sems.at[n]) for n, (src, dst) in enumerate(zip(sources, targets))
    ]
    for copy in copies:
        copy.start()
    return copies


def split_halves(core, total, keep, send):
    for n in range(CHUNKS):
        row, col = chunk_at(n)
        cols = pl.ds(col, CHUNK_COLS)
        keep[n] = total[pl.ds(pl.multiple_of(core * HALF + row, CHUNK_ROWS), CHUNK_ROWS), cols]
        send[n] = total[
            pl.ds(pl.multiple_of((1 - core) * HALF + row, CHUNK_ROWS), CHUNK_ROWS), cols
        ].astype(send.dtype)


def block(zl, core):
    return pl.ds(pl.multiple_of((zl * 2 + core) * ROWS, ROWS), ROWS)


def prepare_kernel(at, ctx, err, own, near, far, low, kept):
    zl, core = at[0], at[1]
    own[...] = ctx[:, block(zl, core)]
    near[...] = ctx[:, block(zl, 1 - core)]
    far[0] = ctx[:, block(1 - zl, core)]
    far[1] = ctx[:, block(1 - zl, 1 - core)]
    rows = err.shape[0]
    kept[...] = err[...].astype(BF16)
    low[pl.ds(pl.multiple_of(pl.program_id(0) * rows, rows), rows), :] = kept[...]


def left_kernel(scale, at, og, ctx, low, w0, w1, w2, w3, keep, send, total):
    zl, core = at[0], at[1]
    where = ((zl, core), (zl, 1 - core), (1 - zl, core), (1 - zl, 1 - core))
    proj = jnp.zeros((TOK, RANK), F32)
    own = jnp.zeros((ROWS, RANK), F32)
    for (a, b), w in zip(where, (w0, w1, w2, w3)):
        cols = block(a, b)
        proj += mm(og[:, cols], w[...], 1, 0)
        own += mm(low[:, cols], w[...], 1, 0)
    first, second = two(proj * scale)
    total[...] = mm(first, ctx[...], 0, 0) + mm(second, ctx[...], 0, 0)
    total[:, block(zl, core)] += own.T
    split_halves(core, total, keep, send)


def unchunk(chunks, half):
    for n in range(CHUNKS):
        row, col = chunk_at(n)
        half[row : row + CHUNK_ROWS, col : col + CHUNK_COLS] = chunks[n]


def right_kernel(scale, at, ctx, og, chunks, low_hbm, out, half_hbm, low, half, total, sems):
    copy = pltpu.make_async_copy(low_hbm, low, sems.at[0])
    copy.start()
    unchunk(chunks, half)
    back = pltpu.make_async_copy(half, half_hbm, sems.at[1])
    back.start()
    first, second = two(mm(half[...], ctx[...], 1, 1) * scale)
    total[...] = mm(first, og[...], 1, 0) + mm(second, og[...], 1, 0)
    own = half[:, block(at[0], at[1])]
    copy.wait()
    total[...] += mm(own, low[...], 1, 0)
    for n in range(CHUNKS):
        row, col = chunk_at(n)
        out[n] = total[row : row + CHUNK_ROWS, col : col + CHUNK_COLS].astype(out.dtype)
    back.wait()


def add_kernel(keep, got, out):
    out[...] = (keep[...] + got[...].astype(F32)).astype(BF16)


def sum_kernel(parts, out):
    out[...] = parts[...].astype(F32).sum(0)


def spread_kernel(part, one, opposite, three, out):
    whole = ((part[...] + opposite[...]) + (one[...] + three[...])).astype(BF16)
    for n in range(CHUNKS):
        out[n] = whole


def row_of(x, k):
    return jnp.broadcast_to(x[k : k + 1, :], x.shape)


def factor_block(rows):
    shape = rows[0].shape
    sub = lax.broadcasted_iota(jnp.int32, shape, 0)
    for p in range(len(rows)):
        cols = [
            [jnp.broadcast_to(r[:, SUB * p + k : SUB * p + k + 1], shape) for k in range(SUB)]
            for r in rows[p:]
        ]
        for k in range(SUB):
            diagonal = row_of(cols[0][k], k)
            inv = lax.rsqrt(diagonal)
            inv = inv * (1.5 - 0.5 * diagonal * inv * inv)
            pivot = row_of(rows[p], k) * inv
            later = [row_of(cols[0][j], k) * inv for j in range(k + 1, SUB)]
            for g, col in enumerate(cols, p):
                times = col[k] * inv
                if g == p:
                    times = jnp.where(sub > k, times, 0.0)
                rows[g] = rows[g] - times * pivot
                if g == p:
                    rows[g] = jnp.where(sub == k, pivot, rows[g])
                for j, entry in zip(range(k + 1, SUB), later):
                    col[j] = col[j] - times * entry
    return rows


def dot_hi(a, b, ca, cb):
    return lax.dot_general(
        a, b, (((ca,), (cb,)), ((), ())), precision=HI, preferred_element_type=F32
    )


def eye(n):
    shape = (n, n)
    same = lax.broadcasted_iota(jnp.int32, shape, 0) == lax.broadcasted_iota(jnp.int32, shape, 1)
    return same.astype(F32)


def eliminate(start, a):
    stop = start + PART
    rows = jnp.concatenate([a[start:stop, start:stop], eye(PART)], 1)
    rows = factor_block([rows[n : n + SUB] for n in range(0, PART, SUB)])
    inverse = jnp.concatenate(rows, 0)[:, PART:]
    panel = dot_hi(inverse, a[start:stop, :], 1, 0)
    a[start:stop, :] = panel
    if stop < RANK:
        a[stop:, :] = a[stop:, :] - dot_hi(panel[:, stop:RANK], panel, 0, 0)


def gram_kernel(at, mine_hbm, other_hbm, a, left, sems):
    core = at[1]
    mine = left.at[pl.ds(pl.multiple_of(core * HALF, HALF), HALF), :]
    other = left.at[pl.ds(pl.multiple_of((1 - core) * HALF, HALF), HALF), :]
    for copy in fetch((mine_hbm, other_hbm), (mine, other), sems):
        copy.wait()
    a[:, :RANK] = mm(left[...], left[...], 1, 1)
    a[:, RANK:] = eye(RANK)
    eliminate(0, a)


def step_kernel(start, a_in, a):
    eliminate(start, a)


def basis_kernel(at, a_in, left, inverse, basis, a):
    a[...] = a_in[...]
    eliminate(RANK - PART, a)
    inverse[...] = a[:, RANK:]
    first, second = two(a[:, RANK:])
    own = left[:, block(at[0], at[1])]
    basis[...] = (mm(first, own, 1, 0) + mm(second, own, 1, 0)).astype(BF16).T


def grad_kernel(h0, h1, h2, h3, weight_hbm, o0, o1, far, weight, g0, g1, g2, g3, sems):
    copies = fetch((weight_hbm, h0, h1, h2, h3), (weight, g0, g1, g2, g3), sems)
    copies[0].wait()
    for g, o, copy in zip((g0, g1, g2, g3), (o0, o1, far.at[0], far.at[1]), copies[1:]):
        copy.wait()
        o[...] = mm(g[...], weight[...], 1, 1).astype(BF16)


def merge_kernel(scale, err, c0, c1, g0, g1, out, t0, t1):
    step = pl.program_id(0)

    @pl.when(step == 0)
    def _():
        t0[...] = c0[...].T
        t1[...] = c1[...].T

    total = mm(t0[...], g0[...], 1, 0) + mm(t1[...], g1[...], 1, 0)
    out[...] = err[...] + total * scale


def columns_of(inverse, half):
    return inverse[:, pl.ds(pl.multiple_of(half * HALF, HALF), HALF)]


def begin_kernel(at, chunks, inverse, c2, c3, out, t2, t3, half):
    t2[...] = c2[0].T
    t3[...] = c3[1].T
    unchunk(chunks, half)
    first, second = two(columns_of(inverse, at[1]))
    out[...] = mm(first, half[...], 1, 0) + mm(second, half[...], 1, 0)


def last_kernel(
    share, scale, at, other, inverse, basis, begun, t2, t3, merged, g2, g3, i0, i1, i2, i3,
    new_error, factor_q, in_grad, half,
):
    step = pl.program_id(0)
    zl, core = at[0], at[1]

    @pl.when(step == 0)
    def _():
        unchunk(other, half)

    cols = pl.ds(pl.multiple_of(step * ROWS, ROWS), ROWS)
    first, second = two(columns_of(inverse, 1 - core))
    q = mm(first, half[:, cols], 1, 0) + mm(second, half[:, cols], 1, 0)
    q = (begun[:, cols] + q) * share
    total = mm(t2[...], g2[...], 1, 0) + mm(t3[...], g3[...], 1, 0)
    new_error[...] = merged[...] + total * scale - mm(basis[...], q.astype(BF16), 1, 0)
    at_zl, at_core = step // 2, step % 2

    @pl.when((at_zl == zl) & (at_core == core))
    def _():
        factor_q[...] = q.T
        in_grad[...] = i0[...]

    @pl.when((at_zl == zl) & (at_core != core))
    def _():
        in_grad[...] = i1[...]

    @pl.when((at_zl != zl) & (at_core == core))
    def _():
        in_grad[...] = i2[...]

    @pl.when((at_zl != zl) & (at_core != core))
    def _():
        in_grad[...] = i3[...]


def size(shape, dtype):
    return math.prod(shape) * jnp.dtype(dtype).itemsize


def in_hbm(x):
    return pltpu.with_memory_space_constraint(x, pltpu.HBM)


def call(
    kernel, outs, args, flops, name, scratch=(), alias=None, limit=20, loose=(), held=(), free=False, sems=0
):
    args = [in_hbm(a) if n in held else a for n, a in enumerate(args)]
    moved = sum(size(a.shape, a.dtype) for a in args) + sum(size(s, d) for s, d in outs)
    scratch = [pltpu.VMEM(s, d) for s, d in scratch]
    if sems:
        scratch.append(pltpu.SemaphoreType.DMA((sems,)))
    return pl.pallas_call(
        kernel,
        out_shape=[(pltpu.HBM if free else jax.ShapeDtypeStruct)(s, d) for s, d in outs],
        in_specs=[
            SMEM if a.dtype == jnp.int32 else ANY if n in loose or n in held else VMEM
            for n, a in enumerate(args)
        ],
        out_specs=[pl.BlockSpec(s, lambda s=s: (0,) * len(s)) if free else VMEM for s, _ in outs],
        scratch_shapes=scratch,
        input_output_aliases=alias or {},
        compiler_params=pltpu.CompilerParams(vmem_limit_bytes=limit * 2**20),
        cost_estimate=pl.CostEstimate(flops=flops, bytes_accessed=moved, transcendentals=0),
        name=name,
    )(*args)


def call_grid(kernel, steps, outs, ins, args, flops, name, scratch=(), sems=0, limit=24, loose=(), alias=None):
    args = [
        a if spec in (SMEM, ANY, VMEM) or n in loose else in_hbm(a)
        for n, (a, spec) in enumerate(zip(args, ins))
    ]
    moved = sum(size(a.shape, a.dtype) for a in args) + sum(size(s, d) for s, d, _ in outs)
    scratch = [pltpu.VMEM(s, d) for s, d in scratch]
    if sems:
        scratch.append(pltpu.SemaphoreType.DMA((sems,)))
    return pl.pallas_call(
        kernel,
        grid=(steps,),
        out_shape=[
            (jax.ShapeDtypeStruct if spec is VMEM else pltpu.HBM)(s, d) for s, d, spec in outs
        ],
        in_specs=ins,
        out_specs=[spec for _, _, spec in outs],
        scratch_shapes=scratch,
        input_output_aliases=alias or {},
        compiler_params=pltpu.CompilerParams(vmem_limit_bytes=limit * 2**20),
        cost_estimate=pl.CostEstimate(flops=flops, bytes_accessed=moved, transcendentals=0),
        name=name,
    )(*args)


def whole(*shape):
    return pl.BlockSpec(shape, lambda j: (0,) * len(shape))


def column(rows):
    return pl.BlockSpec((rows, ROWS), lambda j: (0, j))


def rows_of(rows, cols):
    return pl.BlockSpec((rows, cols), lambda j: (j, 0))


CHUNKED = (CHUNKS, CHUNK_ROWS, CHUNK_COLS)
CHUNK = (CHUNK_ROWS, CHUNK_COLS)


def tied(x, *others):
    return lax.optimization_barrier((x,) + others)[0]


def across_plane(keep, send, beside=()):
    got = swap(send, "core")
    (half,) = call(add_kernel, [(CHUNKED, BF16)], (keep, got), 1_000_000, "add")
    parts = tied(lax.all_to_all(half, ("y", "x"), 0, 0), *beside)
    (part,) = call(sum_kernel, [(CHUNK, F32)], (parts,), 1_000_000, "sum")
    return part


def across_z(part, beside=()):
    far = tied(swap(part, "zl"), *beside)
    part = part + far
    return (part,) + tuple(
        lax.ppermute(part, "zh", [(i, (i + step) % 4) for i in range(4)]) for step in (1, 2, 3)
    )


def back_over_plane(part, one, opposite, three, beside=()):
    (whole,) = call(
        spread_kernel,
        [(CHUNKED, BF16)],
        (tied(part, *beside), one, opposite, three),
        1_000_000,
        "spread",
    )
    return lax.all_to_all(whole, ("y", "x"), 0, 0)


def on_device(context, out_grad, weight, error, warm):
    scale = 1.0 / math.sqrt(TOK * 4)
    core = lax.axis_index("core")
    zl = lax.axis_index("zl")
    at = jnp.stack([zl, core]).astype(jnp.int32)
    error = error[0]
    tokens = ((TOK, ROWS), BF16)
    pair = ((2, TOK, ROWS), BF16)

    warm_far = swap(warm, "zl")
    warm_near = swap(warm, "core")
    quarter = rows_of(TOK // 4, ROWS)
    strip = rows_of(ROWS // 4, FEAT)
    c_own, c_near, c_far, low, kept = call_grid(
        prepare_kernel,
        4,
        [tokens + (quarter,)] * 2
        + [pair + (pl.BlockSpec((2, TOK // 4, ROWS), lambda j: (0, j, 0)),)]
        + [((ROWS, FEAT), BF16, VMEM), ((ROWS, FEAT), BF16, strip)],
        [SMEM, rows_of(TOK // 4, FEAT), strip],
        (at, context, error),
        4_000_000,
        "prepare",
    )
    warm_diag = swap(tied(warm_far, low), "core")

    big = ((ROWS, FEAT), BF16)
    keep, send = call(
        functools.partial(left_kernel, scale),
        [(CHUNKED, F32), (CHUNKED, BF16)],
        (at, out_grad, context, low, warm, warm_near, warm_far, warm_diag),
        2_000_000_000,
        "left",
        [((RANK, FEAT), F32)],
    )
    g_far = swap(tied(out_grad, warm_far, low), "zl")
    g_near = swap(tied(out_grad, warm_far, low), "core")
    c_near = swap(c_near, "core")
    turned = [((ROWS, TOK), BF16)] * 2
    (merged,) = call_grid(
        functools.partial(merge_kernel, scale),
        4,
        [((ROWS, FEAT), F32, column(ROWS))],
        [column(ROWS), VMEM, VMEM, column(TOK), column(TOK)],
        (error, c_own, c_near, out_grad, g_near),
        1_100_000_000,
        "merge",
        turned,
        loose=(3, 4),
    )
    part = across_plane(keep, send, (merged,))
    g_diag = swap(tied(g_far, part), "core")
    zs = across_z(tied(part, g_far))
    c_far = swap(tied(c_far, *zs[1:]), "zl")
    mine = back_over_plane(*zs)

    i_own, i_near, i_far = call(
        grad_kernel,
        [tokens] * 2 + [pair],
        (out_grad, g_near, g_far, g_diag, weight),
        2_200_000_000,
        "grad",
        [big] + [((TOK, FEAT), BF16)] * 4,
        held=range(5),
        free=True,
        sems=5,
    )
    other = swap(tied(mine, i_own, c_far), "core")
    i_far = swap(i_far, "zl")
    i_near = swap(i_near, "core")

    half = ((HALF, FEAT), BF16)

    def right(chunks, dtype):
        return call_grid(
            functools.partial(right_kernel, scale),
            1,
            [(CHUNKED, dtype, VMEM), half + (ANY,)],
            [SMEM, VMEM, VMEM, VMEM, ANY],
            (at, context, out_grad, chunks, in_hbm(kept)),
            1_000_000_000,
            "right",
            [big, half, ((HALF, FEAT), F32)],
            sems=2,
        )

    keep, mine_half = right(mine, F32)
    send, other_half = right(tied(other, keep), BF16)

    table = ((RANK, 2 * RANK), F32)
    a, left = call(
        gram_kernel,
        [table, ((RANK, FEAT), BF16)],
        (at, mine_half, other_half),
        300_000_000,
        "gram",
        held=(1, 2),
        sems=2,
    )
    (a,) = call(
        functools.partial(step_kernel, PART), [table], (a,), 300_000_000, "step", alias={0: 0}
    )
    part = across_plane(keep, send, (a,))
    part = tied(part, i_far, i_near)
    zs = across_z(part)
    (a,) = call(
        functools.partial(step_kernel, 2 * PART), [table], (a,), 300_000_000, "step", alias={0: 0}
    )
    mine = back_over_plane(*zs, beside=(a,))
    c_diag = swap(tied(c_far, *zs[1:]), "core")
    i_diag = swap(tied(i_far, *zs[1:]), "core")
    inverse, basis = call(
        basis_kernel,
        [((RANK, RANK), F32), ((ROWS, RANK), BF16)],
        (at, a, left),
        300_000_000,
        "basis",
        [table],
    )
    block_in = whole(TOK, ROWS)
    first = pl.BlockSpec((None, TOK, ROWS), lambda j: (0, 0, 0))
    second = pl.BlockSpec((None, TOK, ROWS), lambda j: (1, 0, 0))
    other = swap(tied(mine, basis, c_diag, i_diag), "core")
    begun, t2, t3 = call(
        begin_kernel,
        [((RANK, FEAT), F32)] + turned,
        (at, mine, inverse, c_far, c_diag),
        300_000_000,
        "begin",
        [((HALF, FEAT), BF16)],
    )
    other = tied(other, begun)

    new_error, factor_q, in_grad = call_grid(
        functools.partial(last_kernel, 1.0 / (SIZES[0] * SIZES[1] * SIZES[2]), scale),
        4,
        [
            ((ROWS, FEAT), F32, column(ROWS)),
            ((ROWS, RANK), F32, whole(ROWS, RANK)),
            ((TOK, FEAT), BF16, column(TOK)),
        ],
        [SMEM] + [VMEM] * 6 + [column(ROWS), column(TOK), column(TOK)]
        + [block_in, block_in, first, second],
        (
            at, other, inverse, basis, begun, t2, t3, merged, g_far, g_diag,
            i_own, i_near, i_far, i_diag,
        ),
        2_000_000_000,
        "last",
        [((HALF, FEAT), BF16)],
    )
    return in_grad, new_error[None], factor_q


def solution(mesh):
    split = Mesh(np.asarray(mesh.devices).reshape(SIZES), AXES)
    every = ("zh", "y", "x", "zl", "core")
    shard = ("zl", "core")
    return jax.shard_map(
        on_device,
        mesh=split,
        in_specs=(
            P(every, None),
            P(every, None),
            P(shard, None),
            P(("zh", "y", "x"), shard, None),
            P(shard, None),
        ),
        out_specs=(P(every, None), P(("zh", "y", "x"), shard, None), P(shard, None)),
        check_vma=False,
    )
```

```python
import functools
import math

import jax
import jax.numpy as jnp
import numpy as np
from jax import lax
from jax.experimental import pallas as pl
from jax.experimental.pallas import tpu as pltpu
from jax.sharding import Mesh, PartitionSpec as P

BF16 = jnp.bfloat16
F32 = jnp.float32
HI = lax.Precision.HIGHEST
PART = 64
SUB = 8
AXES = ("zh", "y", "x", "zl", "core")
SIZES = (4, 4, 4, 2, 2)
ROWS = 512
RANK = 256
FEAT = 2048
TOK = 256
HALF = RANK // 2
CHUNKS, CHUNK_ROWS, CHUNK_COLS = 16, 16, 1024
VMEM = pl.BlockSpec(memory_space=pltpu.VMEM)
SMEM = pl.BlockSpec(memory_space=pltpu.SMEM)
ANY = pl.BlockSpec(memory_space=pl.ANY)


def swap(x, axis):
    return lax.ppermute(x, axis, [(0, 1), (1, 0)])


def mm(a, b, ca, cb):
    return lax.dot_general(a, b, (((ca,), (cb,)), ((), ())), preferred_element_type=F32)


def two(x):
    high = x.astype(BF16)
    return high, (x - high.astype(F32)).astype(BF16)


def chunk_at(n):
    return n // 2 * CHUNK_ROWS, n % 2 * CHUNK_COLS


def fetch(sources, targets, sems):
    copies = [
        pltpu.make_async_copy(src, dst, sems.at[n]) for n, (src, dst) in enumerate(zip(sources, targets))
    ]
    for copy in copies:
        copy.start()
    return copies


def split_halves(core, total, keep, send):
    for n in range(CHUNKS):
        row, col = chunk_at(n)
        cols = pl.ds(col, CHUNK_COLS)
        keep[n] = total[pl.ds(pl.multiple_of(core * HALF + row, CHUNK_ROWS), CHUNK_ROWS), cols]
        send[n] = total[
            pl.ds(pl.multiple_of((1 - core) * HALF + row, CHUNK_ROWS), CHUNK_ROWS), cols
        ].astype(send.dtype)


def block(zl, core):
    return pl.ds(pl.multiple_of((zl * 2 + core) * ROWS, ROWS), ROWS)


def prepare_kernel(at, ctx, err, own, near, far, low, kept):
    zl, core = at[0], at[1]
    own[...] = ctx[:, block(zl, core)]
    near[...] = ctx[:, block(zl, 1 - core)]
    far[0] = ctx[:, block(1 - zl, core)]
    far[1] = ctx[:, block(1 - zl, 1 - core)]
    rows = err.shape[0]
    kept[...] = err[...].astype(BF16)
    low[pl.ds(pl.multiple_of(pl.program_id(0) * rows, rows), rows), :] = kept[...]


def left_kernel(scale, at, og, ctx, low, w0, w1, w2, w3, keep, send, total):
    zl, core = at[0], at[1]
    where = ((zl, core), (zl, 1 - core), (1 - zl, core), (1 - zl, 1 - core))
    proj = jnp.zeros((TOK, RANK), F32)
    own = jnp.zeros((ROWS, RANK), F32)
    for (a, b), w in zip(where, (w0, w1, w2, w3)):
        cols = block(a, b)
        proj += mm(og[:, cols], w[...], 1, 0)
        own += mm(low[:, cols], w[...], 1, 0)
    first, second = two(proj * scale)
    total[...] = mm(first, ctx[...], 0, 0) + mm(second, ctx[...], 0, 0)
    total[:, block(zl, core)] += own.T
    split_halves(core, total, keep, send)


def unchunk(chunks, half):
    for n in range(CHUNKS):
        row, col = chunk_at(n)
        half[row : row + CHUNK_ROWS, col : col + CHUNK_COLS] = chunks[n]


def early_kernel(ctx, mine, half, proj):
    unchunk(mine, half)
    proj[...] = mm(half[...], ctx[...], 1, 1)


def right_kernel(
    scale, at, ctx, og, low_hbm, mine, proj_mine, other, keep, send, left, total, low, proj, sems
):
    zl, core = at[0], at[1]
    copy = pltpu.make_async_copy(low_hbm, low, sems.at[0])
    copy.start()
    here = pl.ds(pl.multiple_of(core * HALF, HALF), HALF)
    there = pl.ds(pl.multiple_of((1 - core) * HALF, HALF), HALF)
    unchunk(other, left.at[there, :])
    left[here, :] = mine[...]
    proj[here, :] = proj_mine[...]
    proj[there, :] = mm(left[there, :], ctx[...], 1, 1)
    first, second = two(proj[...] * scale)
    total[...] = mm(first, og[...], 1, 0) + mm(second, og[...], 1, 0)
    own = left[:, block(zl, core)]
    copy.wait()
    total[...] += mm(own, low[...], 1, 0)
    split_halves(core, total, keep, send)


def add_kernel(keep, got, out):
    out[...] = (keep[...] + got[...].astype(F32)).astype(BF16)


def sum_kernel(parts, out):
    out[...] = parts[...].astype(F32).sum(0)


def spread_kernel(part, one, opposite, three, out):
    part, one, opposite, three = (x[...].astype(F32) for x in (part, one, opposite, three))
    whole = ((part + opposite) + (one + three)).astype(BF16)
    for n in range(CHUNKS):
        out[n] = whole


def row_of(x, k):
    return jnp.broadcast_to(x[k : k + 1, :], x.shape)


def factor_block(rows):
    shape = rows[0].shape
    sub = lax.broadcasted_iota(jnp.int32, shape, 0)
    for p in range(len(rows)):
        cols = [
            [jnp.broadcast_to(r[:, SUB * p + k : SUB * p + k + 1], shape) for k in range(SUB)]
            for r in rows[p:]
        ]
        for k in range(SUB):
            diagonal = row_of(cols[0][k], k)
            inv = lax.rsqrt(diagonal)
            inv = inv * (1.5 - 0.5 * diagonal * inv * inv)
            pivot = row_of(rows[p], k) * inv
            later = [row_of(cols[0][j], k) * inv for j in range(k + 1, SUB)]
            for g, col in enumerate(cols, p):
                times = col[k] * inv
                if g == p:
                    times = jnp.where(sub > k, times, 0.0)
                rows[g] = rows[g] - times * pivot
                if g == p:
                    rows[g] = jnp.where(sub == k, pivot, rows[g])
                for j, entry in zip(range(k + 1, SUB), later):
                    col[j] = col[j] - times * entry
    return rows


def dot_hi(a, b, ca, cb):
    return lax.dot_general(
        a, b, (((ca,), (cb,)), ((), ())), precision=HI, preferred_element_type=F32
    )


def eye(n):
    shape = (n, n)
    same = lax.broadcasted_iota(jnp.int32, shape, 0) == lax.broadcasted_iota(jnp.int32, shape, 1)
    return same.astype(F32)


def eliminate(start, a):
    stop = start + PART
    rows = jnp.concatenate([a[start:stop, start:stop], eye(PART)], 1)
    rows = factor_block([rows[n : n + SUB] for n in range(0, PART, SUB)])
    inverse = jnp.concatenate(rows, 0)[:, PART:]
    panel = dot_hi(inverse, a[start:stop, :], 1, 0)
    a[start:stop, :] = panel
    if stop < RANK:
        a[stop:, :] = a[stop:, :] - dot_hi(panel[:, stop:RANK], panel, 0, 0)


def gram_kernel(left, a):
    a[:, :RANK] = mm(left[...], left[...], 1, 1)
    a[:, RANK:] = eye(RANK)
    eliminate(0, a)


def step_kernel(start, a_in, a):
    eliminate(start, a)


def basis_kernel(at, a_in, left, inverse, basis, a):
    a[...] = a_in[...]
    eliminate(RANK - PART, a)
    inverse[...] = a[:, RANK:]
    first, second = two(a[:, RANK:])
    own = left[:, block(at[0], at[1])]
    basis[...] = (mm(first, own, 1, 0) + mm(second, own, 1, 0)).astype(BF16).T


def grad_kernel(h0, h1, h2, h3, weight_hbm, o0, o1, far, weight, g0, g1, g2, g3, sems):
    copies = fetch((weight_hbm, h0, h1, h2, h3), (weight, g0, g1, g2, g3), sems)
    copies[0].wait()
    for g, o, copy in zip((g0, g1, g2, g3), (o0, o1, far.at[0], far.at[1]), copies[1:]):
        copy.wait()
        o[...] = mm(g[...], weight[...], 1, 1).astype(BF16)


def merge_kernel(scale, err, c0, c1, g0, g1, out, t0, t1):
    step = pl.program_id(0)

    @pl.when(step == 0)
    def _():
        t0[...] = c0[...].T
        t1[...] = c1[...].T

    total = mm(t0[...], g0[...], 1, 0) + mm(t1[...], g1[...], 1, 0)
    out[...] = err[...] + total * scale


def place_kernel(at, own, near, far, diag, out, sems):
    zl, core = at[0], at[1]
    where = (block(zl, core), block(zl, 1 - core), block(1 - zl, core), block(1 - zl, 1 - core))
    for copy in fetch((own, near, far.at[0], diag.at[1]), [out.at[:, cols] for cols in where], sems):
        copy.wait()


def columns_of(inverse, half):
    return inverse[:, pl.ds(pl.multiple_of(half * HALF, HALF), HALF)]


def begin_kernel(at, chunks, inverse, c2, c3, out, t2, t3, half):
    t2[...] = c2[0].T
    t3[...] = c3[1].T
    unchunk(chunks, half)
    first, second = two(columns_of(inverse, at[1]))
    out[...] = mm(first, half[...], 1, 0) + mm(second, half[...], 1, 0)


def last_kernel(
    share, scale, at, other, inverse, basis, begun, t2, t3, merged, g2, g3,
    new_error, factor_q, half,
):
    step = pl.program_id(0)
    zl, core = at[0], at[1]

    @pl.when(step == 0)
    def _():
        unchunk(other, half)

    cols = pl.ds(pl.multiple_of(step * ROWS, ROWS), ROWS)
    first, second = two(columns_of(inverse, 1 - core))
    q = mm(first, half[:, cols], 1, 0) + mm(second, half[:, cols], 1, 0)
    q = (begun[:, cols] + q) * share
    total = mm(t2[...], g2[...], 1, 0) + mm(t3[...], g3[...], 1, 0)
    new_error[...] = merged[...] + total * scale - mm(basis[...], q.astype(BF16), 1, 0)

    @pl.when(step == zl * 2 + core)
    def _():
        factor_q[...] = q.T


def size(shape, dtype):
    return math.prod(shape) * jnp.dtype(dtype).itemsize


def in_hbm(x):
    return pltpu.with_memory_space_constraint(x, pltpu.HBM)


def call(
    kernel, outs, args, flops, name, scratch=(), alias=None, limit=12, loose=(), held=(), free=False, sems=0
):
    args = [in_hbm(a) if n in held else a for n, a in enumerate(args)]
    moved = sum(size(a.shape, a.dtype) for a in args) + sum(size(s, d) for s, d in outs)
    scratch = [pltpu.VMEM(s, d) for s, d in scratch]
    if sems:
        scratch.append(pltpu.SemaphoreType.DMA((sems,)))
    return pl.pallas_call(
        kernel,
        out_shape=[(pltpu.HBM if free else jax.ShapeDtypeStruct)(s, d) for s, d in outs],
        in_specs=[
            SMEM if a.dtype == jnp.int32 else ANY if n in loose or n in held else VMEM
            for n, a in enumerate(args)
        ],
        out_specs=[pl.BlockSpec(s, lambda s=s: (0,) * len(s)) if free else VMEM for s, _ in outs],
        scratch_shapes=scratch,
        input_output_aliases=alias or {},
        compiler_params=pltpu.CompilerParams(vmem_limit_bytes=limit * 2**20),
        cost_estimate=pl.CostEstimate(flops=flops, bytes_accessed=moved, transcendentals=0),
        name=name,
    )(*args)


def call_grid(kernel, steps, outs, ins, args, flops, name, scratch=(), sems=0, limit=14, loose=(), alias=None):
    args = [
        a if spec in (SMEM, ANY, VMEM) or n in loose else in_hbm(a)
        for n, (a, spec) in enumerate(zip(args, ins))
    ]
    moved = sum(size(a.shape, a.dtype) for a in args) + sum(size(s, d) for s, d, _ in outs)
    scratch = [pltpu.VMEM(s, d) for s, d in scratch]
    if sems:
        scratch.append(pltpu.SemaphoreType.DMA((sems,)))
    return pl.pallas_call(
        kernel,
        grid=(steps,),
        out_shape=[
            (jax.ShapeDtypeStruct if spec is VMEM else pltpu.HBM)(s, d) for s, d, spec in outs
        ],
        in_specs=ins,
        out_specs=[spec for _, _, spec in outs],
        scratch_shapes=scratch,
        input_output_aliases=alias or {},
        compiler_params=pltpu.CompilerParams(vmem_limit_bytes=limit * 2**20),
        cost_estimate=pl.CostEstimate(flops=flops, bytes_accessed=moved, transcendentals=0),
        name=name,
    )(*args)


def whole(*shape):
    return pl.BlockSpec(shape, lambda j: (0,) * len(shape))


def column(rows):
    return pl.BlockSpec((rows, ROWS), lambda j: (0, j))


def rows_of(rows, cols):
    return pl.BlockSpec((rows, cols), lambda j: (j, 0))


CHUNKED = (CHUNKS, CHUNK_ROWS, CHUNK_COLS)
CHUNK = (CHUNK_ROWS, CHUNK_COLS)


def tied(x, *others):
    return lax.optimization_barrier((x,) + others)[0]


def across_plane(keep, send, beside=()):
    got = swap(send, "core")
    (half,) = call(add_kernel, [(CHUNKED, BF16)], (keep, got), 1_000_000, "add")
    parts = tied(lax.all_to_all(half, ("y", "x"), 0, 0), *beside)
    (part,) = call(sum_kernel, [(CHUNK, F32)], (parts,), 1_000_000, "sum")
    return part


def across_z(part, beside=()):
    far = tied(swap(part, "zl"), *beside)
    part = (part + far).astype(BF16)
    return (part,) + tuple(
        lax.ppermute(part, "zh", [(i, (i + step) % 4) for i in range(4)]) for step in (1, 2, 3)
    )


def back_over_plane(part, one, opposite, three, beside=()):
    (whole,) = call(
        spread_kernel,
        [(CHUNKED, BF16)],
        (tied(part, *beside), one, opposite, three),
        1_000_000,
        "spread",
    )
    return lax.all_to_all(whole, ("y", "x"), 0, 0)


def on_device(context, out_grad, weight, error, warm):
    scale = 1.0 / math.sqrt(TOK * 4)
    core = lax.axis_index("core")
    zl = lax.axis_index("zl")
    at = jnp.stack([zl, core]).astype(jnp.int32)
    error = error[0]
    tokens = ((TOK, ROWS), BF16)
    pair = ((2, TOK, ROWS), BF16)

    warm_far = swap(warm, "zl")
    warm_near = swap(warm, "core")
    quarter = rows_of(TOK // 4, ROWS)
    strip = rows_of(ROWS // 4, FEAT)
    c_own, c_near, c_far, low, kept = call_grid(
        prepare_kernel,
        4,
        [tokens + (quarter,)] * 2
        + [pair + (pl.BlockSpec((2, TOK // 4, ROWS), lambda j: (0, j, 0)),)]
        + [((ROWS, FEAT), BF16, VMEM), ((ROWS, FEAT), BF16, strip)],
        [SMEM, rows_of(TOK // 4, FEAT), strip],
        (tied(at, warm_near), context, error),
        4_000_000,
        "prepare",
    )
    warm_diag = swap(tied(warm_far, low), "core")
    c_near = swap(c_near, "core")

    big = ((ROWS, FEAT), BF16)
    keep, send = call(
        functools.partial(left_kernel, scale),
        [(CHUNKED, F32), (CHUNKED, BF16)],
        (at, out_grad, context, tied(low, c_near), warm, warm_near, warm_far, warm_diag),
        2_000_000_000,
        "left",
        [((RANK, FEAT), F32)],
    )
    g_far = swap(tied(out_grad, warm_near), "zl")
    g_near = swap(tied(out_grad, warm_far, low), "core")
    turned = [((ROWS, TOK), BF16)] * 2
    (merged,) = call_grid(
        functools.partial(merge_kernel, scale),
        4,
        [((ROWS, FEAT), F32, column(ROWS))],
        [column(ROWS), VMEM, VMEM, column(TOK), column(TOK)],
        (error, c_own, c_near, out_grad, g_near),
        1_100_000_000,
        "merge",
        turned,
        loose=(3, 4),
    )
    part = across_plane(keep, send, (merged,))
    g_diag = swap(tied(g_far, part), "core")
    zs = across_z(tied(part, g_far))
    c_far = swap(tied(c_far, *zs[1:]), "zl")
    mine = back_over_plane(*zs)

    i_own, i_near, i_far = call(
        grad_kernel,
        [tokens] * 2 + [pair],
        (out_grad, g_near, g_far, g_diag, weight),
        2_200_000_000,
        "grad",
        [big] + [((TOK, FEAT), BF16)] * 4,
        held=range(5),
        free=True,
        sems=5,
    )
    other = swap(tied(mine, i_own, c_far), "core")
    i_far = swap(i_far, "zl")
    i_near = swap(i_near, "core")

    mine_half, proj = call(
        early_kernel,
        [((HALF, FEAT), BF16), ((HALF, TOK), F32)],
        (context, mine),
        150_000_000,
        "early",
    )
    other = tied(other, proj)
    keep, send, left = call(
        functools.partial(right_kernel, scale),
        [(CHUNKED, F32), (CHUNKED, BF16), ((RANK, FEAT), BF16)],
        (at, context, out_grad, kept, mine_half, proj, other),
        2_000_000_000,
        "right",
        [((RANK, FEAT), F32), big, ((RANK, TOK), F32)],
        held=(3,),
        sems=1,
    )

    table = ((RANK, 2 * RANK), F32)
    (a,) = call(gram_kernel, [table], (left,), 300_000_000, "gram")
    (a,) = call(
        functools.partial(step_kernel, PART), [table], (a,), 300_000_000, "step", alias={0: 0}
    )
    part = across_plane(keep, send, (a,))
    part = tied(part, i_far, i_near)
    c_diag = swap(c_far, "core")
    zs = across_z(part)
    i_diag = swap(tied(i_far, zs[0]), "core")
    (a,) = call(
        functools.partial(step_kernel, 2 * PART), [table], (a,), 300_000_000, "step", alias={0: 0}
    )
    mine = back_over_plane(*zs, beside=(a, c_diag, i_diag))
    in_grad = pl.pallas_call(
        place_kernel,
        out_shape=pltpu.HBM((TOK, FEAT), BF16),
        in_specs=[SMEM] + [ANY] * 4,
        out_specs=ANY,
        scratch_shapes=[pltpu.SemaphoreType.DMA((4,))],
        cost_estimate=pl.CostEstimate(flops=0, bytes_accessed=2**21, transcendentals=0),
        name="place",
    )(at, *(in_hbm(x) for x in (i_own, i_near, i_far, i_diag)))
    inverse, basis = call(
        basis_kernel,
        [((RANK, RANK), F32), ((ROWS, RANK), BF16)],
        (at, a, left),
        300_000_000,
        "basis",
        [table],
    )
    other = swap(tied(mine, basis, in_grad), "core")
    begun, t2, t3 = call(
        begin_kernel,
        [((RANK, FEAT), F32)] + turned,
        (at, mine, inverse, c_far, c_diag),
        300_000_000,
        "begin",
        [((HALF, FEAT), BF16)],
    )
    other = tied(other, begun)

    new_error, factor_q = call_grid(
        functools.partial(last_kernel, 1.0 / (SIZES[0] * SIZES[1] * SIZES[2]), scale),
        4,
        [
            ((ROWS, FEAT), F32, column(ROWS)),
            ((ROWS, RANK), F32, whole(ROWS, RANK)),
        ],
        [SMEM, VMEM, VMEM, whole(ROWS, RANK), VMEM, VMEM, VMEM]
        + [column(ROWS), column(TOK), column(TOK)],
        (at, other, inverse, basis, begun, t2, t3, merged, g_far, g_diag),
        2_000_000_000,
        "last",
        [((HALF, FEAT), BF16)],
    )
    return in_grad, new_error[None], factor_q


def solution(mesh):
    split = Mesh(np.asarray(mesh.devices).reshape(SIZES), AXES)
    every = ("zh", "y", "x", "zl", "core")
    shard = ("zl", "core")
    return jax.shard_map(
        on_device,
        mesh=split,
        in_specs=(
            P(every, None),
            P(every, None),
            P(shard, None),
            P(("zh", "y", "x"), shard, None),
            P(shard, None),
        ),
        out_specs=(P(every, None), P(("zh", "y", "x"), shard, None), P(shard, None)),
        check_vma=False,
    )
```

```python
import functools
import math

import jax
import jax.numpy as jnp
import numpy as np
from jax import lax
from jax.experimental import pallas as pl
from jax.experimental.pallas import tpu as pltpu
from jax.sharding import Mesh, PartitionSpec as P

BF16 = jnp.bfloat16
F32 = jnp.float32
HI = lax.Precision.HIGHEST
PART = 64
SUB = 8
AXES = ("zh", "y", "x", "zl", "core")
SIZES = (4, 4, 4, 2, 2)
ROWS = 512
RANK = 256
FEAT = 2048
TOK = 256
HALF = RANK // 2
CHUNKS, CHUNK_ROWS, CHUNK_COLS = 16, 16, 1024
VMEM = pl.BlockSpec(memory_space=pltpu.VMEM)
SMEM = pl.BlockSpec(memory_space=pltpu.SMEM)
ANY = pl.BlockSpec(memory_space=pl.ANY)


def swap(x, axis):
    return lax.ppermute(x, axis, [(0, 1), (1, 0)])


def mm(a, b, ca, cb):
    return lax.dot_general(a, b, (((ca,), (cb,)), ((), ())), preferred_element_type=F32)


def two(x):
    high = x.astype(BF16)
    return high, (x - high.astype(F32)).astype(BF16)


def chunk_at(n):
    return n // 2 * CHUNK_ROWS, n % 2 * CHUNK_COLS


def fetch(sources, targets, sems):
    copies = [
        pltpu.make_async_copy(src, dst, sems.at[n]) for n, (src, dst) in enumerate(zip(sources, targets))
    ]
    for copy in copies:
        copy.start()
    return copies


def split_halves(core, total, keep, send):
    for n in range(CHUNKS):
        row, col = chunk_at(n)
        cols = pl.ds(col, CHUNK_COLS)
        keep[n] = total[pl.ds(pl.multiple_of(core * HALF + row, CHUNK_ROWS), CHUNK_ROWS), cols]
        send[n] = total[
            pl.ds(pl.multiple_of((1 - core) * HALF + row, CHUNK_ROWS), CHUNK_ROWS), cols
        ].astype(send.dtype)


def block(zl, core):
    return pl.ds(pl.multiple_of((zl * 2 + core) * ROWS, ROWS), ROWS)


def prepare_kernel(at, ctx, err, own, near, far, low, kept):
    zl, core = at[0], at[1]
    own[...] = ctx[:, block(zl, core)]
    near[...] = ctx[:, block(zl, 1 - core)]
    far[0] = ctx[:, block(1 - zl, core)]
    far[1] = ctx[:, block(1 - zl, 1 - core)]
    rows = err.shape[0]
    kept[...] = err[...].astype(BF16)
    low[pl.ds(pl.multiple_of(pl.program_id(0) * rows, rows), rows), :] = kept[...]


def left_kernel(scale, at, og, ctx, low, w0, w1, w2, w3, keep, send, total):
    zl, core = at[0], at[1]
    where = ((zl, core), (zl, 1 - core), (1 - zl, core), (1 - zl, 1 - core))
    proj = jnp.zeros((TOK, RANK), F32)
    own = jnp.zeros((ROWS, RANK), F32)
    for (a, b), w in zip(where, (w0, w1, w2, w3)):
        cols = block(a, b)
        proj += mm(og[:, cols], w[...], 1, 0)
        own += mm(low[:, cols], w[...], 1, 0)
    first, second = two(proj * scale)
    total[...] = mm(first, ctx[...], 0, 0) + mm(second, ctx[...], 0, 0)
    total[:, block(zl, core)] += own.T
    split_halves(core, total, keep, send)


def unchunk(chunks, half):
    for n in range(CHUNKS):
        row, col = chunk_at(n)
        half[row : row + CHUNK_ROWS, col : col + CHUNK_COLS] = chunks[n]


def early_kernel(ctx, mine, half, proj):
    unchunk(mine, half)
    proj[...] = mm(half[...], ctx[...], 1, 1)


def right_kernel(
    scale, at, ctx, og, low_hbm, mine, proj_mine, other, keep, send, left, total, low, proj, sems
):
    zl, core = at[0], at[1]
    copy = pltpu.make_async_copy(low_hbm, low, sems.at[0])
    copy.start()
    here = pl.ds(pl.multiple_of(core * HALF, HALF), HALF)
    there = pl.ds(pl.multiple_of((1 - core) * HALF, HALF), HALF)
    unchunk(other, left.at[there, :])
    left[here, :] = mine[...]
    proj[here, :] = proj_mine[...]
    proj[there, :] = mm(left[there, :], ctx[...], 1, 1)
    first, second = two(proj[...] * scale)
    total[...] = mm(first, og[...], 1, 0) + mm(second, og[...], 1, 0)
    own = left[:, block(zl, core)]
    copy.wait()
    total[...] += mm(own, low[...], 1, 0)
    split_halves(core, total, keep, send)


def add_kernel(keep, got, out):
    out[...] = (keep[...] + got[...].astype(F32)).astype(BF16)


def sum_kernel(parts, out):
    out[...] = parts[...].astype(F32).sum(0)


def spread_kernel(part, one, opposite, three, out):
    part, one, opposite, three = (x[...].astype(F32) for x in (part, one, opposite, three))
    whole = ((part + opposite) + (one + three)).astype(BF16)
    for n in range(CHUNKS):
        out[n] = whole


def row_of(x, k):
    return jnp.broadcast_to(x[k : k + 1, :], x.shape)


def factor_block(rows):
    shape = rows[0].shape
    sub = lax.broadcasted_iota(jnp.int32, shape, 0)
    for p in range(len(rows)):
        cols = [
            [jnp.broadcast_to(r[:, SUB * p + k : SUB * p + k + 1], shape) for k in range(SUB)]
            for r in rows[p:]
        ]
        for k in range(SUB):
            diagonal = row_of(cols[0][k], k)
            inv = lax.rsqrt(diagonal)
            inv = inv * (1.5 - 0.5 * diagonal * inv * inv)
            pivot = row_of(rows[p], k) * inv
            later = [row_of(cols[0][j], k) * inv for j in range(k + 1, SUB)]
            for g, col in enumerate(cols, p):
                times = col[k] * inv
                if g == p:
                    times = jnp.where(sub > k, times, 0.0)
                rows[g] = rows[g] - times * pivot
                if g == p:
                    rows[g] = jnp.where(sub == k, pivot, rows[g])
                for j, entry in zip(range(k + 1, SUB), later):
                    col[j] = col[j] - times * entry
    return rows


def dot_hi(a, b, ca, cb):
    return lax.dot_general(
        a, b, (((ca,), (cb,)), ((), ())), precision=HI, preferred_element_type=F32
    )


def eye(n):
    shape = (n, n)
    same = lax.broadcasted_iota(jnp.int32, shape, 0) == lax.broadcasted_iota(jnp.int32, shape, 1)
    return same.astype(F32)


def eliminate(start, a):
    stop = start + PART
    rows = jnp.concatenate([a[start:stop, start:stop], eye(PART)], 1)
    rows = factor_block([rows[n : n + SUB] for n in range(0, PART, SUB)])
    inverse = jnp.concatenate(rows, 0)[:, PART:]
    panel = dot_hi(inverse, a[start:stop, :], 1, 0)
    a[start:stop, :] = panel
    if stop < RANK:
        a[stop:, :] = a[stop:, :] - dot_hi(panel[:, stop:RANK], panel, 0, 0)


def gram_kernel(left, a):
    a[:, :RANK] = mm(left[...], left[...], 1, 1)
    a[:, RANK:] = eye(RANK)
    eliminate(0, a)


def step_kernel(start, a_in, a):
    eliminate(start, a)


def basis_kernel(at, a_in, left, inverse, basis, a):
    a[...] = a_in[...]
    eliminate(RANK - PART, a)
    inverse[...] = a[:, RANK:]
    first, second = two(a[:, RANK:])
    own = left[:, block(at[0], at[1])]
    basis[...] = (mm(first, own, 1, 0) + mm(second, own, 1, 0)).astype(BF16).T


def grad_kernel(h0, h1, h2, h3, weight_hbm, o0, o1, far, weight, g0, g1, g2, g3, sems):
    copies = fetch((weight_hbm, h0, h1, h2, h3), (weight, g0, g1, g2, g3), sems)
    copies[0].wait()
    for g, o, copy in zip((g0, g1, g2, g3), (o0, o1, far.at[0], far.at[1]), copies[1:]):
        copy.wait()
        o[...] = mm(g[...], weight[...], 1, 1).astype(BF16)


def merge_kernel(scale, err, c0, c1, g0, g1, out, t0, t1):
    step = pl.program_id(0)

    @pl.when(step == 0)
    def _():
        t0[...] = c0[...].T
        t1[...] = c1[...].T

    total = mm(t0[...], g0[...], 1, 0) + mm(t1[...], g1[...], 1, 0)
    out[...] = err[...] + total * scale


def place_kernel(at, own, near, far, diag, out):
    step = pl.program_id(0)
    same_zl, same_core = step // 2 == at[0], step % 2 == at[1]
    for piece, here in (
        (own, same_zl & same_core),
        (near, same_zl & jnp.logical_not(same_core)),
        (far, jnp.logical_not(same_zl) & same_core),
        (diag, jnp.logical_not(same_zl) & jnp.logical_not(same_core)),
    ):

        @pl.when(here)
        def _(piece=piece):
            out[...] = piece[...]


def columns_of(inverse, half):
    return inverse[:, pl.ds(pl.multiple_of(half * HALF, HALF), HALF)]


def begin_kernel(at, chunks, inverse, c2, c3, out, t2, t3, half):
    t2[...] = c2[0].T
    t3[...] = c3[1].T
    unchunk(chunks, half)
    first, second = two(columns_of(inverse, at[1]))
    out[...] = mm(first, half[...], 1, 0) + mm(second, half[...], 1, 0)


def last_kernel(
    share, scale, at, other, inverse, basis, begun, t2, t3, merged, g2, g3,
    new_error, factor_q, half,
):
    step = pl.program_id(0)
    zl, core = at[0], at[1]

    @pl.when(step == 0)
    def _():
        unchunk(other, half)

    cols = pl.ds(pl.multiple_of(step * ROWS, ROWS), ROWS)
    first, second = two(columns_of(inverse, 1 - core))
    q = mm(first, half[:, cols], 1, 0) + mm(second, half[:, cols], 1, 0)
    q = (begun[:, cols] + q) * share
    total = mm(t2[...], g2[...], 1, 0) + mm(t3[...], g3[...], 1, 0)
    new_error[...] = merged[...] + total * scale - mm(basis[...], q.astype(BF16), 1, 0)

    @pl.when(step == zl * 2 + core)
    def _():
        factor_q[...] = q.T


def size(shape, dtype):
    return math.prod(shape) * jnp.dtype(dtype).itemsize


def in_hbm(x):
    return pltpu.with_memory_space_constraint(x, pltpu.HBM)


def call(
    kernel, outs, args, flops, name, scratch=(), alias=None, limit=12, loose=(), held=(), free=False, sems=0
):
    args = [in_hbm(a) if n in held else a for n, a in enumerate(args)]
    moved = sum(size(a.shape, a.dtype) for a in args) + sum(size(s, d) for s, d in outs)
    scratch = [pltpu.VMEM(s, d) for s, d in scratch]
    if sems:
        scratch.append(pltpu.SemaphoreType.DMA((sems,)))
    return pl.pallas_call(
        kernel,
        out_shape=[(pltpu.HBM if free else jax.ShapeDtypeStruct)(s, d) for s, d in outs],
        in_specs=[
            SMEM if a.dtype == jnp.int32 else ANY if n in loose or n in held else VMEM
            for n, a in enumerate(args)
        ],
        out_specs=[pl.BlockSpec(s, lambda s=s: (0,) * len(s)) if free else VMEM for s, _ in outs],
        scratch_shapes=scratch,
        input_output_aliases=alias or {},
        compiler_params=pltpu.CompilerParams(vmem_limit_bytes=limit * 2**20),
        cost_estimate=pl.CostEstimate(flops=flops, bytes_accessed=moved, transcendentals=0),
        name=name,
    )(*args)


def call_grid(kernel, steps, outs, ins, args, flops, name, scratch=(), sems=0, limit=14, loose=(), alias=None):
    args = [
        a if spec in (SMEM, ANY, VMEM) or n in loose else in_hbm(a)
        for n, (a, spec) in enumerate(zip(args, ins))
    ]
    moved = sum(size(a.shape, a.dtype) for a in args) + sum(size(s, d) for s, d, _ in outs)
    scratch = [pltpu.VMEM(s, d) for s, d in scratch]
    if sems:
        scratch.append(pltpu.SemaphoreType.DMA((sems,)))
    return pl.pallas_call(
        kernel,
        grid=(steps,),
        out_shape=[
            (jax.ShapeDtypeStruct if spec is VMEM else pltpu.HBM)(s, d) for s, d, spec in outs
        ],
        in_specs=ins,
        out_specs=[spec for _, _, spec in outs],
        scratch_shapes=scratch,
        input_output_aliases=alias or {},
        compiler_params=pltpu.CompilerParams(vmem_limit_bytes=limit * 2**20),
        cost_estimate=pl.CostEstimate(flops=flops, bytes_accessed=moved, transcendentals=0),
        name=name,
    )(*args)


def whole(*shape):
    return pl.BlockSpec(shape, lambda j: (0,) * len(shape))


def column(rows):
    return pl.BlockSpec((rows, ROWS), lambda j: (0, j))


def rows_of(rows, cols):
    return pl.BlockSpec((rows, cols), lambda j: (j, 0))


CHUNKED = (CHUNKS, CHUNK_ROWS, CHUNK_COLS)
CHUNK = (CHUNK_ROWS, CHUNK_COLS)


def tied(x, *others):
    return lax.optimization_barrier((x,) + others)[0]


def across_plane(keep, send, beside=()):
    got = swap(send, "core")
    (half,) = call(add_kernel, [(CHUNKED, BF16)], (keep, got), 1_000_000, "add")
    parts = tied(lax.all_to_all(half, ("y", "x"), 0, 0), *beside)
    (part,) = call(sum_kernel, [(CHUNK, F32)], (parts,), 1_000_000, "sum")
    return part


def across_z(part, beside=()):
    far = tied(swap(part, "zl"), *beside)
    part = (part + far).astype(BF16)
    return (part,) + tuple(
        lax.ppermute(part, "zh", [(i, (i + step) % 4) for i in range(4)]) for step in (1, 2, 3)
    )


def back_over_plane(part, one, opposite, three, beside=()):
    (whole,) = call(
        spread_kernel,
        [(CHUNKED, BF16)],
        (tied(part, *beside), one, opposite, three),
        1_000_000,
        "spread",
    )
    return lax.all_to_all(whole, ("y", "x"), 0, 0)


def on_device(context, out_grad, weight, error, warm):
    scale = 1.0 / math.sqrt(TOK * 4)
    core = lax.axis_index("core")
    zl = lax.axis_index("zl")
    at = jnp.stack([zl, core]).astype(jnp.int32)
    error = error[0]
    tokens = ((TOK, ROWS), BF16)
    pair = ((2, TOK, ROWS), BF16)

    warm_far = swap(warm, "zl")
    warm_near = swap(warm, "core")
    quarter = rows_of(TOK // 4, ROWS)
    strip = rows_of(ROWS // 4, FEAT)
    c_own, c_near, c_far, low, kept = call_grid(
        prepare_kernel,
        4,
        [tokens + (quarter,)] * 2
        + [pair + (pl.BlockSpec((2, TOK // 4, ROWS), lambda j: (0, j, 0)),)]
        + [((ROWS, FEAT), BF16, VMEM), ((ROWS, FEAT), BF16, strip)],
        [SMEM, rows_of(TOK // 4, FEAT), strip],
        (tied(at, warm_near), context, error),
        4_000_000,
        "prepare",
    )
    warm_diag = swap(tied(warm_far, low), "core")
    c_near = swap(c_near, "core")

    big = ((ROWS, FEAT), BF16)
    keep, send = call(
        functools.partial(left_kernel, scale),
        [(CHUNKED, F32), (CHUNKED, BF16)],
        (at, out_grad, context, tied(low, c_near), warm, warm_near, warm_far, warm_diag),
        2_000_000_000,
        "left",
        [((RANK, FEAT), F32)],
    )
    g_far = swap(tied(out_grad, warm_near), "zl")
    g_near = swap(tied(out_grad, warm_far, low), "core")
    turned = [((ROWS, TOK), BF16)] * 2
    (merged,) = call_grid(
        functools.partial(merge_kernel, scale),
        4,
        [((ROWS, FEAT), F32, column(ROWS))],
        [column(ROWS), VMEM, VMEM, column(TOK), column(TOK)],
        (error, c_own, c_near, out_grad, g_near),
        1_100_000_000,
        "merge",
        turned,
        loose=(3, 4),
    )
    part = across_plane(keep, send, (merged,))
    g_diag = swap(tied(g_far, part), "core")
    zs = across_z(tied(part, g_far))
    c_far = swap(tied(c_far, *zs[1:]), "zl")
    mine = back_over_plane(*zs)

    i_own, i_near, i_far = call(
        grad_kernel,
        [tokens] * 2 + [pair],
        (out_grad, g_near, g_far, g_diag, weight),
        2_200_000_000,
        "grad",
        [big] + [((TOK, FEAT), BF16)] * 4,
        held=range(5),
        free=True,
        sems=5,
    )
    other = swap(tied(mine, i_own), "core")
    i_far = swap(i_far, "zl")
    i_near = swap(i_near, "core")

    mine_half, proj = call(
        early_kernel,
        [((HALF, FEAT), BF16), ((HALF, TOK), F32)],
        (context, mine),
        150_000_000,
        "early",
    )
    other = tied(other, proj, c_far)
    keep, send, left = call(
        functools.partial(right_kernel, scale),
        [(CHUNKED, F32), (CHUNKED, BF16), ((RANK, FEAT), BF16)],
        (at, context, out_grad, kept, mine_half, proj, other),
        2_000_000_000,
        "right",
        [((RANK, FEAT), F32), big, ((RANK, TOK), F32)],
        held=(3,),
        sems=1,
    )

    table = ((RANK, 2 * RANK), F32)
    (a,) = call(gram_kernel, [table], (left,), 300_000_000, "gram")
    (a,) = call(
        functools.partial(step_kernel, PART), [table], (a,), 300_000_000, "step", alias={0: 0}
    )
    part = across_plane(keep, send, (a,))
    part = tied(part, i_far, i_near)
    c_diag = swap(c_far, "core")
    zs = across_z(part)
    i_diag = swap(i_far, "core")
    (a,) = call(
        functools.partial(step_kernel, 2 * PART), [table], (a,), 300_000_000, "step", alias={0: 0}
    )
    mine = back_over_plane(*zs, beside=(a, c_diag, i_diag))
    block_in = whole(TOK, ROWS)
    first = pl.BlockSpec((None, TOK, ROWS), lambda j: (0, 0, 0))
    second = pl.BlockSpec((None, TOK, ROWS), lambda j: (1, 0, 0))
    (in_grad,) = call_grid(
        place_kernel,
        4,
        [((TOK, FEAT), BF16, column(TOK))],
        [SMEM, block_in, block_in, first, second],
        (at, i_own, i_near, i_far, i_diag),
        1_000_000,
        "place",
    )
    inverse, basis = call(
        basis_kernel,
        [((RANK, RANK), F32), ((ROWS, RANK), BF16)],
        (at, a, left),
        300_000_000,
        "basis",
        [table],
    )
    other = swap(tied(mine, basis, in_grad), "core")
    begun, t2, t3 = call(
        begin_kernel,
        [((RANK, FEAT), F32)] + turned,
        (at, mine, inverse, c_far, c_diag),
        300_000_000,
        "begin",
        [((HALF, FEAT), BF16)],
    )
    other = tied(other, begun)

    new_error, factor_q = call_grid(
        functools.partial(last_kernel, 1.0 / (SIZES[0] * SIZES[1] * SIZES[2]), scale),
        4,
        [
            ((ROWS, FEAT), F32, column(ROWS)),
            ((ROWS, RANK), F32, whole(ROWS, RANK)),
        ],
        [SMEM, VMEM, VMEM, whole(ROWS, RANK), VMEM, VMEM, VMEM]
        + [column(ROWS), column(TOK), column(TOK)],
        (at, other, inverse, basis, begun, t2, t3, merged, g_far, g_diag),
        2_000_000_000,
        "last",
        [((HALF, FEAT), BF16)],
    )
    return in_grad, new_error[None], factor_q


def solution(mesh):
    split = Mesh(np.asarray(mesh.devices).reshape(SIZES), AXES)
    every = ("zh", "y", "x", "zl", "core")
    shard = ("zl", "core")
    return jax.shard_map(
        on_device,
        mesh=split,
        in_specs=(
            P(every, None),
            P(every, None),
            P(shard, None),
            P(("zh", "y", "x"), shard, None),
            P(shard, None),
        ),
        out_specs=(P(every, None), P(("zh", "y", "x"), shard, None), P(shard, None)),
        check_vma=False,
    )
```

```python
import functools
import math

import jax
import jax.numpy as jnp
import numpy as np
from jax import lax
from jax.experimental import pallas as pl
from jax.experimental.pallas import tpu as pltpu
from jax.sharding import Mesh, PartitionSpec as P

BF16 = jnp.bfloat16
F32 = jnp.float32
HI = lax.Precision.HIGHEST
PART = 64
SUB = 8
AXES = ("zh", "y", "x", "zl", "core")
SIZES = (4, 4, 4, 2, 2)
ROWS = 512
RANK = 256
FEAT = 2048
TOK = 256
HALF = RANK // 2
CHUNKS, CHUNK_ROWS, CHUNK_COLS = 16, 16, 1024
VMEM = pl.BlockSpec(memory_space=pltpu.VMEM)
SMEM = pl.BlockSpec(memory_space=pltpu.SMEM)
ANY = pl.BlockSpec(memory_space=pl.ANY)


def swap(x, axis):
    return lax.ppermute(x, axis, [(0, 1), (1, 0)])


def mm(a, b, ca, cb):
    return lax.dot_general(a, b, (((ca,), (cb,)), ((), ())), preferred_element_type=F32)


def two(x):
    high = x.astype(BF16)
    return high, (x - high.astype(F32)).astype(BF16)


def chunk_at(n):
    return n // 2 * CHUNK_ROWS, n % 2 * CHUNK_COLS


def fetch(sources, targets, sems):
    copies = [
        pltpu.make_async_copy(src, dst, sems.at[n]) for n, (src, dst) in enumerate(zip(sources, targets))
    ]
    for copy in copies:
        copy.start()
    return copies


def split_halves(core, total, keep, send):
    for n in range(CHUNKS):
        row, col = chunk_at(n)
        cols = pl.ds(col, CHUNK_COLS)
        keep[n] = total[pl.ds(pl.multiple_of(core * HALF + row, CHUNK_ROWS), CHUNK_ROWS), cols]
        send[n] = total[
            pl.ds(pl.multiple_of((1 - core) * HALF + row, CHUNK_ROWS), CHUNK_ROWS), cols
        ].astype(send.dtype)


def block(zl, core):
    return pl.ds(pl.multiple_of((zl * 2 + core) * ROWS, ROWS), ROWS)


def prepare_kernel(at, ctx, err, own, near, far, low, kept):
    zl, core = at[0], at[1]
    own[...] = ctx[:, block(zl, core)]
    near[...] = ctx[:, block(zl, 1 - core)]
    far[0] = ctx[:, block(1 - zl, core)]
    far[1] = ctx[:, block(1 - zl, 1 - core)]
    rows = err.shape[0]
    kept[...] = err[...].astype(BF16)
    low[pl.ds(pl.multiple_of(pl.program_id(0) * rows, rows), rows), :] = kept[...]


def left_kernel(scale, at, og, ctx, low, w0, w1, w2, w3, keep, send, total):
    zl, core = at[0], at[1]
    where = ((zl, core), (zl, 1 - core), (1 - zl, core), (1 - zl, 1 - core))
    proj = jnp.zeros((TOK, RANK), F32)
    own = jnp.zeros((ROWS, RANK), F32)
    for (a, b), w in zip(where, (w0, w1, w2, w3)):
        cols = block(a, b)
        proj += mm(og[:, cols], w[...], 1, 0)
        own += mm(low[:, cols], w[...], 1, 0)
    first, second = two(proj * scale)
    total[...] = mm(first, ctx[...], 0, 0) + mm(second, ctx[...], 0, 0)
    total[:, block(zl, core)] += own.T
    split_halves(core, total, keep, send)


def unchunk(chunks, half):
    for n in range(CHUNKS):
        row, col = chunk_at(n)
        half[row : row + CHUNK_ROWS, col : col + CHUNK_COLS] = chunks[n]


def early_kernel(ctx, mine, half, proj):
    unchunk(mine, half)
    proj[...] = mm(half[...], ctx[...], 1, 1)


def right_kernel(
    scale, at, ctx, og, low_hbm, mine, proj_mine, other, keep, send, left, total, low, proj, sems
):
    zl, core = at[0], at[1]
    copy = pltpu.make_async_copy(low_hbm, low, sems.at[0])
    copy.start()
    here = pl.ds(pl.multiple_of(core * HALF, HALF), HALF)
    there = pl.ds(pl.multiple_of((1 - core) * HALF, HALF), HALF)
    unchunk(other, left.at[there, :])
    left[here, :] = mine[...]
    proj[here, :] = proj_mine[...]
    proj[there, :] = mm(left[there, :], ctx[...], 1, 1)
    first, second = two(proj[...] * scale)
    total[...] = mm(first, og[...], 1, 0) + mm(second, og[...], 1, 0)
    own = left[:, block(zl, core)]
    copy.wait()
    total[...] += mm(own, low[...], 1, 0)
    split_halves(core, total, keep, send)


def add_kernel(keep, got, out):
    out[...] = (keep[...] + got[...].astype(F32)).astype(BF16)


def sum_kernel(parts, out):
    out[...] = parts[...].astype(F32).sum(0)


def spread_kernel(part, one, opposite, three, out):
    part, one, opposite, three = (x[...].astype(F32) for x in (part, one, opposite, three))
    whole = ((part + opposite) + (one + three)).astype(BF16)
    for n in range(CHUNKS):
        out[n] = whole


def row_of(x, k):
    return jnp.broadcast_to(x[k : k + 1, :], x.shape)


def factor_block(rows):
    shape = rows[0].shape
    sub = lax.broadcasted_iota(jnp.int32, shape, 0)
    for p in range(len(rows)):
        cols = [
            [jnp.broadcast_to(r[:, SUB * p + k : SUB * p + k + 1], shape) for k in range(SUB)]
            for r in rows[p:]
        ]
        for k in range(SUB):
            diagonal = row_of(cols[0][k], k)
            inv = lax.rsqrt(diagonal)
            inv = inv * (1.5 - 0.5 * diagonal * inv * inv)
            pivot = row_of(rows[p], k) * inv
            later = [row_of(cols[0][j], k) * inv for j in range(k + 1, SUB)]
            for g, col in enumerate(cols, p):
                times = col[k] * inv
                if g == p:
                    times = jnp.where(sub > k, times, 0.0)
                rows[g] = rows[g] - times * pivot
                if g == p:
                    rows[g] = jnp.where(sub == k, pivot, rows[g])
                for j, entry in zip(range(k + 1, SUB), later):
                    col[j] = col[j] - times * entry
    return rows


def dot_hi(a, b, ca, cb):
    return lax.dot_general(
        a, b, (((ca,), (cb,)), ((), ())), precision=HI, preferred_element_type=F32
    )


def eye(n):
    shape = (n, n)
    same = lax.broadcasted_iota(jnp.int32, shape, 0) == lax.broadcasted_iota(jnp.int32, shape, 1)
    return same.astype(F32)


def eliminate(start, a):
    stop = start + PART
    rows = jnp.concatenate([a[start:stop, start:stop], eye(PART)], 1)
    rows = factor_block([rows[n : n + SUB] for n in range(0, PART, SUB)])
    inverse = jnp.concatenate(rows, 0)[:, PART:]
    panel = dot_hi(inverse, a[start:stop, :], 1, 0)
    a[start:stop, :] = panel
    if stop < RANK:
        a[stop:, :] = a[stop:, :] - dot_hi(panel[:, stop:RANK], panel, 0, 0)


def gram_kernel(left, a):
    a[:, :RANK] = mm(left[...], left[...], 1, 1)
    a[:, RANK:] = eye(RANK)
    eliminate(0, a)


def step_kernel(start, a_in, a):
    eliminate(start, a)


def basis_kernel(at, a_in, left, inverse, basis, a):
    a[...] = a_in[...]
    eliminate(RANK - PART, a)
    inverse[...] = a[:, RANK:]
    first, second = two(a[:, RANK:])
    own = left[:, block(at[0], at[1])]
    basis[...] = (mm(first, own, 1, 0) + mm(second, own, 1, 0)).astype(BF16).T


def grad_kernel(h0, h1, weight_hbm, out, weight, g0, g1, sems):
    copies = fetch((weight_hbm, h0, h1), (weight, g0, g1), sems)
    copies[0].wait()
    for n, g in enumerate((g0, g1)):
        copies[n + 1].wait()
        out[n] = mm(g[...], weight[...], 1, 1).astype(BF16)


def merge_kernel(scale, err, c0, c1, g0, g1, out, t0, t1):
    step = pl.program_id(0)

    @pl.when(step == 0)
    def _():
        t0[...] = c0[...].T
        t1[...] = c1[...].T

    total = mm(t0[...], g0[...], 1, 0) + mm(t1[...], g1[...], 1, 0)
    out[...] = err[...] + total * scale


def place_kernel(at, own, near, far, diag, out):
    zl, core = at[0], at[1]
    out[:, block(zl, core)] = own[...]
    out[:, block(zl, 1 - core)] = near[...]
    out[:, block(1 - zl, core)] = far[...]
    out[:, block(1 - zl, 1 - core)] = diag[...]


def columns_of(inverse, half):
    return inverse[:, pl.ds(pl.multiple_of(half * HALF, HALF), HALF)]


def begin_kernel(at, chunks, inverse, c2, c3, out, t2, t3, half):
    t2[...] = c2[0].T
    t3[...] = c3[1].T
    unchunk(chunks, half)
    first, second = two(columns_of(inverse, at[1]))
    out[...] = mm(first, half[...], 1, 0) + mm(second, half[...], 1, 0)


def last_kernel(
    share, scale, at, other, inverse, basis, begun, t2, t3, merged, g2, g3,
    new_error, factor_q, half,
):
    step = pl.program_id(0)
    zl, core = at[0], at[1]

    @pl.when(step == 0)
    def _():
        unchunk(other, half)

    cols = pl.ds(pl.multiple_of(step * ROWS, ROWS), ROWS)
    first, second = two(columns_of(inverse, 1 - core))
    q = mm(first, half[:, cols], 1, 0) + mm(second, half[:, cols], 1, 0)
    q = (begun[:, cols] + q) * share
    total = mm(t2[...], g2[...], 1, 0) + mm(t3[...], g3[...], 1, 0)
    new_error[...] = merged[...] + total * scale - mm(basis[...], q.astype(BF16), 1, 0)

    @pl.when(step == zl * 2 + core)
    def _():
        factor_q[...] = q.T


def size(shape, dtype):
    return math.prod(shape) * jnp.dtype(dtype).itemsize


def in_hbm(x):
    return pltpu.with_memory_space_constraint(x, pltpu.HBM)


def call(
    kernel, outs, args, flops, name, scratch=(), alias=None, limit=12, loose=(), held=(), free=False, sems=0
):
    args = [in_hbm(a) if n in held else a for n, a in enumerate(args)]
    moved = sum(size(a.shape, a.dtype) for a in args) + sum(size(s, d) for s, d in outs)
    scratch = [pltpu.VMEM(s, d) for s, d in scratch]
    if sems:
        scratch.append(pltpu.SemaphoreType.DMA((sems,)))
    return pl.pallas_call(
        kernel,
        out_shape=[(pltpu.HBM if free else jax.ShapeDtypeStruct)(s, d) for s, d in outs],
        in_specs=[
            SMEM if a.dtype == jnp.int32 else ANY if n in loose or n in held else VMEM
            for n, a in enumerate(args)
        ],
        out_specs=[pl.BlockSpec(s, lambda s=s: (0,) * len(s)) if free else VMEM for s, _ in outs],
        scratch_shapes=scratch,
        input_output_aliases=alias or {},
        compiler_params=pltpu.CompilerParams(vmem_limit_bytes=limit * 2**20),
        cost_estimate=pl.CostEstimate(flops=flops, bytes_accessed=moved, transcendentals=0),
        name=name,
    )(*args)


def call_grid(kernel, steps, outs, ins, args, flops, name, scratch=(), sems=0, limit=14, loose=(), alias=None):
    args = [
        a if spec in (SMEM, ANY, VMEM) or n in loose else in_hbm(a)
        for n, (a, spec) in enumerate(zip(args, ins))
    ]
    moved = sum(size(a.shape, a.dtype) for a in args) + sum(size(s, d) for s, d, _ in outs)
    scratch = [pltpu.VMEM(s, d) for s, d in scratch]
    if sems:
        scratch.append(pltpu.SemaphoreType.DMA((sems,)))
    return pl.pallas_call(
        kernel,
        grid=(steps,),
        out_shape=[
            (jax.ShapeDtypeStruct if spec is VMEM else pltpu.HBM)(s, d) for s, d, spec in outs
        ],
        in_specs=ins,
        out_specs=[spec for _, _, spec in outs],
        scratch_shapes=scratch,
        input_output_aliases=alias or {},
        compiler_params=pltpu.CompilerParams(vmem_limit_bytes=limit * 2**20),
        cost_estimate=pl.CostEstimate(flops=flops, bytes_accessed=moved, transcendentals=0),
        name=name,
    )(*args)


def whole(*shape):
    return pl.BlockSpec(shape, lambda j: (0,) * len(shape))


def column(rows):
    return pl.BlockSpec((rows, ROWS), lambda j: (0, j))


def rows_of(rows, cols):
    return pl.BlockSpec((rows, cols), lambda j: (j, 0))


CHUNKED = (CHUNKS, CHUNK_ROWS, CHUNK_COLS)
CHUNK = (CHUNK_ROWS, CHUNK_COLS)


def tied(x, *others):
    return lax.optimization_barrier((x,) + others)[0]


def across_plane(keep, send, beside=()):
    got = swap(send, "core")
    (half,) = call(add_kernel, [(CHUNKED, BF16)], (keep, got), 1_000_000, "add")
    parts = tied(lax.all_to_all(half, ("y", "x"), 0, 0), *beside)
    (part,) = call(sum_kernel, [(CHUNK, F32)], (parts,), 1_000_000, "sum")
    return part


def across_z(part, beside=()):
    far = tied(swap(part, "zl"), *beside)
    part = (part + far).astype(BF16)
    return (part,) + tuple(
        lax.ppermute(part, "zh", [(i, (i + step) % 4) for i in range(4)]) for step in (1, 2, 3)
    )


def back_over_plane(part, one, opposite, three, beside=()):
    (whole,) = call(
        spread_kernel,
        [(CHUNKED, BF16)],
        (tied(part, *beside), one, opposite, three),
        1_000_000,
        "spread",
    )
    return lax.all_to_all(whole, ("y", "x"), 0, 0)


def on_device(context, out_grad, weight, error, warm):
    scale = 1.0 / math.sqrt(TOK * 4)
    core = lax.axis_index("core")
    zl = lax.axis_index("zl")
    at = jnp.stack([zl, core]).astype(jnp.int32)
    error = error[0]
    tokens = ((TOK, ROWS), BF16)
    pair = ((2, TOK, ROWS), BF16)

    warm_far = swap(warm, "zl")
    warm_near = swap(warm, "core")
    quarter = rows_of(TOK // 4, ROWS)
    strip = rows_of(ROWS // 4, FEAT)
    c_own, c_near, c_far, low, kept = call_grid(
        prepare_kernel,
        4,
        [tokens + (quarter,)] * 2
        + [pair + (pl.BlockSpec((2, TOK // 4, ROWS), lambda j: (0, j, 0)),)]
        + [((ROWS, FEAT), BF16, VMEM), ((ROWS, FEAT), BF16, strip)],
        [SMEM, rows_of(TOK // 4, FEAT), strip],
        (tied(at, warm_near), context, error),
        4_000_000,
        "prepare",
    )
    warm_diag = swap(tied(warm_far, low), "core")
    c_near = swap(c_near, "core")

    big = ((ROWS, FEAT), BF16)
    keep, send = call(
        functools.partial(left_kernel, scale),
        [(CHUNKED, F32), (CHUNKED, BF16)],
        (at, out_grad, context, tied(low, c_near), warm, warm_near, warm_far, warm_diag),
        2_000_000_000,
        "left",
        [((RANK, FEAT), F32)],
    )
    g_far = swap(tied(out_grad, warm_near), "zl")
    g_near = in_hbm(swap(tied(out_grad, warm_far, low), "core"))
    turned = [((ROWS, TOK), BF16)] * 2
    (merged,) = call_grid(
        functools.partial(merge_kernel, scale),
        4,
        [((ROWS, FEAT), F32, column(ROWS))],
        [column(ROWS), VMEM, VMEM, column(TOK), column(TOK)],
        (error, c_own, c_near, out_grad, g_near),
        1_100_000_000,
        "merge",
        turned,
        loose=(3,),
    )
    part = across_plane(keep, send, (merged,))
    g_diag = swap(tied(g_far, part), "core")

    def grad(g0, g1):
        (out,) = call(
            grad_kernel,
            [pair],
            (g0, g1, weight),
            1_100_000_000,
            "grad",
            [big] + [((TOK, FEAT), BF16)] * 2,
            held=range(3),
            free=True,
            sems=3,
        )
        return out

    i_home = grad(out_grad, g_near)
    zs = across_z(tied(part, g_far), (i_home,))
    c_far = swap(tied(c_far, *zs[1:]), "zl")
    mine = back_over_plane(*zs)

    i_far = grad(g_far, g_diag)
    other = swap(tied(mine, i_far, c_far), "core")
    i_far = swap(i_far, "zl")
    i_near = swap(i_home, "core")

    mine_half, proj = call(
        early_kernel,
        [((HALF, FEAT), BF16), ((HALF, TOK), F32)],
        (context, mine),
        150_000_000,
        "early",
    )
    other = tied(other, proj)
    keep, send, left = call(
        functools.partial(right_kernel, scale),
        [(CHUNKED, F32), (CHUNKED, BF16), ((RANK, FEAT), BF16)],
        (at, context, out_grad, kept, mine_half, proj, other),
        2_000_000_000,
        "right",
        [((RANK, FEAT), F32), big, ((RANK, TOK), F32)],
        held=(3,),
        sems=1,
    )

    table = ((RANK, 2 * RANK), F32)
    (a,) = call(gram_kernel, [table], (left,), 300_000_000, "gram")
    (a,) = call(
        functools.partial(step_kernel, PART), [table], (a,), 300_000_000, "step", alias={0: 0}
    )
    part = across_plane(keep, send, (a,))
    part = tied(part, i_far, i_near)
    c_diag = swap(c_far, "core")
    zs = across_z(part)
    i_diag = swap(tied(i_far, zs[0]), "core")
    (a,) = call(
        functools.partial(step_kernel, 2 * PART), [table], (a,), 300_000_000, "step", alias={0: 0}
    )
    mine = back_over_plane(*zs, beside=(a, c_diag, i_diag))
    first = pl.BlockSpec((None, TOK, ROWS), lambda j: (0, 0, 0))
    second = pl.BlockSpec((None, TOK, ROWS), lambda j: (1, 0, 0))
    (in_grad,) = call_grid(
        place_kernel,
        1,
        [((TOK, FEAT), BF16, whole(TOK, FEAT))],
        [SMEM, first, second, first, second],
        (at, i_home, i_near, i_far, i_diag),
        1_000_000,
        "place",
    )
    inverse, basis = call(
        basis_kernel,
        [((RANK, RANK), F32), ((ROWS, RANK), BF16)],
        (at, a, left),
        300_000_000,
        "basis",
        [table],
    )
    other = swap(tied(mine, basis, in_grad), "core")
    begun, t2, t3 = call(
        begin_kernel,
        [((RANK, FEAT), F32)] + turned,
        (at, mine, inverse, c_far, c_diag),
        300_000_000,
        "begin",
        [((HALF, FEAT), BF16)],
    )
    other = tied(other, begun)

    new_error, factor_q = call_grid(
        functools.partial(last_kernel, 1.0 / (SIZES[0] * SIZES[1] * SIZES[2]), scale),
        4,
        [
            ((ROWS, FEAT), F32, column(ROWS)),
            ((ROWS, RANK), F32, whole(ROWS, RANK)),
        ],
        [SMEM, VMEM, VMEM, whole(ROWS, RANK), VMEM, VMEM, VMEM]
        + [column(ROWS), column(TOK), column(TOK)],
        (at, other, inverse, basis, begun, t2, t3, merged, g_far, g_diag),
        2_000_000_000,
        "last",
        [((HALF, FEAT), BF16)],
    )
    return in_grad, new_error[None], factor_q


def solution(mesh):
    split = Mesh(np.asarray(mesh.devices).reshape(SIZES), AXES)
    every = ("zh", "y", "x", "zl", "core")
    shard = ("zl", "core")
    return jax.shard_map(
        on_device,
        mesh=split,
        in_specs=(
            P(every, None),
            P(every, None),
            P(shard, None),
            P(("zh", "y", "x"), shard, None),
            P(shard, None),
        ),
        out_specs=(P(every, None), P(("zh", "y", "x"), shard, None), P(shard, None)),
        check_vma=False,
    )
```

```python
import functools
import math

import jax
import jax.numpy as jnp
import numpy as np
from jax import lax
from jax.experimental import pallas as pl
from jax.experimental.pallas import tpu as pltpu
from jax.sharding import Mesh, PartitionSpec as P

BF16 = jnp.bfloat16
F32 = jnp.float32
HI = lax.Precision.HIGHEST
PART = 64
SUB = 8
AXES = ("zh", "y", "x", "zl", "core")
SIZES = (4, 4, 4, 2, 2)
ROWS = 512
RANK = 256
FEAT = 2048
TOK = 256
HALF = RANK // 2
CHUNKS, CHUNK_ROWS, CHUNK_COLS = 16, 16, 1024
VMEM = pl.BlockSpec(memory_space=pltpu.VMEM)
SMEM = pl.BlockSpec(memory_space=pltpu.SMEM)
ANY = pl.BlockSpec(memory_space=pl.ANY)


def swap(x, axis):
    return lax.ppermute(x, axis, [(0, 1), (1, 0)])


def mm(a, b, ca, cb):
    return lax.dot_general(a, b, (((ca,), (cb,)), ((), ())), preferred_element_type=F32)


def two(x):
    high = x.astype(BF16)
    return high, (x - high.astype(F32)).astype(BF16)


def chunk_at(n):
    return n // 2 * CHUNK_ROWS, n % 2 * CHUNK_COLS


def fetch(sources, targets, sems):
    copies = [
        pltpu.make_async_copy(src, dst, sems.at[n]) for n, (src, dst) in enumerate(zip(sources, targets))
    ]
    for copy in copies:
        copy.start()
    return copies


def split_halves(core, total, keep, send):
    for n in range(CHUNKS):
        row, col = chunk_at(n)
        cols = pl.ds(col, CHUNK_COLS)
        keep[n] = total[pl.ds(pl.multiple_of(core * HALF + row, CHUNK_ROWS), CHUNK_ROWS), cols]
        send[n] = total[
            pl.ds(pl.multiple_of((1 - core) * HALF + row, CHUNK_ROWS), CHUNK_ROWS), cols
        ].astype(send.dtype)


def block(zl, core):
    return pl.ds(pl.multiple_of((zl * 2 + core) * ROWS, ROWS), ROWS)


def prepare_kernel(at, ctx, err, own, near, far, low, kept):
    zl, core = at[0], at[1]
    own[...] = ctx[:, block(zl, core)]
    near[...] = ctx[:, block(zl, 1 - core)]
    far[0] = ctx[:, block(1 - zl, core)]
    far[1] = ctx[:, block(1 - zl, 1 - core)]
    rows = err.shape[0]
    kept[...] = err[...].astype(BF16)
    low[pl.ds(pl.multiple_of(pl.program_id(0) * rows, rows), rows), :] = kept[...]


def left_kernel(scale, at, og, ctx, low, w0, w1, w2, w3, keep, send, total):
    zl, core = at[0], at[1]
    where = ((zl, core), (zl, 1 - core), (1 - zl, core), (1 - zl, 1 - core))
    proj = jnp.zeros((TOK, RANK), F32)
    own = jnp.zeros((ROWS, RANK), F32)
    for (a, b), w in zip(where, (w0, w1, w2, w3)):
        cols = block(a, b)
        proj += mm(og[:, cols], w[...], 1, 0)
        own += mm(low[:, cols], w[...], 1, 0)
    first, second = two(proj * scale)
    total[...] = mm(first, ctx[...], 0, 0) + mm(second, ctx[...], 0, 0)
    total[:, block(zl, core)] += own.T
    split_halves(core, total, keep, send)


def unchunk(chunks, half):
    for n in range(CHUNKS):
        row, col = chunk_at(n)
        half[row : row + CHUNK_ROWS, col : col + CHUNK_COLS] = chunks[n]


def early_kernel(ctx, mine, half, proj):
    unchunk(mine, half)
    proj[...] = mm(half[...], ctx[...], 1, 1)


def right_kernel(
    scale, at, ctx, og, low_hbm, mine, proj_mine, other, keep, send, left, total, low, proj, sems
):
    zl, core = at[0], at[1]
    copy = pltpu.make_async_copy(low_hbm, low, sems.at[0])
    copy.start()
    here = pl.ds(pl.multiple_of(core * HALF, HALF), HALF)
    there = pl.ds(pl.multiple_of((1 - core) * HALF, HALF), HALF)
    unchunk(other, left.at[there, :])
    left[here, :] = mine[...]
    proj[here, :] = proj_mine[...]
    proj[there, :] = mm(left[there, :], ctx[...], 1, 1)
    first, second = two(proj[...] * scale)
    total[...] = mm(first, og[...], 1, 0) + mm(second, og[...], 1, 0)
    own = left[:, block(zl, core)]
    copy.wait()
    total[...] += mm(own, low[...], 1, 0)
    split_halves(core, total, keep, send)


def add_kernel(keep, got, out):
    out[...] = (keep[...] + got[...].astype(F32)).astype(BF16)


def spread_kernel(parts, out):
    total = parts[0].astype(F32)
    for n in range(1, parts.shape[0]):
        total += parts[n].astype(F32)
    total = total.astype(BF16)
    for n in range(out.shape[0]):
        out[n] = total


def row_of(x, k):
    return jnp.broadcast_to(x[k : k + 1, :], x.shape)


def factor_block(rows):
    shape = rows[0].shape
    sub = lax.broadcasted_iota(jnp.int32, shape, 0)
    for p in range(len(rows)):
        cols = [
            [jnp.broadcast_to(r[:, SUB * p + k : SUB * p + k + 1], shape) for k in range(SUB)]
            for r in rows[p:]
        ]
        for k in range(SUB):
            diagonal = row_of(cols[0][k], k)
            inv = lax.rsqrt(diagonal)
            inv = inv * (1.5 - 0.5 * diagonal * inv * inv)
            pivot = row_of(rows[p], k) * inv
            later = [row_of(cols[0][j], k) * inv for j in range(k + 1, SUB)]
            for g, col in enumerate(cols, p):
                times = col[k] * inv
                if g == p:
                    times = jnp.where(sub > k, times, 0.0)
                rows[g] = rows[g] - times * pivot
                if g == p:
                    rows[g] = jnp.where(sub == k, pivot, rows[g])
                for j, entry in zip(range(k + 1, SUB), later):
                    col[j] = col[j] - times * entry
    return rows


def dot_hi(a, b, ca, cb):
    return lax.dot_general(
        a, b, (((ca,), (cb,)), ((), ())), precision=HI, preferred_element_type=F32
    )


def eye(n):
    shape = (n, n)
    same = lax.broadcasted_iota(jnp.int32, shape, 0) == lax.broadcasted_iota(jnp.int32, shape, 1)
    return same.astype(F32)


def eliminate(start, a):
    stop = start + PART
    rows = jnp.concatenate([a[start:stop, start:stop], eye(PART)], 1)
    rows = factor_block([rows[n : n + SUB] for n in range(0, PART, SUB)])
    inverse = jnp.concatenate(rows, 0)[:, PART:]
    panel = dot_hi(inverse, a[start:stop, :], 1, 0)
    a[start:stop, :] = panel
    if stop < RANK:
        a[stop:, :] = a[stop:, :] - dot_hi(panel[:, stop:RANK], panel, 0, 0)


def gram_kernel(left, a):
    a[:, :RANK] = mm(left[...], left[...], 1, 1)
    a[:, RANK:] = eye(RANK)
    eliminate(0, a)


def step_kernel(start, a_in, a):
    eliminate(start, a)


def basis_kernel(at, a_in, left, inverse, basis, a):
    a[...] = a_in[...]
    eliminate(RANK - PART, a)
    inverse[...] = a[:, RANK:]
    first, second = two(a[:, RANK:])
    own = left[:, block(at[0], at[1])]
    basis[...] = (mm(first, own, 1, 0) + mm(second, own, 1, 0)).astype(BF16).T


def grad_kernel(h0, h1, weight_hbm, out, weight, g0, g1, sems):
    copies = fetch((weight_hbm, h0, h1), (weight, g0, g1), sems)
    copies[0].wait()
    for n, g in enumerate((g0, g1)):
        copies[n + 1].wait()
        out[n] = mm(g[...], weight[...], 1, 1).astype(BF16)


def merge_kernel(scale, err, c0, c1, g0, g1, out, t0, t1):
    step = pl.program_id(0)

    @pl.when(step == 0)
    def _():
        t0[...] = c0[...].T
        t1[...] = c1[...].T

    total = mm(t0[...], g0[...], 1, 0) + mm(t1[...], g1[...], 1, 0)
    out[...] = err[...] + total * scale


def place_kernel(at, own, near, far, diag, out):
    zl, core = at[0], at[1]
    out[:, block(zl, core)] = own[...]
    out[:, block(zl, 1 - core)] = near[...]
    out[:, block(1 - zl, core)] = far[...]
    out[:, block(1 - zl, 1 - core)] = diag[...]


def columns_of(inverse, half):
    return inverse[:, pl.ds(pl.multiple_of(half * HALF, HALF), HALF)]


def begin_kernel(at, chunks, inverse, c2, c3, out, t2, t3, half):
    t2[...] = c2[0].T
    t3[...] = c3[1].T
    unchunk(chunks, half)
    first, second = two(columns_of(inverse, at[1]))
    out[...] = mm(first, half[...], 1, 0) + mm(second, half[...], 1, 0)


def last_kernel(
    share, scale, at, other, inverse, basis, begun, t2, t3, merged, g2, g3,
    new_error, factor_q, half,
):
    step = pl.program_id(0)
    zl, core = at[0], at[1]

    @pl.when(step == 0)
    def _():
        unchunk(other, half)

    cols = pl.ds(pl.multiple_of(step * ROWS, ROWS), ROWS)
    first, second = two(columns_of(inverse, 1 - core))
    q = mm(first, half[:, cols], 1, 0) + mm(second, half[:, cols], 1, 0)
    q = (begun[:, cols] + q) * share
    total = mm(t2[...], g2[...], 1, 0) + mm(t3[...], g3[...], 1, 0)
    new_error[...] = merged[...] + total * scale - mm(basis[...], q.astype(BF16), 1, 0)

    @pl.when(step == zl * 2 + core)
    def _():
        factor_q[...] = q.T


def size(shape, dtype):
    return math.prod(shape) * jnp.dtype(dtype).itemsize


def in_hbm(x):
    return pltpu.with_memory_space_constraint(x, pltpu.HBM)


def call(
    kernel, outs, args, flops, name, scratch=(), alias=None, limit=12, loose=(), held=(), free=False, sems=0
):
    args = [in_hbm(a) if n in held else a for n, a in enumerate(args)]
    moved = sum(size(a.shape, a.dtype) for a in args) + sum(size(s, d) for s, d in outs)
    scratch = [pltpu.VMEM(s, d) for s, d in scratch]
    if sems:
        scratch.append(pltpu.SemaphoreType.DMA((sems,)))
    return pl.pallas_call(
        kernel,
        out_shape=[(pltpu.HBM if free else jax.ShapeDtypeStruct)(s, d) for s, d in outs],
        in_specs=[
            SMEM if a.dtype == jnp.int32 else ANY if n in loose or n in held else VMEM
            for n, a in enumerate(args)
        ],
        out_specs=[pl.BlockSpec(s, lambda s=s: (0,) * len(s)) if free else VMEM for s, _ in outs],
        scratch_shapes=scratch,
        input_output_aliases=alias or {},
        compiler_params=pltpu.CompilerParams(vmem_limit_bytes=limit * 2**20),
        cost_estimate=pl.CostEstimate(flops=flops, bytes_accessed=moved, transcendentals=0),
        name=name,
    )(*args)


def call_grid(kernel, steps, outs, ins, args, flops, name, scratch=(), sems=0, limit=14, loose=(), alias=None):
    args = [
        a if spec in (SMEM, ANY, VMEM) or n in loose else in_hbm(a)
        for n, (a, spec) in enumerate(zip(args, ins))
    ]
    moved = sum(size(a.shape, a.dtype) for a in args) + sum(size(s, d) for s, d, _ in outs)
    scratch = [pltpu.VMEM(s, d) for s, d in scratch]
    if sems:
        scratch.append(pltpu.SemaphoreType.DMA((sems,)))
    return pl.pallas_call(
        kernel,
        grid=(steps,),
        out_shape=[
            (jax.ShapeDtypeStruct if spec is VMEM else pltpu.HBM)(s, d) for s, d, spec in outs
        ],
        in_specs=ins,
        out_specs=[spec for _, _, spec in outs],
        scratch_shapes=scratch,
        input_output_aliases=alias or {},
        compiler_params=pltpu.CompilerParams(vmem_limit_bytes=limit * 2**20),
        cost_estimate=pl.CostEstimate(flops=flops, bytes_accessed=moved, transcendentals=0),
        name=name,
    )(*args)


def whole(*shape):
    return pl.BlockSpec(shape, lambda j: (0,) * len(shape))


def column(rows):
    return pl.BlockSpec((rows, ROWS), lambda j: (0, j))


def rows_of(rows, cols):
    return pl.BlockSpec((rows, cols), lambda j: (j, 0))


CHUNKED = (CHUNKS, CHUNK_ROWS, CHUNK_COLS)
CHUNK = (CHUNK_ROWS, CHUNK_COLS)


def tied(x, *others):
    return lax.optimization_barrier((x,) + others)[0]


def spread(parts, times):
    (out,) = call(spread_kernel, [((times,) + CHUNK, BF16)], (parts,), 1_000_000, "spread")
    return out


def across_plane(keep, send, beside=()):
    got = swap(send, "core")
    (half,) = call(add_kernel, [(CHUNKED, BF16)], (keep, got), 1_000_000, "add")
    parts = tied(lax.all_to_all(half, ("y", "x"), 0, 0), *beside)
    return spread(parts, 8)


def across_z(copies, beside=()):
    return tied(lax.all_to_all(copies, ("zh", "zl"), 0, 0), *beside)


def back_over_plane(parts, beside=()):
    return lax.all_to_all(spread(tied(parts, *beside), CHUNKS), ("y", "x"), 0, 0)


def on_device(context, out_grad, weight, error, warm):
    scale = 1.0 / math.sqrt(TOK * 4)
    core = lax.axis_index("core")
    zl = lax.axis_index("zl")
    at = jnp.stack([zl, core]).astype(jnp.int32)
    error = error[0]
    tokens = ((TOK, ROWS), BF16)
    pair = ((2, TOK, ROWS), BF16)

    warm_far = swap(warm, "zl")
    warm_near = swap(warm, "core")
    quarter = rows_of(TOK // 4, ROWS)
    strip = rows_of(ROWS // 4, FEAT)
    c_own, c_near, c_far, low, kept = call_grid(
        prepare_kernel,
        4,
        [tokens + (quarter,)] * 2
        + [pair + (pl.BlockSpec((2, TOK // 4, ROWS), lambda j: (0, j, 0)),)]
        + [((ROWS, FEAT), BF16, VMEM), ((ROWS, FEAT), BF16, strip)],
        [SMEM, rows_of(TOK // 4, FEAT), strip],
        (tied(at, warm_near), context, error),
        4_000_000,
        "prepare",
    )
    warm_diag = swap(tied(warm_far, low), "core")
    c_near = swap(c_near, "core")

    big = ((ROWS, FEAT), BF16)
    keep, send = call(
        functools.partial(left_kernel, scale),
        [(CHUNKED, F32), (CHUNKED, BF16)],
        (at, out_grad, context, tied(low, c_near), warm, warm_near, warm_far, warm_diag),
        2_000_000_000,
        "left",
        [((RANK, FEAT), F32)],
    )
    g_far = swap(tied(out_grad, warm_near), "zl")
    g_near = in_hbm(swap(tied(out_grad, warm_far, low), "core"))
    turned = [((ROWS, TOK), BF16)] * 2
    (merged,) = call_grid(
        functools.partial(merge_kernel, scale),
        4,
        [((ROWS, FEAT), F32, column(ROWS))],
        [column(ROWS), VMEM, VMEM, column(TOK), column(TOK)],
        (error, c_own, c_near, out_grad, g_near),
        1_100_000_000,
        "merge",
        turned,
        loose=(3,),
    )
    part = across_plane(keep, send, (merged,))
    g_diag = swap(tied(g_far, part), "core")

    def grad(g0, g1):
        (out,) = call(
            grad_kernel,
            [pair],
            (g0, g1, weight),
            1_100_000_000,
            "grad",
            [big] + [((TOK, FEAT), BF16)] * 2,
            held=range(3),
            free=True,
            sems=3,
        )
        return out

    i_home = grad(out_grad, g_near)
    zs = across_z(tied(part, g_far), (i_home,))
    c_far = swap(tied(c_far, zs), "zl")
    mine = back_over_plane(zs)

    i_far = grad(g_far, g_diag)
    other = swap(tied(mine, i_far, c_far), "core")
    i_far = swap(i_far, "zl")
    i_near = swap(i_home, "core")

    mine_half, proj = call(
        early_kernel,
        [((HALF, FEAT), BF16), ((HALF, TOK), F32)],
        (context, mine),
        150_000_000,
        "early",
    )
    other = tied(other, proj)
    keep, send, left = call(
        functools.partial(right_kernel, scale),
        [(CHUNKED, F32), (CHUNKED, BF16), ((RANK, FEAT), BF16)],
        (at, context, out_grad, kept, mine_half, proj, other),
        2_000_000_000,
        "right",
        [((RANK, FEAT), F32), big, ((RANK, TOK), F32)],
        held=(3,),
        sems=1,
    )

    table = ((RANK, 2 * RANK), F32)
    (a,) = call(gram_kernel, [table], (left,), 300_000_000, "gram")
    (a,) = call(
        functools.partial(step_kernel, PART), [table], (a,), 300_000_000, "step", alias={0: 0}
    )
    part = across_plane(keep, send, (a,))
    part = tied(part, i_far, i_near)
    c_diag = swap(c_far, "core")
    i_diag = swap(tied(i_far, part), "core")
    (a,) = call(
        functools.partial(step_kernel, 2 * PART), [table], (a,), 300_000_000, "step", alias={0: 0}
    )
    zs = across_z(part, (a,))
    mine = back_over_plane(zs)
    first = pl.BlockSpec((None, TOK, ROWS), lambda j: (0, 0, 0))
    second = pl.BlockSpec((None, TOK, ROWS), lambda j: (1, 0, 0))
    (in_grad,) = call_grid(
        place_kernel,
        1,
        [((TOK, FEAT), BF16, whole(TOK, FEAT))],
        [SMEM, first, second, first, second],
        (at, i_home, i_near, i_far, i_diag),
        1_000_000,
        "place",
    )
    inverse, basis = call(
        basis_kernel,
        [((RANK, RANK), F32), ((ROWS, RANK), BF16)],
        (at, a, left),
        300_000_000,
        "basis",
        [table],
    )
    other = swap(tied(mine, basis, in_grad), "core")
    begun, t2, t3 = call(
        begin_kernel,
        [((RANK, FEAT), F32)] + turned,
        (at, mine, inverse, c_far, c_diag),
        300_000_000,
        "begin",
        [((HALF, FEAT), BF16)],
    )
    other = tied(other, begun)

    new_error, factor_q = call_grid(
        functools.partial(last_kernel, 1.0 / (SIZES[0] * SIZES[1] * SIZES[2]), scale),
        4,
        [
            ((ROWS, FEAT), F32, column(ROWS)),
            ((ROWS, RANK), F32, whole(ROWS, RANK)),
        ],
        [SMEM, VMEM, VMEM, whole(ROWS, RANK), VMEM, VMEM, VMEM]
        + [column(ROWS), column(TOK), column(TOK)],
        (at, other, inverse, basis, begun, t2, t3, merged, g_far, g_diag),
        2_000_000_000,
        "last",
        [((HALF, FEAT), BF16)],
    )
    return in_grad, new_error[None], factor_q


def solution(mesh):
    split = Mesh(np.asarray(mesh.devices).reshape(SIZES), AXES)
    every = ("zh", "y", "x", "zl", "core")
    shard = ("zl", "core")
    return jax.shard_map(
        on_device,
        mesh=split,
        in_specs=(
            P(every, None),
            P(every, None),
            P(shard, None),
            P(("zh", "y", "x"), shard, None),
            P(shard, None),
        ),
        out_specs=(P(every, None), P(("zh", "y", "x"), shard, None), P(shard, None)),
        check_vma=False,
    )
```

```python
import functools
import math

import jax
import jax.numpy as jnp
import numpy as np
from jax import lax
from jax.experimental import pallas as pl
from jax.experimental.pallas import tpu as pltpu
from jax.sharding import Mesh, PartitionSpec as P

BF16 = jnp.bfloat16
F32 = jnp.float32
HI = lax.Precision.HIGHEST
PART = 64
SUB = 8
AXES = ("zh", "y", "x", "zl", "core")
SIZES = (4, 4, 4, 2, 2)
ROWS = 512
RANK = 256
FEAT = 2048
TOK = 256
HALF = RANK // 2
CHUNKS, CHUNK_ROWS, CHUNK_COLS = 16, 16, 1024
VMEM = pl.BlockSpec(memory_space=pltpu.VMEM)
SMEM = pl.BlockSpec(memory_space=pltpu.SMEM)
ANY = pl.BlockSpec(memory_space=pl.ANY)


def swap(x, axis):
    return lax.ppermute(x, axis, [(0, 1), (1, 0)])


def mm(a, b, ca, cb):
    return lax.dot_general(a, b, (((ca,), (cb,)), ((), ())), preferred_element_type=F32)


def two(x):
    high = x.astype(BF16)
    return high, (x - high.astype(F32)).astype(BF16)


def chunk_at(n):
    return n // 2 * CHUNK_ROWS, n % 2 * CHUNK_COLS


def fetch(sources, targets, sems):
    copies = [
        pltpu.make_async_copy(src, dst, sems.at[n]) for n, (src, dst) in enumerate(zip(sources, targets))
    ]
    for copy in copies:
        copy.start()
    return copies


def split_halves(core, total, keep, send):
    for n in range(CHUNKS):
        row, col = chunk_at(n)
        cols = pl.ds(col, CHUNK_COLS)
        keep[n] = total[pl.ds(pl.multiple_of(core * HALF + row, CHUNK_ROWS), CHUNK_ROWS), cols]
        send[n] = total[
            pl.ds(pl.multiple_of((1 - core) * HALF + row, CHUNK_ROWS), CHUNK_ROWS), cols
        ].astype(send.dtype)


def block(zl, core):
    return pl.ds(pl.multiple_of((zl * 2 + core) * ROWS, ROWS), ROWS)


def prepare_kernel(at, ctx, err, own, near, far, low, kept):
    zl, core = at[0], at[1]
    own[...] = ctx[:, block(zl, core)]
    near[...] = ctx[:, block(zl, 1 - core)]
    far[0] = ctx[:, block(1 - zl, core)]
    far[1] = ctx[:, block(1 - zl, 1 - core)]
    rows = err.shape[0]
    kept[...] = err[...].astype(BF16)
    low[pl.ds(pl.multiple_of(pl.program_id(0) * rows, rows), rows), :] = kept[...]


def left_kernel(scale, at, og, ctx, low, w0, w1, w2, w3, keep, send, total):
    zl, core = at[0], at[1]
    where = ((zl, core), (zl, 1 - core), (1 - zl, core), (1 - zl, 1 - core))
    proj = jnp.zeros((TOK, RANK), F32)
    own = jnp.zeros((ROWS, RANK), F32)
    for (a, b), w in zip(where, (w0, w1, w2, w3)):
        cols = block(a, b)
        proj += mm(og[:, cols], w[...], 1, 0)
        own += mm(low[:, cols], w[...], 1, 0)
    first, second = two(proj * scale)
    total[...] = mm(first, ctx[...], 0, 0) + mm(second, ctx[...], 0, 0)
    total[:, block(zl, core)] += own.T
    split_halves(core, total, keep, send)


def unchunk(chunks, half):
    for n in range(CHUNKS):
        row, col = chunk_at(n)
        half[row : row + CHUNK_ROWS, col : col + CHUNK_COLS] = chunks[n]


def early_kernel(ctx, mine, half, proj):
    unchunk(mine, half)
    proj[...] = mm(half[...], ctx[...], 1, 1)


def right_kernel(
    scale, at, ctx, og, low_hbm, mine, proj_mine, other, keep, send, left, total, low, proj, sems
):
    zl, core = at[0], at[1]
    copy = pltpu.make_async_copy(low_hbm, low, sems.at[0])
    copy.start()
    here = pl.ds(pl.multiple_of(core * HALF, HALF), HALF)
    there = pl.ds(pl.multiple_of((1 - core) * HALF, HALF), HALF)
    unchunk(other, left.at[there, :])
    left[here, :] = mine[...]
    proj[here, :] = proj_mine[...]
    proj[there, :] = mm(left[there, :], ctx[...], 1, 1)
    first, second = two(proj[...] * scale)
    total[...] = mm(first, og[...], 1, 0) + mm(second, og[...], 1, 0)
    own = left[:, block(zl, core)]
    copy.wait()
    total[...] += mm(own, low[...], 1, 0)
    split_halves(core, total, keep, send)


def add_kernel(keep, got, out):
    out[...] = (keep[...] + got[...].astype(F32)).astype(BF16)


def spread_kernel(parts, out):
    total = parts[0].astype(F32)
    for n in range(1, parts.shape[0]):
        total += parts[n].astype(F32)
    total = total.astype(BF16)
    for n in range(out.shape[0]):
        out[n] = total


def row_of(x, k):
    return jnp.broadcast_to(x[k : k + 1, :], x.shape)


def factor_block(rows):
    shape = rows[0].shape
    sub = lax.broadcasted_iota(jnp.int32, shape, 0)
    for p in range(len(rows)):
        cols = [
            [jnp.broadcast_to(r[:, SUB * p + k : SUB * p + k + 1], shape) for k in range(SUB)]
            for r in rows[p:]
        ]
        for k in range(SUB):
            diagonal = row_of(cols[0][k], k)
            inv = lax.rsqrt(diagonal)
            inv = inv * (1.5 - 0.5 * diagonal * inv * inv)
            pivot = row_of(rows[p], k) * inv
            later = [row_of(cols[0][j], k) * inv for j in range(k + 1, SUB)]
            for g, col in enumerate(cols, p):
                times = col[k] * inv
                if g == p:
                    times = jnp.where(sub > k, times, 0.0)
                rows[g] = rows[g] - times * pivot
                if g == p:
                    rows[g] = jnp.where(sub == k, pivot, rows[g])
                for j, entry in zip(range(k + 1, SUB), later):
                    col[j] = col[j] - times * entry
    return rows


def dot_hi(a, b, ca, cb):
    return lax.dot_general(
        a, b, (((ca,), (cb,)), ((), ())), precision=HI, preferred_element_type=F32
    )


def eye(n):
    shape = (n, n)
    same = lax.broadcasted_iota(jnp.int32, shape, 0) == lax.broadcasted_iota(jnp.int32, shape, 1)
    return same.astype(F32)


def eliminate(start, a):
    stop = start + PART
    rows = jnp.concatenate([a[start:stop, start:stop], eye(PART)], 1)
    rows = factor_block([rows[n : n + SUB] for n in range(0, PART, SUB)])
    inverse = jnp.concatenate(rows, 0)[:, PART:]
    panel = dot_hi(inverse, a[start:stop, :], 1, 0)
    a[start:stop, :] = panel
    if stop < RANK:
        a[stop:, :] = a[stop:, :] - dot_hi(panel[:, stop:RANK], panel, 0, 0)


def gram_kernel(left, a):
    a[:, :RANK] = mm(left[...], left[...], 1, 1)
    a[:, RANK:] = eye(RANK)
    eliminate(0, a)


def step_kernel(start, a_in, a):
    eliminate(start, a)


def basis_kernel(at, a_in, left, inverse, basis, a):
    a[...] = a_in[...]
    eliminate(RANK - PART, a)
    inverse[...] = a[:, RANK:]
    first, second = two(a[:, RANK:])
    own = left[:, block(at[0], at[1])]
    basis[...] = -(mm(first, own, 1, 0) + mm(second, own, 1, 0)).astype(BF16).T


def grad_kernel(h0, h1, weight_hbm, out, weight, g0, g1, sems):
    copies = fetch((weight_hbm, h0, h1), (weight, g0, g1), sems)
    copies[0].wait()
    for n, g in enumerate((g0, g1)):
        copies[n + 1].wait()
        out[n] = mm(g[...], weight[...], 1, 1).astype(BF16)


def merge_kernel(scale, err, c0, c1, g0, g1, out, t0, t1):
    step = pl.program_id(0)

    @pl.when(step == 0)
    def _():
        t0[...] = c0[...].T
        t1[...] = c1[...].T

    total = mm(t0[...], g0[...], 1, 0) + mm(t1[...], g1[...], 1, 0)
    out[...] = err[...] + total * scale


def place_kernel(at, own, near, far, diag, out):
    zl, core = at[0], at[1]
    out[:, block(zl, core)] = own[...]
    out[:, block(zl, 1 - core)] = near[...]
    out[:, block(1 - zl, core)] = far[...]
    out[:, block(1 - zl, 1 - core)] = diag[...]


def columns_of(inverse, half):
    return inverse[:, pl.ds(pl.multiple_of(half * HALF, HALF), HALF)]


def begin_kernel(scale, at, chunks, inverse, c2, c3, out, turned, half):
    turned[:, :TOK] = (c2[0].T * scale).astype(BF16)
    turned[:, TOK:] = (c3[1].T * scale).astype(BF16)
    unchunk(chunks, half)
    first, second = two(columns_of(inverse, at[1]))
    out[...] = mm(first, half[...], 1, 0) + mm(second, half[...], 1, 0)


def last_kernel(
    share, at, other, inverse, basis, begun, turned, merged, g2, g3,
    new_error, factor_q, half,
):
    step = pl.program_id(0)
    zl, core = at[0], at[1]

    @pl.when(step == 0)
    def _():
        unchunk(other, half)

    cols = pl.ds(pl.multiple_of(step * ROWS, ROWS), ROWS)
    first, second = two(columns_of(inverse, 1 - core))
    q = mm(first, half[:, cols], 1, 0) + mm(second, half[:, cols], 1, 0)
    q = (begun[:, cols] + q) * share
    lhs = jnp.concatenate([turned[...], basis[...]], 1)
    rhs = jnp.concatenate([g2[...], g3[...], q.astype(BF16)], 0)
    new_error[...] = merged[...] + mm(lhs, rhs, 1, 0)

    @pl.when(step == zl * 2 + core)
    def _():
        factor_q[...] = q.T


def size(shape, dtype):
    return math.prod(shape) * jnp.dtype(dtype).itemsize


def in_hbm(x):
    return pltpu.with_memory_space_constraint(x, pltpu.HBM)


def call(
    kernel, outs, args, flops, name, scratch=(), alias=None, limit=12, loose=(), held=(), free=False, sems=0
):
    args = [in_hbm(a) if n in held else a for n, a in enumerate(args)]
    moved = sum(size(a.shape, a.dtype) for a in args) + sum(size(s, d) for s, d in outs)
    scratch = [pltpu.VMEM(s, d) for s, d in scratch]
    if sems:
        scratch.append(pltpu.SemaphoreType.DMA((sems,)))
    return pl.pallas_call(
        kernel,
        out_shape=[(pltpu.HBM if free else jax.ShapeDtypeStruct)(s, d) for s, d in outs],
        in_specs=[
            SMEM if a.dtype == jnp.int32 else ANY if n in loose or n in held else VMEM
            for n, a in enumerate(args)
        ],
        out_specs=[pl.BlockSpec(s, lambda s=s: (0,) * len(s)) if free else VMEM for s, _ in outs],
        scratch_shapes=scratch,
        input_output_aliases=alias or {},
        compiler_params=pltpu.CompilerParams(vmem_limit_bytes=limit * 2**20),
        cost_estimate=pl.CostEstimate(flops=flops, bytes_accessed=moved, transcendentals=0),
        name=name,
    )(*args)


def call_grid(kernel, steps, outs, ins, args, flops, name, scratch=(), sems=0, limit=14, loose=(), alias=None):
    args = [
        a if spec in (SMEM, ANY, VMEM) or n in loose else in_hbm(a)
        for n, (a, spec) in enumerate(zip(args, ins))
    ]
    moved = sum(size(a.shape, a.dtype) for a in args) + sum(size(s, d) for s, d, _ in outs)
    scratch = [pltpu.VMEM(s, d) for s, d in scratch]
    if sems:
        scratch.append(pltpu.SemaphoreType.DMA((sems,)))
    return pl.pallas_call(
        kernel,
        grid=(steps,),
        out_shape=[
            (jax.ShapeDtypeStruct if spec is VMEM else pltpu.HBM)(s, d) for s, d, spec in outs
        ],
        in_specs=ins,
        out_specs=[spec for _, _, spec in outs],
        scratch_shapes=scratch,
        input_output_aliases=alias or {},
        compiler_params=pltpu.CompilerParams(vmem_limit_bytes=limit * 2**20),
        cost_estimate=pl.CostEstimate(flops=flops, bytes_accessed=moved, transcendentals=0),
        name=name,
    )(*args)


def whole(*shape):
    return pl.BlockSpec(shape, lambda j: (0,) * len(shape))


def column(rows):
    return pl.BlockSpec((rows, ROWS), lambda j: (0, j))


def rows_of(rows, cols):
    return pl.BlockSpec((rows, cols), lambda j: (j, 0))


CHUNKED = (CHUNKS, CHUNK_ROWS, CHUNK_COLS)
CHUNK = (CHUNK_ROWS, CHUNK_COLS)


def tied(x, *others):
    return lax.optimization_barrier((x,) + others)[0]


def spread(parts, times):
    (out,) = call(spread_kernel, [((times,) + CHUNK, BF16)], (parts,), 1_000_000, "spread")
    return out


def across_plane(keep, send, beside=()):
    got = swap(send, "core")
    (half,) = call(add_kernel, [(CHUNKED, BF16)], (keep, got), 1_000_000, "add")
    parts = tied(lax.all_to_all(half, ("y", "x"), 0, 0), *beside)
    return spread(parts, 8)


def across_z(copies, beside=()):
    return tied(lax.all_to_all(copies, ("zh", "zl"), 0, 0), *beside)


def back_over_plane(parts, beside=()):
    return lax.all_to_all(spread(tied(parts, *beside), CHUNKS), ("y", "x"), 0, 0)


def on_device(context, out_grad, weight, error, warm):
    scale = 1.0 / math.sqrt(TOK * 4)
    core = lax.axis_index("core")
    zl = lax.axis_index("zl")
    at = jnp.stack([zl, core]).astype(jnp.int32)
    error = error[0]
    tokens = ((TOK, ROWS), BF16)
    pair = ((2, TOK, ROWS), BF16)

    warm_far = swap(warm, "zl")
    warm_near = swap(warm, "core")
    quarter = rows_of(TOK // 4, ROWS)
    strip = rows_of(ROWS // 4, FEAT)
    c_own, c_near, c_far, low, kept = call_grid(
        prepare_kernel,
        4,
        [tokens + (quarter,)] * 2
        + [pair + (pl.BlockSpec((2, TOK // 4, ROWS), lambda j: (0, j, 0)),)]
        + [((ROWS, FEAT), BF16, VMEM), ((ROWS, FEAT), BF16, strip)],
        [SMEM, rows_of(TOK // 4, FEAT), strip],
        (tied(at, warm_near), context, error),
        4_000_000,
        "prepare",
    )
    warm_diag = swap(tied(warm_far, low), "core")
    c_near = swap(c_near, "core")

    big = ((ROWS, FEAT), BF16)
    keep, send = call(
        functools.partial(left_kernel, scale),
        [(CHUNKED, F32), (CHUNKED, BF16)],
        (at, out_grad, context, tied(low, c_near), warm, warm_near, warm_far, warm_diag),
        2_000_000_000,
        "left",
        [((RANK, FEAT), F32)],
    )
    g_far = swap(tied(out_grad, warm_near), "zl")
    g_near = in_hbm(swap(tied(out_grad, warm_far, low), "core"))
    turned = [((ROWS, TOK), BF16)] * 2
    (merged,) = call_grid(
        functools.partial(merge_kernel, scale),
        4,
        [((ROWS, FEAT), F32, column(ROWS))],
        [column(ROWS), VMEM, VMEM, column(TOK), column(TOK)],
        (error, c_own, c_near, out_grad, g_near),
        1_100_000_000,
        "merge",
        turned,
        loose=(3,),
    )
    part = across_plane(keep, send, (merged,))
    g_diag = swap(tied(g_far, part), "core")

    def grad(g0, g1):
        (out,) = call(
            grad_kernel,
            [pair],
            (g0, g1, weight),
            1_100_000_000,
            "grad",
            [big] + [((TOK, FEAT), BF16)] * 2,
            held=range(3),
            free=True,
            sems=3,
        )
        return out

    i_home = grad(out_grad, g_near)
    zs = across_z(tied(part, g_far), (i_home,))
    c_far = swap(tied(c_far, zs), "zl")
    mine = back_over_plane(zs)

    i_far = grad(g_far, g_diag)
    other = swap(tied(mine, i_far, c_far), "core")
    i_far = swap(i_far, "zl")
    i_near = swap(i_home, "core")

    mine_half, proj = call(
        early_kernel,
        [((HALF, FEAT), BF16), ((HALF, TOK), F32)],
        (context, mine),
        150_000_000,
        "early",
    )
    other = tied(other, proj)
    keep, send, left = call(
        functools.partial(right_kernel, scale),
        [(CHUNKED, F32), (CHUNKED, BF16), ((RANK, FEAT), BF16)],
        (at, context, out_grad, kept, mine_half, proj, other),
        2_000_000_000,
        "right",
        [((RANK, FEAT), F32), big, ((RANK, TOK), F32)],
        held=(3,),
        sems=1,
    )

    table = ((RANK, 2 * RANK), F32)
    (a,) = call(gram_kernel, [table], (left,), 300_000_000, "gram")
    (a,) = call(
        functools.partial(step_kernel, PART), [table], (a,), 300_000_000, "step", alias={0: 0}
    )
    part = across_plane(keep, send, (a,))
    part = tied(part, i_far)
    c_diag = swap(c_far, "core")
    i_diag = swap(tied(i_far, part), "core")
    (a,) = call(
        functools.partial(step_kernel, 2 * PART), [table], (a,), 300_000_000, "step", alias={0: 0}
    )
    inverse, basis = call(
        basis_kernel,
        [((RANK, RANK), F32), ((ROWS, RANK), BF16)],
        (at, a, left),
        300_000_000,
        "basis",
        [table],
    )
    zs = across_z(part, (basis,))
    mine = back_over_plane(zs)
    first = pl.BlockSpec((None, TOK, ROWS), lambda j: (0, 0, 0))
    second = pl.BlockSpec((None, TOK, ROWS), lambda j: (1, 0, 0))
    (in_grad,) = call_grid(
        place_kernel,
        1,
        [((TOK, FEAT), BF16, whole(TOK, FEAT))],
        [SMEM, first, second, first, second],
        (at, i_home, i_near, i_far, i_diag),
        1_000_000,
        "place",
    )
    other = swap(tied(mine, in_grad), "core")
    begun, far_turned = call(
        functools.partial(begin_kernel, scale),
        [((RANK, FEAT), F32), ((ROWS, 2 * TOK), BF16)],
        (at, mine, inverse, c_far, c_diag),
        300_000_000,
        "begin",
        [((HALF, FEAT), BF16)],
    )
    other = tied(other, begun)

    new_error, factor_q = call_grid(
        functools.partial(last_kernel, 1.0 / (SIZES[0] * SIZES[1] * SIZES[2])),
        4,
        [
            ((ROWS, FEAT), F32, column(ROWS)),
            ((ROWS, RANK), F32, whole(ROWS, RANK)),
        ],
        [SMEM, VMEM, VMEM, whole(ROWS, RANK), VMEM, VMEM]
        + [column(ROWS), column(TOK), column(TOK)],
        (at, other, inverse, basis, begun, far_turned, merged, g_far, g_diag),
        2_000_000_000,
        "last",
        [((HALF, FEAT), BF16)],
    )
    return in_grad, new_error[None], factor_q


def solution(mesh):
    split = Mesh(np.asarray(mesh.devices).reshape(SIZES), AXES)
    every = ("zh", "y", "x", "zl", "core")
    shard = ("zl", "core")
    return jax.shard_map(
        on_device,
        mesh=split,
        in_specs=(
            P(every, None),
            P(every, None),
            P(shard, None),
            P(("zh", "y", "x"), shard, None),
            P(shard, None),
        ),
        out_specs=(P(every, None), P(("zh", "y", "x"), shard, None), P(shard, None)),
        check_vma=False,
    )
```

```python
import functools
import math

import jax
import jax.numpy as jnp
import numpy as np
from jax import lax
from jax.experimental import pallas as pl
from jax.experimental.pallas import tpu as pltpu
from jax.sharding import Mesh, PartitionSpec as P

BF16 = jnp.bfloat16
F32 = jnp.float32
HI = lax.Precision.HIGHEST
PART = 64
SUB = 8
AXES = ("zh", "y", "x", "zl", "core")
SIZES = (4, 4, 4, 2, 2)
ROWS = 512
RANK = 256
FEAT = 2048
TOK = 256
HALF = RANK // 2
CHUNKS, CHUNK_ROWS, CHUNK_COLS = 16, 16, 1024
VMEM = pl.BlockSpec(memory_space=pltpu.VMEM)
SMEM = pl.BlockSpec(memory_space=pltpu.SMEM)
ANY = pl.BlockSpec(memory_space=pl.ANY)


def swap(x, axis):
    return lax.ppermute(x, axis, [(0, 1), (1, 0)])


def mm(a, b, ca, cb):
    return lax.dot_general(a, b, (((ca,), (cb,)), ((), ())), preferred_element_type=F32)


def two(x):
    high = x.astype(BF16)
    return high, (x - high.astype(F32)).astype(BF16)


def chunk_at(n):
    return n // 2 * CHUNK_ROWS, n % 2 * CHUNK_COLS


def fetch(sources, targets, sems):
    copies = [
        pltpu.make_async_copy(src, dst, sems.at[n]) for n, (src, dst) in enumerate(zip(sources, targets))
    ]
    for copy in copies:
        copy.start()
    return copies


def split_halves(core, total, keep, send):
    for n in range(CHUNKS):
        row, col = chunk_at(n)
        cols = pl.ds(col, CHUNK_COLS)
        keep[n] = total[pl.ds(pl.multiple_of(core * HALF + row, CHUNK_ROWS), CHUNK_ROWS), cols]
        send[n] = total[
            pl.ds(pl.multiple_of((1 - core) * HALF + row, CHUNK_ROWS), CHUNK_ROWS), cols
        ].astype(send.dtype)


def block(zl, core):
    return pl.ds(pl.multiple_of((zl * 2 + core) * ROWS, ROWS), ROWS)


def prepare_kernel(at, ctx, err, own, near, far, low, kept):
    zl, core = at[0], at[1]
    own[...] = ctx[:, block(zl, core)]
    near[...] = ctx[:, block(zl, 1 - core)]
    far[0] = ctx[:, block(1 - zl, core)]
    far[1] = ctx[:, block(1 - zl, 1 - core)]
    rows = err.shape[0]
    kept[...] = err[...].astype(BF16)
    low[pl.ds(pl.multiple_of(pl.program_id(0) * rows, rows), rows), :] = kept[...]


def left_kernel(scale, at, og, ctx, low, w0, w1, w2, w3, keep, send, total):
    zl, core = at[0], at[1]
    where = ((zl, core), (zl, 1 - core), (1 - zl, core), (1 - zl, 1 - core))
    proj = jnp.zeros((TOK, RANK), F32)
    own = jnp.zeros((ROWS, RANK), F32)
    for (a, b), w in zip(where, (w0, w1, w2, w3)):
        cols = block(a, b)
        proj += mm(og[:, cols], w[...], 1, 0)
        own += mm(low[:, cols], w[...], 1, 0)
    first, second = two(proj * scale)
    total[...] = mm(first, ctx[...], 0, 0) + mm(second, ctx[...], 0, 0)
    total[:, block(zl, core)] += own.T
    split_halves(core, total, keep, send)


def unchunk(chunks, half):
    for n in range(CHUNKS):
        row, col = chunk_at(n)
        half[row : row + CHUNK_ROWS, col : col + CHUNK_COLS] = chunks[n]


def early_kernel(ctx, mine, half, proj):
    unchunk(mine, half)
    proj[...] = mm(half[...], ctx[...], 1, 1)


def right_kernel(
    scale, at, ctx, og, low_hbm, mine, proj_mine, other, keep, send, left, total, low, proj, sems
):
    zl, core = at[0], at[1]
    copy = pltpu.make_async_copy(low_hbm, low, sems.at[0])
    copy.start()
    here = pl.ds(pl.multiple_of(core * HALF, HALF), HALF)
    there = pl.ds(pl.multiple_of((1 - core) * HALF, HALF), HALF)
    unchunk(other, left.at[there, :])
    left[here, :] = mine[...]
    proj[here, :] = proj_mine[...]
    proj[there, :] = mm(left[there, :], ctx[...], 1, 1)
    first, second = two(proj[...] * scale)
    total[...] = mm(first, og[...], 1, 0) + mm(second, og[...], 1, 0)
    own = left[:, block(zl, core)]
    copy.wait()
    total[...] += mm(own, low[...], 1, 0)
    split_halves(core, total, keep, send)


def add_kernel(keep, got, out):
    out[...] = (keep[...] + got[...].astype(F32)).astype(BF16)


def sum_kernel(parts, out):
    out[...] = parts[...].astype(F32).sum(0)


def close_kernel(part, one, opposite, three, out):
    part, one, opposite, three = (x[...].astype(F32) for x in (part, one, opposite, three))
    whole = ((part + opposite) + (one + three)).astype(BF16)
    for n in range(CHUNKS):
        out[n] = whole


def spread_kernel(parts, out):
    total = parts[0].astype(F32)
    for n in range(1, parts.shape[0]):
        total += parts[n].astype(F32)
    total = total.astype(BF16)
    for n in range(out.shape[0]):
        out[n] = total


def row_of(x, k):
    return jnp.broadcast_to(x[k : k + 1, :], x.shape)


def factor_block(rows):
    shape = rows[0].shape
    sub = lax.broadcasted_iota(jnp.int32, shape, 0)
    for p in range(len(rows)):
        cols = [
            [jnp.broadcast_to(r[:, SUB * p + k : SUB * p + k + 1], shape) for k in range(SUB)]
            for r in rows[p:]
        ]
        for k in range(SUB):
            diagonal = row_of(cols[0][k], k)
            inv = lax.rsqrt(diagonal)
            inv = inv * (1.5 - 0.5 * diagonal * inv * inv)
            pivot = row_of(rows[p], k) * inv
            later = [row_of(cols[0][j], k) * inv for j in range(k + 1, SUB)]
            for g, col in enumerate(cols, p):
                times = col[k] * inv
                if g == p:
                    times = jnp.where(sub > k, times, 0.0)
                rows[g] = rows[g] - times * pivot
                if g == p:
                    rows[g] = jnp.where(sub == k, pivot, rows[g])
                for j, entry in zip(range(k + 1, SUB), later):
                    col[j] = col[j] - times * entry
    return rows


def dot_hi(a, b, ca, cb):
    return lax.dot_general(
        a, b, (((ca,), (cb,)), ((), ())), precision=HI, preferred_element_type=F32
    )


def eye(n):
    shape = (n, n)
    same = lax.broadcasted_iota(jnp.int32, shape, 0) == lax.broadcasted_iota(jnp.int32, shape, 1)
    return same.astype(F32)


def eliminate(start, a):
    stop = start + PART
    rows = jnp.concatenate([a[start:stop, start:stop], eye(PART)], 1)
    rows = factor_block([rows[n : n + SUB] for n in range(0, PART, SUB)])
    inverse = jnp.concatenate(rows, 0)[:, PART:]
    panel = dot_hi(inverse, a[start:stop, :], 1, 0)
    a[start:stop, :] = panel
    if stop < RANK:
        a[stop:, :] = a[stop:, :] - dot_hi(panel[:, stop:RANK], panel, 0, 0)


def gram_kernel(left, a):
    a[:, :RANK] = mm(left[...], left[...], 1, 1)
    a[:, RANK:] = eye(RANK)
    eliminate(0, a)


def step_kernel(start, a_in, a):
    eliminate(start, a)


def basis_kernel(at, a_in, left, inverse, basis, a):
    a[...] = a_in[...]
    eliminate(RANK - PART, a)
    inverse[...] = a[:, RANK:]
    first, second = two(a[:, RANK:])
    own = left[:, block(at[0], at[1])]
    basis[...] = -(mm(first, own, 1, 0) + mm(second, own, 1, 0)).astype(BF16).T


def grad_kernel(h0, h1, weight_hbm, out, weight, g0, g1, sems):
    copies = fetch((weight_hbm, h0, h1), (weight, g0, g1), sems)
    copies[0].wait()
    for n, g in enumerate((g0, g1)):
        copies[n + 1].wait()
        out[n] = mm(g[...], weight[...], 1, 1).astype(BF16)


def merge_kernel(scale, err, c0, c1, g0, g1, out, t0, t1):
    step = pl.program_id(0)

    @pl.when(step == 0)
    def _():
        t0[...] = c0[...].T
        t1[...] = c1[...].T

    total = mm(t0[...], g0[...], 1, 0) + mm(t1[...], g1[...], 1, 0)
    out[...] = err[...] + total * scale


def place_kernel(at, own, near, far, diag, out):
    zl, core = at[0], at[1]
    out[:, block(zl, core)] = own[...]
    out[:, block(zl, 1 - core)] = near[...]
    out[:, block(1 - zl, core)] = far[...]
    out[:, block(1 - zl, 1 - core)] = diag[...]


def columns_of(inverse, half):
    return inverse[:, pl.ds(pl.multiple_of(half * HALF, HALF), HALF)]


def begin_kernel(scale, at, chunks, inverse, c2, c3, out, turned, half):
    turned[:, :TOK] = (c2[0].T * scale).astype(BF16)
    turned[:, TOK:] = (c3[1].T * scale).astype(BF16)
    unchunk(chunks, half)
    first, second = two(columns_of(inverse, at[1]))
    out[...] = mm(first, half[...], 1, 0) + mm(second, half[...], 1, 0)


def last_kernel(
    share, at, other, inverse, basis, begun, turned, merged_hbm, g2_hbm, g3_hbm,
    out_hbm, factor_q, half, held, g2, g3, sems_in, sems_out,
):
    zl, core = at[0], at[1]
    steps = FEAT // ROWS
    blocks = [pl.ds(n * ROWS, ROWS) for n in range(steps)]
    tops = [pl.ds(n * TOK, TOK) for n in range(ROWS // TOK)]
    arriving, leaving = [], []
    for n, cols in enumerate(blocks):
        pairs = [(g2_hbm.at[:, cols], g2.at[:, cols]), (g3_hbm.at[:, cols], g3.at[:, cols])]
        pairs += [(merged_hbm.at[r, cols], held.at[r, cols]) for r in tops]
        arriving.append(
            [pltpu.make_async_copy(*pair, sems_in.at[n, m]) for m, pair in enumerate(pairs)]
        )
        for copy in arriving[n]:
            copy.start()
    unchunk(other, half)
    first, second = two(columns_of(inverse, 1 - core))
    for n, cols in enumerate(blocks):
        q = mm(first, half[:, cols], 1, 0) + mm(second, half[:, cols], 1, 0)
        q = (begun[:, cols] + q) * share

        @pl.when(zl * 2 + core == n)
        def _(q=q):
            factor_q[...] = q.T

        for copy in arriving[n]:
            copy.wait()
        lhs = jnp.concatenate([turned[...], basis[...]], 1)
        rhs = jnp.concatenate([g2[:, cols], g3[:, cols], q.astype(BF16)], 0)
        held[:, cols] = held[:, cols] + mm(lhs, rhs, 1, 0)
        for m, r in enumerate(tops):
            copy = pltpu.make_async_copy(held.at[r, cols], out_hbm.at[r, cols], sems_out.at[n, m])
            copy.start()
            leaving.append(copy)
    for copy in leaving:
        copy.wait()


def size(shape, dtype):
    return math.prod(shape) * jnp.dtype(dtype).itemsize


def in_hbm(x):
    return pltpu.with_memory_space_constraint(x, pltpu.HBM)


def call(
    kernel, outs, args, flops, name, scratch=(), alias=None, limit=12, loose=(), held=(), free=False, sems=0
):
    args = [in_hbm(a) if n in held else a for n, a in enumerate(args)]
    moved = sum(size(a.shape, a.dtype) for a in args) + sum(size(s, d) for s, d in outs)
    scratch = [pltpu.VMEM(s, d) for s, d in scratch]
    if sems:
        scratch.append(pltpu.SemaphoreType.DMA((sems,)))
    return pl.pallas_call(
        kernel,
        out_shape=[(pltpu.HBM if free else jax.ShapeDtypeStruct)(s, d) for s, d in outs],
        in_specs=[
            SMEM if a.dtype == jnp.int32 else ANY if n in loose or n in held else VMEM
            for n, a in enumerate(args)
        ],
        out_specs=[pl.BlockSpec(s, lambda s=s: (0,) * len(s)) if free else VMEM for s, _ in outs],
        scratch_shapes=scratch,
        input_output_aliases=alias or {},
        compiler_params=pltpu.CompilerParams(vmem_limit_bytes=limit * 2**20),
        cost_estimate=pl.CostEstimate(flops=flops, bytes_accessed=moved, transcendentals=0),
        name=name,
    )(*args)


def call_grid(kernel, steps, outs, ins, args, flops, name, scratch=(), sems=0, limit=14, loose=(), alias=None):
    args = [
        a if spec in (SMEM, ANY, VMEM) or n in loose else in_hbm(a)
        for n, (a, spec) in enumerate(zip(args, ins))
    ]
    moved = sum(size(a.shape, a.dtype) for a in args) + sum(size(s, d) for s, d, _ in outs)
    scratch = [pltpu.VMEM(s, d) for s, d in scratch]
    if sems:
        scratch.append(pltpu.SemaphoreType.DMA((sems,)))
    return pl.pallas_call(
        kernel,
        grid=(steps,),
        out_shape=[
            (jax.ShapeDtypeStruct if spec is VMEM else pltpu.HBM)(s, d) for s, d, spec in outs
        ],
        in_specs=ins,
        out_specs=[spec for _, _, spec in outs],
        scratch_shapes=scratch,
        input_output_aliases=alias or {},
        compiler_params=pltpu.CompilerParams(vmem_limit_bytes=limit * 2**20),
        cost_estimate=pl.CostEstimate(flops=flops, bytes_accessed=moved, transcendentals=0),
        name=name,
    )(*args)


def whole(*shape):
    return pl.BlockSpec(shape, lambda j: (0,) * len(shape))


def column(rows):
    return pl.BlockSpec((rows, ROWS), lambda j: (0, j))


def rows_of(rows, cols):
    return pl.BlockSpec((rows, cols), lambda j: (j, 0))


CHUNKED = (CHUNKS, CHUNK_ROWS, CHUNK_COLS)
CHUNK = (CHUNK_ROWS, CHUNK_COLS)


def tied(x, *others):
    return lax.optimization_barrier((x,) + others)[0]


def spread(parts, times):
    (out,) = call(spread_kernel, [((times,) + CHUNK, BF16)], (parts,), 1_000_000, "spread")
    return out


def across_plane(keep, send, beside=(), copies=8):
    got = swap(send, "core")
    (half,) = call(add_kernel, [(CHUNKED, BF16)], (keep, got), 1_000_000, "add")
    parts = tied(lax.all_to_all(half, ("y", "x"), 0, 0), *beside)
    if copies:
        return spread(parts, copies)
    (part,) = call(sum_kernel, [(CHUNK, F32)], (parts,), 1_000_000, "sum")
    return part


def across_z_by_steps(part, beside=()):
    far = tied(swap(part, "zl"), *beside)
    part = (part + far).astype(BF16)
    return (part,) + tuple(
        lax.ppermute(part, "zh", [(i, (i + step) % 4) for i in range(4)]) for step in (1, 2, 3)
    )


def across_z(copies, beside=()):
    return tied(lax.all_to_all(copies, ("zh", "zl"), 0, 0), *beside)


def back_over_plane(parts, beside=()):
    return lax.all_to_all(spread(tied(parts, *beside), CHUNKS), ("y", "x"), 0, 0)


def on_device(context, out_grad, weight, error, warm):
    scale = 1.0 / math.sqrt(TOK * 4)
    core = lax.axis_index("core")
    zl = lax.axis_index("zl")
    at = jnp.stack([zl, core]).astype(jnp.int32)
    error = error[0]
    tokens = ((TOK, ROWS), BF16)
    pair = ((2, TOK, ROWS), BF16)

    warm_far = swap(warm, "zl")
    warm_near = swap(warm, "core")
    quarter = rows_of(TOK // 4, ROWS)
    strip = rows_of(ROWS // 4, FEAT)
    c_own, c_near, c_far, low, kept = call_grid(
        prepare_kernel,
        4,
        [tokens + (quarter,)] * 2
        + [pair + (pl.BlockSpec((2, TOK // 4, ROWS), lambda j: (0, j, 0)),)]
        + [((ROWS, FEAT), BF16, VMEM), ((ROWS, FEAT), BF16, strip)],
        [SMEM, rows_of(TOK // 4, FEAT), strip],
        (tied(at, warm_near), context, error),
        4_000_000,
        "prepare",
    )
    warm_diag = swap(tied(warm_far, low), "core")
    c_near = swap(c_near, "core")

    big = ((ROWS, FEAT), BF16)
    keep, send = call(
        functools.partial(left_kernel, scale),
        [(CHUNKED, F32), (CHUNKED, BF16)],
        (at, out_grad, context, tied(low, c_near), warm, warm_near, warm_far, warm_diag),
        2_000_000_000,
        "left",
        [((RANK, FEAT), F32)],
    )
    g_far = swap(tied(out_grad, warm_near), "zl")
    g_near = in_hbm(swap(tied(out_grad, warm_far, low), "core"))
    turned = [((ROWS, TOK), BF16)] * 2
    (merged,) = call_grid(
        functools.partial(merge_kernel, scale),
        4,
        [((ROWS, FEAT), F32, column(ROWS))],
        [column(ROWS), VMEM, VMEM, column(TOK), column(TOK)],
        (error, c_own, c_near, out_grad, g_near),
        1_100_000_000,
        "merge",
        turned,
        loose=(3,),
    )
    part = across_plane(keep, send, (merged,), 0)
    g_diag = swap(tied(g_far, part), "core")

    def grad(g0, g1):
        (out,) = call(
            grad_kernel,
            [pair],
            (g0, g1, weight),
            1_100_000_000,
            "grad",
            [big] + [((TOK, FEAT), BF16)] * 2,
            held=range(3),
            free=True,
            sems=3,
        )
        return out

    i_home = grad(out_grad, g_near)
    zs = across_z_by_steps(tied(part, g_far), (i_home,))
    c_far = swap(tied(c_far, *zs[1:]), "zl")
    (whole_part,) = call(close_kernel, [(CHUNKED, BF16)], zs, 1_000_000, "close")
    mine = lax.all_to_all(whole_part, ("y", "x"), 0, 0)

    i_far = grad(g_far, g_diag)
    other = swap(tied(mine, i_far, c_far), "core")
    i_far = swap(i_far, "zl")
    i_near = swap(i_home, "core")

    mine_half, proj = call(
        early_kernel,
        [((HALF, FEAT), BF16), ((HALF, TOK), F32)],
        (context, mine),
        150_000_000,
        "early",
    )
    other = tied(other, proj)
    keep, send, left = call(
        functools.partial(right_kernel, scale),
        [(CHUNKED, F32), (CHUNKED, BF16), ((RANK, FEAT), BF16)],
        (at, context, out_grad, kept, mine_half, proj, other),
        2_000_000_000,
        "right",
        [((RANK, FEAT), F32), big, ((RANK, TOK), F32)],
        held=(3,),
        sems=1,
    )

    table = ((RANK, 2 * RANK), F32)
    (a,) = call(gram_kernel, [table], (left,), 300_000_000, "gram")
    (a,) = call(
        functools.partial(step_kernel, PART), [table], (a,), 300_000_000, "step", alias={0: 0}
    )
    part = across_plane(keep, send, (a,))
    part = tied(part, i_far)
    c_diag = swap(c_far, "core")
    i_diag = swap(tied(i_far, part), "core")
    (a,) = call(
        functools.partial(step_kernel, 2 * PART), [table], (a,), 300_000_000, "step", alias={0: 0}
    )
    inverse, basis = call(
        basis_kernel,
        [((RANK, RANK), F32), ((ROWS, RANK), BF16)],
        (at, a, left),
        300_000_000,
        "basis",
        [table],
    )
    zs = across_z(part, (basis,))
    mine = back_over_plane(zs)
    first = pl.BlockSpec((None, TOK, ROWS), lambda j: (0, 0, 0))
    second = pl.BlockSpec((None, TOK, ROWS), lambda j: (1, 0, 0))
    (in_grad,) = call_grid(
        place_kernel,
        1,
        [((TOK, FEAT), BF16, whole(TOK, FEAT))],
        [SMEM, first, second, first, second],
        (at, i_home, i_near, i_far, i_diag),
        1_000_000,
        "place",
    )
    other = swap(tied(mine, in_grad), "core")
    begun, far_turned = call(
        functools.partial(begin_kernel, scale),
        [((RANK, FEAT), F32), ((ROWS, 2 * TOK), BF16)],
        (at, mine, inverse, c_far, c_diag),
        300_000_000,
        "begin",
        [((HALF, FEAT), BF16)],
    )
    other = tied(other, begun)

    new_error, factor_q = pl.pallas_call(
        functools.partial(last_kernel, 1.0 / (SIZES[0] * SIZES[1] * SIZES[2])),
        out_shape=[pltpu.HBM((ROWS, FEAT), F32), jax.ShapeDtypeStruct((ROWS, RANK), F32)],
        in_specs=[SMEM, VMEM, VMEM, VMEM, VMEM, VMEM, ANY, ANY, ANY],
        out_specs=[ANY, VMEM],
        scratch_shapes=[
            pltpu.VMEM((HALF, FEAT), BF16),
            pltpu.VMEM((ROWS, FEAT), F32),
            pltpu.VMEM((TOK, FEAT), BF16),
            pltpu.VMEM((TOK, FEAT), BF16),
            pltpu.SemaphoreType.DMA((4, 4)),
            pltpu.SemaphoreType.DMA((4, 2)),
        ],
        compiler_params=pltpu.CompilerParams(vmem_limit_bytes=20 * 2**20),
        cost_estimate=pl.CostEstimate(
            flops=2_000_000_000, bytes_accessed=10_000_000, transcendentals=0
        ),
        name="last",
    )(
        at, other, inverse, basis, begun, far_turned,
        in_hbm(merged), in_hbm(g_far), in_hbm(g_diag),
    )
    return in_grad, new_error[None], factor_q


def solution(mesh):
    split = Mesh(np.asarray(mesh.devices).reshape(SIZES), AXES)
    every = ("zh", "y", "x", "zl", "core")
    shard = ("zl", "core")
    return jax.shard_map(
        on_device,
        mesh=split,
        in_specs=(
            P(every, None),
            P(every, None),
            P(shard, None),
            P(("zh", "y", "x"), shard, None),
            P(shard, None),
        ),
        out_specs=(P(every, None), P(("zh", "y", "x"), shard, None), P(shard, None)),
        check_vma=False,
    )
```
